256 devices in a mesh: slab: 8 (over z), plane: 32 (over x, y, core).
Axes of the slice: x: 4, y: 4, z: 8, core: 2. Of those that a mesh axis runs over, the one named last changes fastest.
Arguments:
- grain_coordinates: float32 [8, 32, 64, 3, 128], P('slab', 'plane'), may hold values from 0 to 1
- grain_motion_speeds: float32 [8, 32, 64, 3, 128], P('slab', 'plane'), may hold values from -4 to 4
- grain_warmth: float32 [8, 32, 64, 128], P('slab', 'plane'), may hold values from 0.5 to 2
- grain_weights: float32 [8, 32, 64, 128], P('slab', 'plane'), may hold values from 0.00390625 to 0.015625
- cell_grain_tally: int32 [8, 32, 64], P('slab', 'plane'), may hold values from 32 to 128, as said below
- cell_deposit_tier: int32 [8, 32, 64], P('slab', 'plane'), may hold values from 0 to 7
- tier_thermal_coefficient: float32 [8], replicated, may hold values from 0.2 to 5
- loaned_cell_indices: int32 [8, 32, 32, 4], P('slab', 'plane'), may hold values from 0 to 63
- loaned_cell_tally: int32 [8, 32, 32], P('slab', 'plane'), may hold values from 0 to 4, as said below
- cell_couples: int32 [8, 32, 256, 2], P('slab', 'plane'), may hold values from 0 to 203, as said below
- couple_entry_tally: int32 [8, 32], P('slab', 'plane'), may hold values from 1 to 256, as said below
Outputs:
- density: float32 [8, 32, 64, 128], P('slab', 'plane')
- rates: float32 [8, 32, 64, 4, 128], P('slab', 'plane')
The draws below stay inside these ranges and needn't reach their ends.
Inputs may be any that keep to these rules, and one draw needn't show every extreme that they name: `cell_grain_tally`: in every draw some block of every device is full. `loaned_cell_tally`: every device has a peer list with all 4 slots live. `cell_couples`: each entry (a, b) has a < 64 and a < b. `couple_entry_tally`: at least one device has a full list.
All inputs are finite; a program needn't handle non-finite values.
Results may differ from the reference program's by a relative error of at most 0.0001.
Values sent between devices are 32-bit elements; how exact they have to be, the bound alone decides.
A program may use at most 128 MiB of HBM per device.

```python
import math
import jax
import jax.numpy as jnp
from jax import lax

GRAIN_CAPACITY = 128
CELLS_ON_DEVICE = 64
E = 6
S = 4
LAYERS = 8
NPAIR = 256
TABLE = 204
N_SLAB = 8
N_PLANE = 32


def draw_cell_grain_tally(key, part):
    key = jax.random.fold_in(key, 11)
    base = jax.random.randint(key, (N_SLAB, N_PLANE, CELLS_ON_DEVICE), GRAIN_CAPACITY // 4, GRAIN_CAPACITY + 1)
    full_at = jax.random.randint(jax.random.fold_in(key, 1), (N_SLAB, N_PLANE, 1), 0, CELLS_ON_DEVICE)
    return jnp.where(jnp.arange(CELLS_ON_DEVICE)[None, None, :] == full_at, GRAIN_CAPACITY, base).astype(jnp.int32)


def draw_loaned_cell_tally(key, part):
    key = jax.random.fold_in(key, 12)
    base = jax.random.randint(key, (N_SLAB, N_PLANE, N_PLANE), 0, S + 1)
    full_at = jax.random.randint(jax.random.fold_in(key, 1), (N_SLAB, N_PLANE, 1), 0, N_PLANE)
    return jnp.where(jnp.arange(N_PLANE)[None, None, :] == full_at, S, base).astype(jnp.int32)


def draw_couple_entry_tally(key, part):
    key = jax.random.fold_in(key, 13)
    total = N_SLAB * N_PLANE
    level = jax.random.randint(key, (total,), 1, 17)
    top_at = jax.random.randint(jax.random.fold_in(key, 1), (), 0, total)
    level = jnp.where(jnp.arange(total) == top_at, 16, level)
    counted = jnp.maximum(NPAIR * level * level // 256, 1)
    return counted.reshape(N_SLAB, N_PLANE).astype(jnp.int32)


def draw_cell_couples(key, part):
    key = jax.random.fold_in(key, 14)
    shape = (N_SLAB, N_PLANE, NPAIR)
    first = jax.random.randint(jax.random.fold_in(key, 1), shape, 0, CELLS_ON_DEVICE)
    choose_kind = jax.random.randint(jax.random.fold_in(key, 2), shape, 0, 4)
    spread = jnp.maximum(CELLS_ON_DEVICE - 1 - first, 1)
    nearby = first + 1 + jax.random.randint(jax.random.fold_in(key, 3), shape, 0, spread)
    faraway = jax.random.randint(jax.random.fold_in(key, 4), shape, CELLS_ON_DEVICE, TABLE)
    second = jnp.where(choose_kind == 0, nearby, faraway)
    return jnp.stack([first, second], axis=-1).astype(jnp.int32)


def place_ends(drawn, stream_key, low, largest):
    spot = [jax.random.randint(jax.random.fold_in(stream_key, axis), (), 0, length) for axis, length in enumerate(drawn.shape)]
    widest = drawn.shape.index(max(drawn.shape))
    neighbour = spot[:widest] + [(spot[widest] + 1) % drawn.shape[widest]] + spot[widest + 1:]
    return drawn.at[tuple(spot)].set(low).at[tuple(neighbour)].set(largest)


def levels(own_key, dims, split, least, high):
    loudness = 1.0
    for position, shards_of in split:
        steps = jax.random.uniform(jax.random.fold_in(jax.random.fold_in(own_key, 6), position), (shards_of,), jnp.float32, least / len(split), high / len(split))
        loudness = loudness * jnp.repeat(jnp.exp(steps), dims[position] // shards_of).reshape((-1,) + (1,) * (len(dims) - 1 - position))
    return loudness


def scatter_about(rng, extent, width, reach, cuts=(), kind=jnp.bfloat16):
    result = width * jax.random.normal(rng, extent, jnp.float32)
    if cuts:
        result = result * levels(rng, extent, cuts, -0.22, 0.18)
    return jnp.clip(result, -reach, reach).astype(kind)


def setup_inputs(seed: int = 0) -> dict:
    keys = jax.random.split(jax.random.key(seed), 12)
    return {
        "grain_coordinates": jnp.clip(1.0 * jax.random.uniform(keys[0], (N_SLAB, N_PLANE, CELLS_ON_DEVICE, 3, GRAIN_CAPACITY), jnp.float32) ** levels(keys[0], (N_SLAB, N_PLANE, CELLS_ON_DEVICE, 3, GRAIN_CAPACITY), ((0, 8), (1, 32)), -0.2, 0.2), 0.0, 1.0),
        "grain_motion_speeds": scatter_about(keys[1], (N_SLAB, N_PLANE, CELLS_ON_DEVICE, 3, GRAIN_CAPACITY), 1.0, 4.0, ((0, 8), (1, 32)), jnp.float32),
        "grain_warmth": jnp.clip(0.5 + 1.5 * jax.random.uniform(keys[2], (N_SLAB, N_PLANE, CELLS_ON_DEVICE, GRAIN_CAPACITY), jnp.float32) ** levels(keys[2], (N_SLAB, N_PLANE, CELLS_ON_DEVICE, GRAIN_CAPACITY), ((0, 8), (1, 32)), -0.2, 0.2), 0.5, 2.0),
        "grain_weights": jnp.clip(jnp.exp(math.log(0.015625) - 1.3862944 * jax.random.uniform(keys[3], (N_SLAB, N_PLANE, CELLS_ON_DEVICE, GRAIN_CAPACITY), jnp.float32) ** levels(keys[3], (N_SLAB, N_PLANE, CELLS_ON_DEVICE, GRAIN_CAPACITY), ((0, 8), (1, 32)), -0.2, 0.2)), 0.00390625, 0.015625),
        "cell_grain_tally": draw_cell_grain_tally(jax.random.fold_in(keys[11], 71), 0),
        "cell_deposit_tier": place_ends(jax.random.randint(keys[5], (N_SLAB, N_PLANE, CELLS_ON_DEVICE), 0, LAYERS), jax.random.fold_in(keys[5], 1), 0, LAYERS - 1).astype(jnp.int32),
        "tier_thermal_coefficient": jnp.clip(jnp.exp(jax.random.uniform(keys[6], (LAYERS,), jnp.float32, math.log(0.2), math.log(5.0))), 0.2, 5.0),
        "loaned_cell_indices": place_ends(jax.random.randint(keys[7], (N_SLAB, N_PLANE, N_PLANE, S), 0, CELLS_ON_DEVICE), jax.random.fold_in(keys[7], 1), 0, CELLS_ON_DEVICE - 1).astype(jnp.int32),
        "loaned_cell_tally": draw_loaned_cell_tally(jax.random.fold_in(keys[11], 71), 0),
        "cell_couples": draw_cell_couples(jax.random.fold_in(keys[11], 71), 0),
        "couple_entry_tally": draw_couple_entry_tally(jax.random.fold_in(keys[11], 71), 0),
    }


press_coef = 0.2
visc_coef = 0.1
tension_coef = 2.0


def kernel_weight(first_block, second_block):
    offset = first_block[0:3, :, None] - second_block[0:3, None, :]
    distance = jnp.sum(offset * offset, axis=0)
    return offset, jnp.maximum(1.0 - distance, 0.0)


def density_tile(first_block, second_block):
    offset, weight = kernel_weight(first_block, second_block)
    cubed = weight * weight * weight
    return jnp.sum(cubed * second_block[7][None, :], axis=1), jnp.sum(cubed * first_block[7][:, None], axis=0)


def force_tile(first_block, second_block, inv_first, inv_second):
    offset, weight = kernel_weight(first_block, second_block)
    square = weight * weight
    inv_left = inv_first[:, None]
    inv_right = inv_second[None, :]
    radial = 6.0 * press_coef * (inv_left + inv_right) * square + tension_coef * weight * (weight - 0.5)
    shear_term = visc_coef * inv_left * inv_right * square
    cond_left = first_block[8][:, None]
    cond_right = second_block[8][None, :]
    blend_cond = 2.0 * cond_left * cond_right / (cond_left + cond_right)
    heat_flow = blend_cond * inv_left * inv_right * square * (second_block[6][None, :] - first_block[6][:, None])
    push_vec = radial[None] * offset + shear_term[None] * (second_block[3:6, None, :] - first_block[3:6, :, None])
    components = jnp.concatenate([push_vec, heat_flow[None]], axis=0)
    return jnp.sum(components * second_block[7][None, None, :], axis=2), -jnp.sum(components * first_block[7][None, :, None], axis=1)


def reference(grain_coordinates, grain_motion_speeds, grain_warmth, grain_weights, cell_grain_tally, cell_deposit_tier, tier_thermal_coefficient, loaned_cell_indices, loaned_cell_tally, cell_couples, couple_entry_tally):
    grain_active_gate = (jnp.arange(GRAIN_CAPACITY)[None, None, None, :] < cell_grain_tally[..., None]).astype(jnp.float32)
    diffuse_thermal_energy = jnp.broadcast_to(tier_thermal_coefficient[cell_deposit_tier][..., None], grain_active_gate.shape)
    grain_quantities_bundle = jnp.concatenate([grain_coordinates, grain_motion_speeds, grain_warmth[:, :, :, None], (grain_weights * grain_active_gate)[:, :, :, None], diffuse_thermal_energy[:, :, :, None]], axis=3)
    slot_live = (jnp.arange(S)[None, None, None, :] < loaned_cell_tally[..., None]).astype(jnp.float32)
    ghosts = N_PLANE * S

    def build_table(values, with_mass):
        sent_rows = jax.vmap(jax.vmap(lambda held_rows, pick_rows: held_rows[pick_rows]))(values, loaned_cell_indices)
        if with_mass:
            scaling = jnp.where((jnp.arange(9) == 7)[:, None], slot_live[..., None, None], 1.0)
            sent_rows = sent_rows * scaling
        taken_rows = jnp.swapaxes(sent_rows, 1, 2).reshape((N_SLAB, N_PLANE, ghosts) + values.shape[3:])
        empty_rows = jnp.zeros_like(values[:1])
        below_rim = jnp.concatenate([empty_rows, values[:-1]], axis=0)[:, :, CELLS_ON_DEVICE - E:]
        above_rim = jnp.concatenate([values[1:], empty_rows], axis=0)[:, :, :E]
        return jnp.concatenate([values, taken_rows, below_rim, above_rim], axis=2)

    def collect(running):
        owned_rows = running[:, :, :CELLS_ON_DEVICE]
        returned = running[:, :, CELLS_ON_DEVICE:CELLS_ON_DEVICE + ghosts].reshape((N_SLAB, N_PLANE, N_PLANE, S) + running.shape[3:])
        returned = jnp.swapaxes(returned, 1, 2) * slot_live.reshape(slot_live.shape + (1,) * (running.ndim - 3))
        flat_back = returned.reshape((N_SLAB, N_PLANE, ghosts) + running.shape[3:])
        flat_index = loaned_cell_indices.reshape(N_SLAB, N_PLANE, ghosts)
        owned_rows = jax.vmap(jax.vmap(lambda held_rows, pick_rows, extra_rows: held_rows.at[pick_rows].add(extra_rows)))(owned_rows, flat_index, flat_back)
        empty_rows = jnp.zeros_like(running[:1, :, :E])
        lower_part = running[:, :, CELLS_ON_DEVICE + ghosts:CELLS_ON_DEVICE + ghosts + E]
        upper_part = running[:, :, CELLS_ON_DEVICE + ghosts + E:]
        from_above = jnp.concatenate([lower_part[1:], empty_rows], axis=0)
        from_below = jnp.concatenate([empty_rows, upper_part[:-1]], axis=0)
        owned_rows = owned_rows.at[:, :, CELLS_ON_DEVICE - E:].add(from_above)
        owned_rows = owned_rows.at[:, :, :E].add(from_below)
        return owned_rows

    devices_all = N_SLAB * N_PLANE
    flat_pairs = cell_couples.reshape(devices_all, NPAIR, 2)
    flat_counts = couple_entry_tally.reshape(devices_all)
    block_table = build_table(grain_quantities_bundle, True)

    def device_density(device_args):
        rows_here, own_pairs, live_count = device_args
        running = jnp.zeros((TABLE, GRAIN_CAPACITY), jnp.float32)
        running = running.at[:CELLS_ON_DEVICE].add(jax.vmap(density_tile)(rows_here[:CELLS_ON_DEVICE], rows_here[:CELLS_ON_DEVICE])[0])

        def add_pair(pair_index, running):
            first = own_pairs[pair_index, 0]
            second = own_pairs[pair_index, 1]
            first_part, second_part = density_tile(rows_here[first], rows_here[second])
            return running.at[first].add(first_part).at[second].add(second_part)

        return lax.fori_loop(0, live_count, add_pair, running)

    dens_acc = lax.map(device_density, (block_table.reshape(devices_all, TABLE, 9, GRAIN_CAPACITY), flat_pairs, flat_counts))
    density = collect(dens_acc.reshape(N_SLAB, N_PLANE, TABLE, GRAIN_CAPACITY))
    inverse = jnp.where(grain_active_gate > 0, 1.0 / jnp.where(grain_active_gate > 0, density, 1.0), 0.0)
    inv_table = build_table(inverse, False)

    def device_rates(device_args):
        rows_here, inv_here, own_pairs, live_count = device_args
        running = jnp.zeros((TABLE, 4, GRAIN_CAPACITY), jnp.float32)
        running = running.at[:CELLS_ON_DEVICE].add(jax.vmap(force_tile)(rows_here[:CELLS_ON_DEVICE], rows_here[:CELLS_ON_DEVICE], inv_here[:CELLS_ON_DEVICE], inv_here[:CELLS_ON_DEVICE])[0])

        def add_pair(pair_index, running):
            first = own_pairs[pair_index, 0]
            second = own_pairs[pair_index, 1]
            first_part, second_part = force_tile(rows_here[first], rows_here[second], inv_here[first], inv_here[second])
            return running.at[first].add(first_part).at[second].add(second_part)

        return lax.fori_loop(0, live_count, add_pair, running)

    rate_acc = lax.map(device_rates, (block_table.reshape(devices_all, TABLE, 9, GRAIN_CAPACITY), inv_table.reshape(devices_all, TABLE, GRAIN_CAPACITY), flat_pairs, flat_counts))
    rates = collect(rate_acc.reshape(N_SLAB, N_PLANE, TABLE, 4, GRAIN_CAPACITY))
    return density * grain_active_gate, rates * grain_active_gate[:, :, :, None, :]
```

```python
import functools
import jax
import jax.numpy as jnp
from jax import lax
from jax.experimental import pallas as pl
from jax.experimental.pallas import tpu as pltpu
from jax.sharding import PartitionSpec as P

E = 6
LAYERS = 8
UNROLL = 8

press_coef = 0.2
visc_coef = 0.1
tension_coef = 2.0

f32 = jnp.float32
bf16 = jnp.bfloat16
MESH = pl.DeviceIdType.MESH


def dot(a, b):
    return lax.dot_general(a, b, (((1,), (0,)), ((), ())), preferred_element_type=f32)


def split2(x):
    hi = x.astype(bf16)
    return hi, (x - hi.astype(f32)).astype(bf16)


def split3(x):
    a = x.astype(bf16).astype(f32)
    b = (x - a).astype(bf16).astype(f32)
    return a, b, x - a - b


def exact_dot(select, values):
    a, b, c = split3(values)
    parts = jnp.concatenate([a.astype(bf16), b.astype(bf16), c.astype(bf16)], axis=1)
    out = dot(select, parts)
    n = values.shape[1]
    return out[:, 0:n] + out[:, n : 2 * n] + out[:, 2 * n : 3 * n]


def wide(row):
    return jnp.broadcast_to(row, (8, 128))


def step_kernel(
    cells,
    lanes,
    peers,
    slabs,
    npair,
    ints,
    vecs,
    state,
    dens_out,
    rates_out,
    xo,
    yo,
    xt,
    yt,
    kg,
    sx,
    sy,
    feat,
    gcol,
    coef,
    xd,
    acc,
    dpart,
    rpart,
    selfd,
    selfr,
    ownr,
    zmat,
    rd,
    rdr,
    si,
    sir,
    ri,
    rir,
    invt,
    kt,
    sr,
    srr,
    rr,
    rrr,
    load_sem,
    send_sem,
    recv_sem,
):
    slots = 4
    ghosts = peers * slots
    rim0 = cells + ghosts
    me = lax.axis_index("plane")
    slab = lax.axis_index("slab")
    below = lax.rem(slab + slabs - 1, slabs)
    above = lax.rem(slab + 1, slabs)
    has_below = jnp.where(slab > 0, 1.0, 0.0).astype(f32)
    has_above = jnp.where(slab < slabs - 1, 1.0, 0.0).astype(f32)
    row8 = lax.broadcasted_iota(jnp.int32, (8, 128), 0)
    top = row8 < 4

    loads = [
        pltpu.make_async_copy(state.at[pl.ds(0, 4 * cells)], xo, load_sem.at[0]),
        pltpu.make_async_copy(state.at[pl.ds(4 * cells, 4 * cells)], yo, load_sem.at[1]),
        pltpu.make_async_copy(state.at[pl.ds(8 * cells, 2 * cells)], kg, load_sem.at[2]),
    ]
    for load in loads:
        load.start()

    barrier = pltpu.get_barrier_semaphore()

    def greet(d, c):
        pl.semaphore_signal(
            barrier, inc=1, device_id=(slab, lax.rem(me + d, peers)), device_id_type=MESH
        )
        return c

    lax.fori_loop(1, peers, greet, 0)
    pl.semaphore_signal(barrier, inc=1, device_id=(below, me), device_id_type=MESH)
    pl.semaphore_signal(barrier, inc=1, device_id=(above, me), device_id_type=MESH)

    def peer_copy(phase, src, dst, d):
        q = lax.rem(me + d, peers)
        return pltpu.make_async_remote_copy(
            src_ref=src(q),
            dst_ref=dst(me),
            send_sem=send_sem.at[phase, d],
            recv_sem=recv_sem.at[phase, me],
            device_id=(slab, q),
            device_id_type=MESH,
        )

    def peer_arrival(phase, src, dst, d):
        q = lax.rem(me + d, peers)
        return pltpu.make_async_remote_copy(
            src_ref=src(q),
            dst_ref=dst(q),
            send_sem=send_sem.at[phase, d],
            recv_sem=recv_sem.at[phase, q],
            device_id=(slab, q),
            device_id_type=MESH,
        )

    def rim_copies(phase, to_above, in_below, to_below, in_above):
        return (
            pltpu.make_async_remote_copy(
                src_ref=to_above,
                dst_ref=in_below,
                send_sem=send_sem.at[phase, peers],
                recv_sem=recv_sem.at[phase, peers],
                device_id=(above, me),
                device_id_type=MESH,
            ),
            pltpu.make_async_remote_copy(
                src_ref=to_below,
                dst_ref=in_above,
                send_sem=send_sem.at[phase, peers + 1],
                recv_sem=recv_sem.at[phase, peers + 1],
                device_id=(below, me),
                device_id_type=MESH,
            ),
        )

    def send_all(phase, src, dst, rims):
        def go(d, c):
            peer_copy(phase, src, dst, d).start()
            return c

        lax.fori_loop(1, peers, go, 0)
        for rim in rims:
            rim.start()

    def wait_all(phase, src, dst, rims):
        def go(d, c):
            peer_arrival(phase, src, dst, d).wait_recv()
            return c

        lax.fori_loop(1, peers, go, 0)
        for rim in rims:
            rim.wait_recv()

    def drain(phase, src, dst, rims):
        def go(d, c):
            peer_copy(phase, src, dst, d).wait_send()
            return c

        lax.fori_loop(1, peers, go, 0)
        for rim in rims:
            rim.wait_send()

    def stage_blocks(table, stage, with_mass):
        def go(q, c):
            live = ints[2 * npair + ghosts + q]
            for k in range(slots):
                pick = ints[2 * npair + q * slots + k]
                block = table[pl.ds(pick * 4, 4), :]
                if with_mass:
                    lent = jnp.minimum(jnp.maximum(live - k, 0), 1).astype(f32)
                    block = block * jnp.where(row8[0:4] < 3, 1.0, lent)
                stage[q, 4 * k : 4 * k + 4, :] = block
            return c

        lax.fori_loop(0, peers, go, 0, unroll=4)

    x_src = lambda q: sx.at[q]
    x_dst = lambda q: xt.at[pl.ds(pl.multiple_of(4 * cells + 16 * q, 8), 16)]
    x_rims = rim_copies(
        0,
        xo.at[pl.ds(4 * (cells - E), 4 * E)],
        xt.at[pl.ds(4 * rim0, 4 * E)],
        xo.at[pl.ds(0, 4 * E)],
        xt.at[pl.ds(4 * rim0 + 4 * E, 4 * E)],
    )
    y_src = lambda q: sy.at[q]
    y_dst = lambda q: yt.at[pl.ds(pl.multiple_of(4 * cells + 16 * q, 8), 16)]
    y_rims = rim_copies(
        1,
        yo.at[pl.ds(4 * (cells - E), 4 * E)],
        yt.at[pl.ds(4 * rim0, 4 * E)],
        yo.at[pl.ds(0, 4 * E)],
        yt.at[pl.ds(4 * rim0 + 4 * E, 4 * E)],
    )

    loads[0].wait()
    stage_blocks(xo, sx, True)
    xt[0 : 4 * cells, :] = xo[...]
    pl.semaphore_wait(barrier, peers + 1)
    send_all(0, x_src, x_dst, x_rims)
    xt[pl.ds(pl.multiple_of(4 * cells + 16 * me, 8), 16), :] = sx[me]
    loads[1].wait()
    stage_blocks(yo, sy, False)
    yt[0 : 4 * cells, :] = yo[...]
    send_all(1, y_src, y_dst, y_rims)
    yt[pl.ds(pl.multiple_of(4 * cells + 16 * me, 8), 16), :] = sy[me]
    loads[2].wait()

    def features(t, scale):
        base = t * 4
        x0, x1, x2, mu = (wide(xt[pl.ds(base + c, 1), :]) for c in range(4))
        if scale is not None:
            mu = mu * scale
        rm = row8 & 3
        sq = x0 * x0 + x1 * x1 + x2 * x2
        xyz = jnp.where(rm == 0, x0, jnp.where(rm == 1, x1, x2))
        last = rm == 3
        xd[t] = jnp.where(last, 1.0, xyz)
        q1, q2, q3 = split3(jnp.where(last, -sq, xyz))
        ones = jnp.where(row8 < 3, 1.0, 0.0)
        feat[t] = jnp.concatenate(
            [jnp.where(top, q1, q2), jnp.where(top, q3, q1), jnp.where(top, q2, q1), ones], axis=0
        ).astype(bf16)
        p1, p2, p3 = split3(mu * jnp.where(last, 1.0, xyz * 2.0))
        u1, u2, u3 = split3(mu * (1.0 - sq))
        tail = jnp.where(
            row8 == 0, u1, jnp.where(row8 == 1, u2, jnp.where(row8 == 2, u3, 0.0))
        )
        return [p1, jnp.where(top, p1, p2), jnp.where(top, p2, p3), tail]

    def prepare(first, count, scale):
        def go(g, c):
            base = first + g * 4
            tiles = []
            for k in range(4):
                tiles += features(base + k, scale(base + k))
            turned = jnp.concatenate(tiles, axis=0).T
            for k in range(4):
                gcol[base + k] = turned[:, 32 * k : 32 * k + 32].astype(bf16)
            return c

        lax.fori_loop(0, count // 4, go, 0)

    def rim_scale(t):
        return jnp.where(t < rim0 + E, has_below, has_above)

    def weight(s, t):
        return jnp.maximum(dot(gcol[s], feat[t]), 0.0)

    def density_part(s, t):
        w = weight(s, t)
        return jnp.sum(w * w * w, axis=0, keepdims=True)

    prepare(0, cells, lambda t: None)

    def own_density(t, c):
        selfd[pl.ds(t, 1), :] = density_part(t, t)
        return c

    lax.fori_loop(0, cells, own_density, 0, unroll=8)

    zrow = lax.broadcasted_iota(jnp.int32, (cells + 8 * peers + 16, 2 * npair), 0)
    ghost_row = cells + ((zrow - cells) >> 3) * 4 + (zrow & 3)
    rim_row = zrow - (cells + 8 * peers)
    rim_block = jnp.where((rim_row & 7) < E, rim0 + (rim_row >> 3) * E + (rim_row & 7), -2)
    block_of = jnp.where(zrow < cells, zrow, jnp.where(rim_row < 0, ghost_row, rim_block))
    zmat[...] = jnp.where(vecs[0:1, 0 : 2 * npair] == block_of, 1.0, 0.0).astype(bf16)

    wait_all(0, x_src, x_dst, x_rims)
    prepare(cells, ghosts, lambda t: None)
    prepare(rim0, 2 * E, rim_scale)

    def pair_density(g, c):
        for u in range(UNROLL):
            n = g * UNROLL + u
            a = ints[n]
            b = ints[npair + n]
            dpart[pl.ds(n, 1), :] = density_part(b, a)
            dpart[pl.ds(npair + n, 1), :] = density_part(a, b)
        return c

    lax.fori_loop(0, npair // UNROLL, pair_density, 0)

    acc[...] = exact_dot(zmat[...], dpart[...])

    d_src = lambda q: acc.at[pl.ds(pl.multiple_of(cells + 8 * q, 8), 8)]
    d_dst = lambda q: rd.at[pl.ds(pl.multiple_of(8 * q, 8), 8)]
    rim_at = cells + 8 * peers
    d_rims = rim_copies(
        2, acc.at[pl.ds(rim_at + 8, 8)], rdr.at[0], acc.at[pl.ds(rim_at, 8)], rdr.at[1]
    )
    send_all(2, d_src, d_dst, d_rims)
    rd[pl.ds(pl.multiple_of(8 * me, 8), 8), :] = acc[pl.ds(pl.multiple_of(cells + 8 * me, 8), 8), :]
    own_row = lax.broadcasted_iota(jnp.int32, (cells, 8 * peers), 0)
    zrecv = jnp.where(vecs[1:2, 0 : 8 * peers] == own_row, 1.0, 0.0).astype(bf16)
    wait_all(2, d_src, d_dst, d_rims)
    selfd[...] = selfd[...] + acc[0:cells, :] + exact_dot(zrecv, rd[...])
    selfd[0:E, :] = selfd[0:E, :] + rdr[0, 0:E, :] * has_below
    selfd[cells - E : cells, :] = selfd[cells - E : cells, :] + rdr[1, 0:E, :] * has_above
    gate = kg[cells : 2 * cells, :]
    density = selfd[...]
    dens_out[...] = density * gate
    invt[0:cells, :] = jnp.where(gate > 0.0, 1.0 / jnp.where(gate > 0.0, density, 1.0), 0.0)
    kt[0:cells, :] = kg[0:cells, :]

    def stage_inverse(q, c):
        for k in range(slots):
            pick = ints[2 * npair + q * slots + k]
            si[q, k : k + 1, :] = invt[pl.ds(pick, 1), :]
            si[q, slots + k : slots + k + 1, :] = kt[pl.ds(pick, 1), :]
        return c

    lax.fori_loop(0, peers, stage_inverse, 0, unroll=4)
    for side, start in ((0, cells - E), (1, 0)):
        sir[side, 0:E, :] = invt[start : start + E, :]
        sir[side, 8 : 8 + E, :] = kt[start : start + E, :]
    i_src = lambda q: si.at[q]
    i_dst = lambda q: ri.at[q]
    i_rims = rim_copies(3, sir.at[0], rir.at[0], sir.at[1], rir.at[1])
    send_all(3, i_src, i_dst, i_rims)
    ri[me] = si[me]

    def coefficients(t, scale):
        base = t * 4
        mu = wide(xt[pl.ds(base + 3, 1), :])
        if scale is not None:
            mu = mu * scale
        inv = wide(invt[pl.ds(t, 1), :])
        y4 = yt[pl.ds(pl.multiple_of(base, 4), 4), :]
        y8 = jnp.concatenate([y4, jnp.ones_like(y4)], axis=0)
        place = mu * xd[t]
        press = jnp.where(top, 1.0, (6.0 * press_coef) * inv + tension_coef) * place
        flow = (mu * inv) * y8
        linear = jnp.where(top, 0.0, (-0.5 * tension_coef) * mu * place)
        square = jnp.concatenate([press, flow], axis=0)
        line = jnp.concatenate([linear, jnp.zeros_like(linear)], axis=0)
        sh, sl = split2(square)
        lh, ll = split2(line)
        coef[t, 0:16, 0:128] = sh
        coef[t, 16:32, 0:128] = sl
        coef[t, 0:16, 128:256] = lh
        coef[t, 16:32, 128:256] = ll

    def force_part(s, t, heat):
        w = weight(s, t)
        qh, ql = split2(w * w)
        wh, wl = split2(w)
        square = coef[s, :, 0:128]
        line = coef[s, :, 128:256]
        out = dot(
            jnp.concatenate([square, square, line, line], axis=1),
            jnp.concatenate([qh, ql, wh, wl], axis=0),
        )
        out = out[0:16] + out[16:32]
        ae = out[0:8]
        flow = out[8:16]
        moved = xd[t] * jnp.where(top, wide(ae[3:4]), wide(ae[7:8])) - ae
        y4 = yt[pl.ds(t * 4, 4), :]
        carried = flow[0:4] - y4 * flow[4:5]
        gain = jnp.where(row8[0:4] == 3, jnp.broadcast_to(heat, (4, 128)), visc_coef)
        inv = invt[pl.ds(t, 1), :]
        return inv * ((6.0 * press_coef) * moved[0:4] + gain * carried) + moved[4:8]

    def own_coef(t, c):
        coefficients(t, None)
        return c

    lax.fori_loop(0, cells, own_coef, 0, unroll=4)

    def own_force(t, c):
        part = force_part(t, t, kt[pl.ds(t, 1), :])
        for k in range(4):
            selfr[k, pl.ds(t, 1), :] = part[k : k + 1, :]
        return c

    lax.fori_loop(0, cells, own_force, 0, unroll=4)

    wait_all(1, y_src, y_dst, y_rims)
    wait_all(3, i_src, i_dst, i_rims)

    def spread(q, c):
        invt[pl.ds(cells + 4 * q, 4), :] = ri[q, 0:4, :]
        kt[pl.ds(cells + 4 * q, 4), :] = ri[q, 4:8, :]
        return c

    lax.fori_loop(0, peers, spread, 0, unroll=4)
    for side in range(2):
        invt[rim0 + side * E : rim0 + side * E + E, :] = rir[side, 0:E, :]
        kt[rim0 + side * E : rim0 + side * E + E, :] = rir[side, 8 : 8 + E, :]

    def ghost_coef(t, c):
        coefficients(cells + t, None)
        return c

    lax.fori_loop(0, ghosts, ghost_coef, 0, unroll=4)

    def rim_coef(t, c):
        coefficients(rim0 + t, rim_scale(rim0 + t))
        return c

    lax.fori_loop(0, 2 * E, rim_coef, 0, unroll=4)

    def pair_force(g, c):
        for u in range(UNROLL):
            n = g * UNROLL + u
            a = ints[n]
            b = ints[npair + n]
            ka = kt[pl.ds(a, 1), :]
            kb = kt[pl.ds(b, 1), :]
            heat = 2.0 * ka * kb / (ka + kb)
            first = force_part(b, a, heat)
            second = force_part(a, b, heat)
            for k in range(4):
                rpart[k, pl.ds(n, 1), :] = first[k : k + 1, :]
                rpart[k, pl.ds(npair + n, 1), :] = second[k : k + 1, :]
        return c

    lax.fori_loop(0, npair // UNROLL, pair_force, 0)

    held = None
    half = (lax.broadcasted_iota(jnp.int32, (8 * peers, 128), 0) & 7) < 4
    for k in range(4):
        sums = exact_dot(zmat[...], rpart[k])
        ownr[k] = sums[0:cells]
        for side in range(2):
            srr[side, 8 * k : 8 * k + 8, :] = sums[rim_at + 8 * side : rim_at + 8 * side + 8]
        lent = sums[cells:rim_at]
        if k % 2 == 0:
            held = lent
        else:
            sr[:, 4 * (k - 1) : 4 * (k - 1) + 8, :] = jnp.where(half, held, lent).reshape(peers, 8, 128)

    r_src = lambda q: sr.at[q]
    r_dst = lambda q: rr.at[q]
    r_rims = rim_copies(4, srr.at[1], rrr.at[0], srr.at[0], rrr.at[1])
    send_all(4, r_src, r_dst, r_rims)
    rr[me] = sr[me]
    drain(0, x_src, x_dst, x_rims)
    drain(1, y_src, y_dst, y_rims)
    drain(2, d_src, d_dst, d_rims)
    drain(3, i_src, i_dst, i_rims)
    wait_all(4, r_src, r_dst, r_rims)
    a, b, c3 = split3(rr[...].reshape(16 * peers, 128))
    parts = jnp.concatenate([a.astype(bf16), b.astype(bf16), c3.astype(bf16)], axis=1)
    own_row = 4 * lax.broadcasted_iota(jnp.int32, (cells, 16 * peers), 0)
    for k in range(4):
        pick = jnp.where(vecs[2:3, 0 : 16 * peers] == own_row + k, 1.0, 0.0).astype(bf16)
        got = dot(pick, parts)
        ownr[k] = ownr[k] + selfr[k] + (got[:, 0:128] + got[:, 128:256] + got[:, 256:384])
        ownr[k, 0:E, :] = ownr[k, 0:E, :] + rrr[0, 8 * k : 8 * k + E, :] * has_below
        ownr[k, cells - E : cells, :] = (
            ownr[k, cells - E : cells, :] + rrr[1, 8 * k : 8 * k + E, :] * has_above
        )
        rates_out[pl.ds(k, cells, stride=4), :] = ownr[k] * gate
    drain(4, r_src, r_dst, r_rims)


def shards(
    grain_coordinates,
    grain_motion_speeds,
    grain_warmth,
    grain_weights,
    cell_grain_tally,
    cell_deposit_tier,
    tier_thermal_coefficient,
    loaned_cell_indices,
    loaned_cell_tally,
    cell_couples,
    couple_entry_tally,
):
    coords = grain_coordinates[0, 0]
    cells, _, lanes = coords.shape
    gate = (jnp.arange(lanes)[None, :] < cell_grain_tally[0, 0][:, None]).astype(f32)
    heat = jnp.sum(
        jnp.where(
            cell_deposit_tier[0, 0][:, None] == jnp.arange(LAYERS)[None, :],
            tier_thermal_coefficient[None, :],
            0.0,
        ),
        axis=1,
    )
    weights = grain_weights[0, 0]
    root = jnp.exp(jnp.log(weights) * (1.0 / 3.0))
    root = root - (root * root * root - weights) / (3.0 * root * root)
    root = root * gate
    state = jnp.concatenate(
        [
            jnp.concatenate([coords - 0.5, root[:, None]], axis=1).reshape(4 * cells, lanes),
            jnp.concatenate([grain_motion_speeds[0, 0], grain_warmth[0, 0][:, None]], axis=1).reshape(
                4 * cells, lanes
            ),
            jnp.broadcast_to(heat[:, None], (cells, lanes)),
            gate,
        ],
        axis=0,
    )
    picks = loaned_cell_indices[0, 0]
    peers, slots = picks.shape
    slabs = lax.axis_size("slab")
    couples = cell_couples[0, 0]
    npair = couples.shape[0]
    ints = jnp.concatenate([couples[:, 0], couples[:, 1], picks.reshape(-1), loaned_cell_tally[0, 0]])
    alive = jnp.arange(npair) < couple_entry_tally[0, 0]
    pair_rows = jnp.where(alive[:, None], couples, -1).T.reshape(-1)
    lent = jnp.where(jnp.arange(slots)[None, :] < loaned_cell_tally[0, 0][:, None], picks, -1)
    lent8 = jnp.concatenate([lent, jnp.full_like(lent, -1)], axis=1).reshape(-1)
    lent16 = jnp.where(
        lent[:, None, :] >= 0, lent[:, None, :] * 4 + jnp.arange(4)[None, :, None], -1
    ).reshape(-1)
    width = max(2 * npair, 16 * peers)
    vecs = jnp.stack(
        [jnp.pad(v, (0, width - v.shape[0]), constant_values=-1) for v in (pair_rows, lent8, lent16)]
        + [jnp.full((width,), -1, jnp.int32)] * 5
    )
    table = cells + slots * peers + 2 * E
    zrows = cells + 8 * peers + 16
    vmem = lambda *shape: pltpu.VMEM(shape, f32)
    density, rates = pl.pallas_call(
        functools.partial(step_kernel, cells, lanes, peers, slabs, npair),
        out_shape=(
            jax.ShapeDtypeStruct((cells, lanes), f32),
            jax.ShapeDtypeStruct((4 * cells, lanes), f32),
        ),
        in_specs=[
            pl.BlockSpec(memory_space=pltpu.SMEM),
            pl.BlockSpec(memory_space=pltpu.VMEM),
            pl.BlockSpec(memory_space=pl.ANY),
        ],
        out_specs=(
            pl.BlockSpec(memory_space=pltpu.VMEM),
            pl.BlockSpec(memory_space=pltpu.VMEM),
        ),
        scratch_shapes=[
            vmem(4 * cells, lanes),
            vmem(4 * cells, lanes),
            vmem(4 * table, lanes),
            vmem(4 * table, lanes),
            vmem(2 * cells, lanes),
            vmem(peers, 16, lanes),
            vmem(peers, 16, lanes),
            pltpu.VMEM((table, 32, lanes), bf16),
            pltpu.VMEM((table, lanes, 32), bf16),
            pltpu.VMEM((table, 32, 2 * lanes), bf16),
            vmem(table, 8, lanes),
            vmem(zrows, lanes),
            vmem(2 * npair, lanes),
            vmem(4, 2 * npair, lanes),
            vmem(cells, lanes),
            vmem(4, cells, lanes),
            vmem(4, cells, lanes),
            pltpu.VMEM((zrows, 2 * npair), bf16),
            vmem(8 * peers, lanes),
            vmem(2, 8, lanes),
            vmem(peers, 8, lanes),
            vmem(2, 16, lanes),
            vmem(peers, 8, lanes),
            vmem(2, 16, lanes),
            vmem(table, lanes),
            vmem(table, lanes),
            vmem(peers, 16, lanes),
            vmem(2, 32, lanes),
            vmem(peers, 16, lanes),
            vmem(2, 32, lanes),
            pltpu.SemaphoreType.DMA((3,)),
            pltpu.SemaphoreType.DMA((5, peers + 2)),
            pltpu.SemaphoreType.DMA((5, peers + 2)),
        ],
        compiler_params=pltpu.CompilerParams(
            collective_id=0, has_side_effects=True, vmem_limit_bytes=40 * 1024 * 1024
        ),
        name="force_step",
    )(ints, vecs, state)
    return density[None, None], rates.reshape(1, 1, cells, 4, lanes)


def solution(mesh):
    return jax.shard_map(
        shards,
        mesh=mesh,
        in_specs=(
            P("slab", "plane", None, None, None),
            P("slab", "plane", None, None, None),
            P("slab", "plane", None, None),
            P("slab", "plane", None, None),
            P("slab", "plane", None),
            P("slab", "plane", None),
            P(),
            P("slab", "plane", None, None),
            P("slab", "plane", None),
            P("slab", "plane", None, None),
            P("slab", "plane"),
        ),
        out_specs=(P("slab", "plane", None, None), P("slab", "plane", None, None, None)),
        check_vma=False,
    )
```

```python
import functools
import jax
import jax.numpy as jnp
from jax import lax
from jax.experimental import pallas as pl
from jax.experimental.pallas import tpu as pltpu
from jax.sharding import PartitionSpec as P

E = 6
LAYERS = 8
UNROLL = 16
FILL = 16
USE = 16
SELF_UNROLL = 16
DENS_UNROLL = 32
PREP_UNROLL = 8

press_coef = 0.2
visc_coef = 0.1
tension_coef = 2.0

f32 = jnp.float32
bf16 = jnp.bfloat16
MESH = pl.DeviceIdType.MESH


def dot(a, b):
    return lax.dot_general(a, b, (((1,), (0,)), ((), ())), preferred_element_type=f32)


def split2(x):
    hi = x.astype(bf16)
    return hi, (x - hi.astype(f32)).astype(bf16)


def split3(x):
    a = x.astype(bf16).astype(f32)
    b = (x - a).astype(bf16).astype(f32)
    return a, b, x - a - b


def exact_dot(select, values):
    a, b, c = split3(values)
    parts = jnp.concatenate([a.astype(bf16), b.astype(bf16), c.astype(bf16)], axis=1)
    out = dot(select, parts)
    n = values.shape[1]
    return out[:, 0:n] + out[:, n : 2 * n] + out[:, 2 * n : 3 * n]


def wide(row):
    return jnp.broadcast_to(row, (8, 128))


def step_kernel(
    cells,
    lanes,
    peers,
    slabs,
    npair,
    ints,
    vecs,
    state,
    dens_out,
    rates_out,
    xo,
    yo,
    xt,
    yt,
    kg,
    sx,
    sy,
    feat,
    gcol,
    coef,
    wtile,
    xd,
    acc,
    dpart,
    rpart,
    selfd,
    selfr,
    ownr,
    zmat,
    rd,
    rdr,
    si,
    sir,
    ri,
    rir,
    invt,
    kt,
    sr,
    srr,
    rr,
    rrr,
    load_sem,
    send_sem,
    recv_sem,
):
    slots = 4
    ghosts = peers * slots
    rim0 = cells + ghosts
    me = lax.axis_index("plane")
    slab = lax.axis_index("slab")
    below = lax.rem(slab + slabs - 1, slabs)
    above = lax.rem(slab + 1, slabs)
    has_below = jnp.where(slab > 0, 1.0, 0.0).astype(f32)
    has_above = jnp.where(slab < slabs - 1, 1.0, 0.0).astype(f32)
    row8 = lax.broadcasted_iota(jnp.int32, (8, 128), 0)
    top = row8 < 4

    loads = [
        pltpu.make_async_copy(state.at[pl.ds(0, 4 * cells)], xo, load_sem.at[0]),
        pltpu.make_async_copy(state.at[pl.ds(4 * cells, 4 * cells)], yo, load_sem.at[1]),
        pltpu.make_async_copy(state.at[pl.ds(8 * cells, 2 * cells)], kg, load_sem.at[2]),
    ]
    for load in loads:
        load.start()

    barrier = pltpu.get_barrier_semaphore()

    def greet(d, c):
        pl.semaphore_signal(
            barrier, inc=1, device_id=(slab, lax.rem(me + d, peers)), device_id_type=MESH
        )
        return c

    lax.fori_loop(1, peers, greet, 0)
    pl.semaphore_signal(barrier, inc=1, device_id=(below, me), device_id_type=MESH)
    pl.semaphore_signal(barrier, inc=1, device_id=(above, me), device_id_type=MESH)

    def peer_copy(phase, src, dst, d):
        q = lax.rem(me + d, peers)
        return pltpu.make_async_remote_copy(
            src_ref=src(q),
            dst_ref=dst(me),
            send_sem=send_sem.at[phase, d],
            recv_sem=recv_sem.at[phase, me],
            device_id=(slab, q),
            device_id_type=MESH,
        )

    def peer_arrival(phase, src, dst, d):
        q = lax.rem(me + d, peers)
        return pltpu.make_async_remote_copy(
            src_ref=src(q),
            dst_ref=dst(q),
            send_sem=send_sem.at[phase, d],
            recv_sem=recv_sem.at[phase, q],
            device_id=(slab, q),
            device_id_type=MESH,
        )

    def rim_copies(phase, to_above, in_below, to_below, in_above):
        return (
            pltpu.make_async_remote_copy(
                src_ref=to_above,
                dst_ref=in_below,
                send_sem=send_sem.at[phase, peers],
                recv_sem=recv_sem.at[phase, peers],
                device_id=(above, me),
                device_id_type=MESH,
            ),
            pltpu.make_async_remote_copy(
                src_ref=to_below,
                dst_ref=in_above,
                send_sem=send_sem.at[phase, peers + 1],
                recv_sem=recv_sem.at[phase, peers + 1],
                device_id=(below, me),
                device_id_type=MESH,
            ),
        )

    def send_all(phase, src, dst, rims):
        def go(d, c):
            peer_copy(phase, src, dst, d).start()
            return c

        lax.fori_loop(1, peers, go, 0)
        for rim in rims:
            rim.start()

    def wait_all(phase, src, dst, rims):
        def go(d, c):
            peer_arrival(phase, src, dst, d).wait_recv()
            return c

        lax.fori_loop(1, peers, go, 0)
        for rim in rims:
            rim.wait_recv()

    def drain(phase, src, dst, rims):
        def go(d, c):
            peer_copy(phase, src, dst, d).wait_send()
            return c

        lax.fori_loop(1, peers, go, 0)
        for rim in rims:
            rim.wait_send()

    def stage_blocks(table, stage, with_mass):
        def go(q, c):
            live = ints[2 * npair + ghosts + q]
            for k in range(slots):
                pick = ints[2 * npair + q * slots + k]
                block = table[pl.ds(pick * 4, 4), :]
                if with_mass:
                    lent = jnp.minimum(jnp.maximum(live - k, 0), 1).astype(f32)
                    block = block * jnp.where(row8[0:4] < 3, 1.0, lent)
                stage[q, 4 * k : 4 * k + 4, :] = block
            return c

        lax.fori_loop(0, peers, go, 0, unroll=4)

    x_src = lambda q: sx.at[q]
    x_dst = lambda q: xt.at[pl.ds(pl.multiple_of(4 * cells + 16 * q, 8), 16)]
    x_rims = rim_copies(
        0,
        xo.at[pl.ds(4 * (cells - E), 4 * E)],
        xt.at[pl.ds(4 * rim0, 4 * E)],
        xo.at[pl.ds(0, 4 * E)],
        xt.at[pl.ds(4 * rim0 + 4 * E, 4 * E)],
    )
    y_src = lambda q: sy.at[q]
    y_dst = lambda q: yt.at[pl.ds(pl.multiple_of(4 * cells + 16 * q, 8), 16)]
    y_rims = rim_copies(
        1,
        yo.at[pl.ds(4 * (cells - E), 4 * E)],
        yt.at[pl.ds(4 * rim0, 4 * E)],
        yo.at[pl.ds(0, 4 * E)],
        yt.at[pl.ds(4 * rim0 + 4 * E, 4 * E)],
    )

    loads[0].wait()
    stage_blocks(xo, sx, True)
    xt[0 : 4 * cells, :] = xo[...]
    pl.semaphore_wait(barrier, peers + 1)
    send_all(0, x_src, x_dst, x_rims)
    xt[pl.ds(pl.multiple_of(4 * cells + 16 * me, 8), 16), :] = sx[me]
    loads[1].wait()
    stage_blocks(yo, sy, False)
    yt[0 : 4 * cells, :] = yo[...]
    send_all(1, y_src, y_dst, y_rims)
    yt[pl.ds(pl.multiple_of(4 * cells + 16 * me, 8), 16), :] = sy[me]
    loads[2].wait()

    def features(t, scale):
        base = t * 4
        x0, x1, x2, mu = (wide(xt[pl.ds(base + c, 1), :]) for c in range(4))
        if scale is not None:
            mu = mu * scale
        rm = row8 & 3
        sq = x0 * x0 + x1 * x1 + x2 * x2
        xyz = jnp.where(rm == 0, x0, jnp.where(rm == 1, x1, x2))
        last = rm == 3
        xd[t] = jnp.where(last, 1.0, xyz)
        q1, q2, q3 = split3(jnp.where(last, -sq, xyz))
        ones = jnp.where(row8 < 3, 1.0, 0.0)
        feat[t] = jnp.concatenate(
            [jnp.where(top, q1, q2), jnp.where(top, q3, q1), jnp.where(top, q2, q1), ones], axis=0
        ).astype(bf16)
        p1, p2, p3 = split3(mu * jnp.where(last, 1.0, xyz * 2.0))
        u1, u2, u3 = split3(mu * (1.0 - sq))
        tail = jnp.where(
            row8 == 0, u1, jnp.where(row8 == 1, u2, jnp.where(row8 == 2, u3, 0.0))
        )
        return [p1, jnp.where(top, p1, p2), jnp.where(top, p2, p3), tail]

    def prepare(first, count, scale):
        def go(g, c):
            base = first + g * 4
            tiles = []
            for k in range(4):
                tiles += features(base + k, scale(base + k))
            turned = jnp.concatenate(tiles, axis=0).T
            for k in range(4):
                gcol[base + k] = turned[:, 32 * k : 32 * k + 32].astype(bf16)
            return c

        lax.fori_loop(0, count // 4, go, 0, unroll=PREP_UNROLL if count // 4 % PREP_UNROLL == 0 else 1)

    def rim_scale(t):
        return jnp.where(t < rim0 + E, has_below, has_above)

    def weight(s, t):
        return jnp.maximum(dot(gcol[s], feat[t]), 0.0)

    def density_part(s, t):
        w = weight(s, t)
        return jnp.sum(w * w * w, axis=0, keepdims=True)

    prepare(0, cells, lambda t: None)

    def own_density(t, c):
        selfd[pl.ds(t, 1), :] = density_part(t, t)
        return c

    lax.fori_loop(0, cells, own_density, 0, unroll=16)

    zrow = lax.broadcasted_iota(jnp.int32, (cells + 8 * peers + 16, 2 * npair), 0)
    ghost_row = cells + ((zrow - cells) >> 3) * 4 + (zrow & 3)
    rim_row = zrow - (cells + 8 * peers)
    rim_block = jnp.where((rim_row & 7) < E, rim0 + (rim_row >> 3) * E + (rim_row & 7), -2)
    block_of = jnp.where(zrow < cells, zrow, jnp.where(rim_row < 0, ghost_row, rim_block))
    zmat[...] = jnp.where(vecs[0:1, 0 : 2 * npair] == block_of, 1.0, 0.0).astype(bf16)

    wait_all(0, x_src, x_dst, x_rims)
    prepare(cells, ghosts, lambda t: None)
    prepare(rim0, 2 * E, rim_scale)

    def pair_density(g, c):
        for u in range(DENS_UNROLL):
            n = g * DENS_UNROLL + u
            a = ints[n]
            b = ints[npair + n]
            dpart[pl.ds(n, 1), :] = density_part(b, a)
            dpart[pl.ds(npair + n, 1), :] = density_part(a, b)
        return c

    lax.fori_loop(0, npair // DENS_UNROLL, pair_density, 0)

    acc[...] = exact_dot(zmat[...], dpart[...])

    d_src = lambda q: acc.at[pl.ds(pl.multiple_of(cells + 8 * q, 8), 8)]
    d_dst = lambda q: rd.at[pl.ds(pl.multiple_of(8 * q, 8), 8)]
    rim_at = cells + 8 * peers
    d_rims = rim_copies(
        2, acc.at[pl.ds(rim_at + 8, 8)], rdr.at[0], acc.at[pl.ds(rim_at, 8)], rdr.at[1]
    )
    send_all(2, d_src, d_dst, d_rims)
    rd[pl.ds(pl.multiple_of(8 * me, 8), 8), :] = acc[pl.ds(pl.multiple_of(cells + 8 * me, 8), 8), :]
    own_row = lax.broadcasted_iota(jnp.int32, (cells, 8 * peers), 0)
    zrecv = jnp.where(vecs[1:2, 0 : 8 * peers] == own_row, 1.0, 0.0).astype(bf16)
    wait_all(2, d_src, d_dst, d_rims)
    selfd[...] = selfd[...] + acc[0:cells, :] + exact_dot(zrecv, rd[...])
    selfd[0:E, :] = selfd[0:E, :] + rdr[0, 0:E, :] * has_below
    selfd[cells - E : cells, :] = selfd[cells - E : cells, :] + rdr[1, 0:E, :] * has_above
    gate = kg[cells : 2 * cells, :]
    density = selfd[...]
    dens_out[...] = density * gate
    invt[0:cells, :] = jnp.where(gate > 0.0, 1.0 / jnp.where(gate > 0.0, density, 1.0), 0.0)
    kt[0:cells, :] = kg[0:cells, :]

    def stage_inverse(q, c):
        for k in range(slots):
            pick = ints[2 * npair + q * slots + k]
            si[q, k : k + 1, :] = invt[pl.ds(pick, 1), :]
            si[q, slots + k : slots + k + 1, :] = kt[pl.ds(pick, 1), :]
        return c

    lax.fori_loop(0, peers, stage_inverse, 0, unroll=4)
    for side, start in ((0, cells - E), (1, 0)):
        sir[side, 0:E, :] = invt[start : start + E, :]
        sir[side, 8 : 8 + E, :] = kt[start : start + E, :]
    i_src = lambda q: si.at[q]
    i_dst = lambda q: ri.at[q]
    i_rims = rim_copies(3, sir.at[0], rir.at[0], sir.at[1], rir.at[1])
    send_all(3, i_src, i_dst, i_rims)
    ri[me] = si[me]

    def coefficients(t, scale):
        base = t * 4
        mu = wide(xt[pl.ds(base + 3, 1), :])
        if scale is not None:
            mu = mu * scale
        inv = wide(invt[pl.ds(t, 1), :])
        y4 = yt[pl.ds(pl.multiple_of(base, 4), 4), :]
        y8 = jnp.concatenate([y4, jnp.ones_like(y4)], axis=0)
        place = mu * xd[t]
        press = jnp.where(top, 1.0, (6.0 * press_coef) * inv + tension_coef) * place
        flow = (mu * inv) * y8
        linear = jnp.where(top, 0.0, (-0.5 * tension_coef) * mu * place)
        square = jnp.concatenate([press, flow], axis=0)
        line = jnp.concatenate([linear, jnp.zeros_like(linear)], axis=0)
        sh, sl = split2(square)
        lh, ll = split2(line)
        coef[t, 0:16, 0:128] = sh
        coef[t, 16:32, 0:128] = sl
        coef[t, 0:16, 128:256] = lh
        coef[t, 16:32, 128:256] = ll

    def stage_weight(slot, s, t):
        w = weight(s, t)
        qh, ql = split2(w * w)
        wh, wl = split2(w)
        wtile[slot, 0:128, 0:128] = qh
        wtile[slot, 0:128, 128:256] = ql
        wtile[slot, 128:256, 0:128] = wh
        wtile[slot, 128:256, 128:256] = wl

    def force_part(slot, s, t, heat):
        out = dot(coef[s], wtile[slot])
        out = out[0:16, 0:128] + out[0:16, 128:256] + out[16:32, 0:128] + out[16:32, 128:256]
        ae = out[0:8]
        flow = out[8:16]
        moved = xd[t] * jnp.where(top, wide(ae[3:4]), wide(ae[7:8])) - ae
        y4 = yt[pl.ds(t * 4, 4), :]
        carried = flow[0:4] - y4 * flow[4:5]
        gain = jnp.where(row8[0:4] == 3, jnp.broadcast_to(heat, (4, 128)), visc_coef)
        inv = invt[pl.ds(t, 1), :]
        return inv * ((6.0 * press_coef) * moved[0:4] + gain * carried) + moved[4:8]

    def own_coef(t, c):
        coefficients(t, None)
        return c

    lax.fori_loop(0, cells, own_coef, 0, unroll=4)

    def own_force(g, c):
        for u in range(SELF_UNROLL):
            t = g * SELF_UNROLL + u
            stage_weight(u, t, t)
        for u in range(SELF_UNROLL):
            t = g * SELF_UNROLL + u
            part = force_part(u, t, t, kt[pl.ds(t, 1), :])
            for k in range(4):
                selfr[k, pl.ds(t, 1), :] = part[k : k + 1, :]
        return c

    lax.fori_loop(0, cells // SELF_UNROLL, own_force, 0)

    wait_all(1, y_src, y_dst, y_rims)
    wait_all(3, i_src, i_dst, i_rims)

    def spread(q, c):
        invt[pl.ds(cells + 4 * q, 4), :] = ri[q, 0:4, :]
        kt[pl.ds(cells + 4 * q, 4), :] = ri[q, 4:8, :]
        return c

    lax.fori_loop(0, peers, spread, 0, unroll=4)
    for side in range(2):
        invt[rim0 + side * E : rim0 + side * E + E, :] = rir[side, 0:E, :]
        kt[rim0 + side * E : rim0 + side * E + E, :] = rir[side, 8 : 8 + E, :]

    def ghost_coef(t, c):
        coefficients(cells + t, None)
        return c

    lax.fori_loop(0, ghosts, ghost_coef, 0, unroll=4)

    def rim_coef(t, c):
        coefficients(rim0 + t, rim_scale(rim0 + t))
        return c

    lax.fori_loop(0, 2 * E, rim_coef, 0, unroll=4)

    def pair_force(g, c):
        def fill(h, c):
            for v in range(FILL):
                u = h * FILL + v
                a = ints[g * UNROLL + u]
                b = ints[npair + g * UNROLL + u]
                stage_weight(2 * u, b, a)
                stage_weight(2 * u + 1, a, b)
            return c

        def use(h, c):
            for v in range(USE):
                u = h * USE + v
                n = g * UNROLL + u
                a = ints[n]
                b = ints[npair + n]
                ka = kt[pl.ds(a, 1), :]
                kb = kt[pl.ds(b, 1), :]
                heat = 2.0 * ka * kb / (ka + kb)
                first = force_part(2 * u, b, a, heat)
                second = force_part(2 * u + 1, a, b, heat)
                for k in range(4):
                    rpart[k, pl.ds(n, 1), :] = first[k : k + 1, :]
                    rpart[k, pl.ds(npair + n, 1), :] = second[k : k + 1, :]
            return c

        if FILL == UNROLL:
            fill(0, 0)
        else:
            lax.fori_loop(0, UNROLL // FILL, fill, 0)
        if USE == UNROLL:
            use(0, 0)
        else:
            lax.fori_loop(0, UNROLL // USE, use, 0)
        return c

    lax.fori_loop(0, npair // UNROLL, pair_force, 0)

    held = None
    half = (lax.broadcasted_iota(jnp.int32, (8 * peers, 128), 0) & 7) < 4
    for k in range(4):
        sums = exact_dot(zmat[...], rpart[k])
        ownr[k] = sums[0:cells]
        for side in range(2):
            srr[side, 8 * k : 8 * k + 8, :] = sums[rim_at + 8 * side : rim_at + 8 * side + 8]
        lent = sums[cells:rim_at]
        if k % 2 == 0:
            held = lent
        else:
            sr[:, 4 * (k - 1) : 4 * (k - 1) + 8, :] = jnp.where(half, held, lent).reshape(peers, 8, 128)

    r_src = lambda q: sr.at[q]
    r_dst = lambda q: rr.at[q]
    r_rims = rim_copies(4, srr.at[1], rrr.at[0], srr.at[0], rrr.at[1])
    send_all(4, r_src, r_dst, r_rims)
    rr[me] = sr[me]
    drain(0, x_src, x_dst, x_rims)
    drain(1, y_src, y_dst, y_rims)
    drain(2, d_src, d_dst, d_rims)
    drain(3, i_src, i_dst, i_rims)
    wait_all(4, r_src, r_dst, r_rims)
    a, b, c3 = split3(rr[...].reshape(16 * peers, 128))
    parts = jnp.concatenate([a.astype(bf16), b.astype(bf16), c3.astype(bf16)], axis=1)
    own_row = 4 * lax.broadcasted_iota(jnp.int32, (cells, 16 * peers), 0)
    for k in range(4):
        pick = jnp.where(vecs[2:3, 0 : 16 * peers] == own_row + k, 1.0, 0.0).astype(bf16)
        got = dot(pick, parts)
        ownr[k] = ownr[k] + selfr[k] + (got[:, 0:128] + got[:, 128:256] + got[:, 256:384])
        ownr[k, 0:E, :] = ownr[k, 0:E, :] + rrr[0, 8 * k : 8 * k + E, :] * has_below
        ownr[k, cells - E : cells, :] = (
            ownr[k, cells - E : cells, :] + rrr[1, 8 * k : 8 * k + E, :] * has_above
        )
        rates_out[pl.ds(k, cells, stride=4), :] = ownr[k] * gate
    drain(4, r_src, r_dst, r_rims)


def shards(
    grain_coordinates,
    grain_motion_speeds,
    grain_warmth,
    grain_weights,
    cell_grain_tally,
    cell_deposit_tier,
    tier_thermal_coefficient,
    loaned_cell_indices,
    loaned_cell_tally,
    cell_couples,
    couple_entry_tally,
):
    coords = grain_coordinates[0, 0]
    cells, _, lanes = coords.shape
    gate = (jnp.arange(lanes)[None, :] < cell_grain_tally[0, 0][:, None]).astype(f32)
    heat = jnp.sum(
        jnp.where(
            cell_deposit_tier[0, 0][:, None] == jnp.arange(LAYERS)[None, :],
            tier_thermal_coefficient[None, :],
            0.0,
        ),
        axis=1,
    )
    weights = grain_weights[0, 0]
    root = jnp.exp(jnp.log(weights) * (1.0 / 3.0))
    root = root - (root * root * root - weights) / (3.0 * root * root)
    root = root * gate
    state = jnp.concatenate(
        [
            jnp.concatenate([coords - 0.5, root[:, None]], axis=1).reshape(4 * cells, lanes),
            jnp.concatenate([grain_motion_speeds[0, 0], grain_warmth[0, 0][:, None]], axis=1).reshape(
                4 * cells, lanes
            ),
            jnp.broadcast_to(heat[:, None], (cells, lanes)),
            gate,
        ],
        axis=0,
    )
    picks = loaned_cell_indices[0, 0]
    peers, slots = picks.shape
    slabs = lax.axis_size("slab")
    couples = cell_couples[0, 0]
    npair = couples.shape[0]
    ints = jnp.concatenate([couples[:, 0], couples[:, 1], picks.reshape(-1), loaned_cell_tally[0, 0]])
    alive = jnp.arange(npair) < couple_entry_tally[0, 0]
    pair_rows = jnp.where(alive[:, None], couples, -1).T.reshape(-1)
    lent = jnp.where(jnp.arange(slots)[None, :] < loaned_cell_tally[0, 0][:, None], picks, -1)
    lent8 = jnp.concatenate([lent, jnp.full_like(lent, -1)], axis=1).reshape(-1)
    lent16 = jnp.where(
        lent[:, None, :] >= 0, lent[:, None, :] * 4 + jnp.arange(4)[None, :, None], -1
    ).reshape(-1)
    width = max(2 * npair, 16 * peers)
    vecs = jnp.stack(
        [jnp.pad(v, (0, width - v.shape[0]), constant_values=-1) for v in (pair_rows, lent8, lent16)]
        + [jnp.full((width,), -1, jnp.int32)] * 5
    )
    table = cells + slots * peers + 2 * E
    zrows = cells + 8 * peers + 16
    vmem = lambda *shape: pltpu.VMEM(shape, f32)
    density, rates = pl.pallas_call(
        functools.partial(step_kernel, cells, lanes, peers, slabs, npair),
        out_shape=(
            jax.ShapeDtypeStruct((cells, lanes), f32),
            jax.ShapeDtypeStruct((4 * cells, lanes), f32),
        ),
        in_specs=[
            pl.BlockSpec(memory_space=pltpu.SMEM),
            pl.BlockSpec(memory_space=pltpu.VMEM),
            pl.BlockSpec(memory_space=pl.ANY),
        ],
        out_specs=(
            pl.BlockSpec(memory_space=pltpu.VMEM),
            pl.BlockSpec(memory_space=pltpu.VMEM),
        ),
        scratch_shapes=[
            vmem(4 * cells, lanes),
            vmem(4 * cells, lanes),
            vmem(4 * table, lanes),
            vmem(4 * table, lanes),
            vmem(2 * cells, lanes),
            vmem(peers, 16, lanes),
            vmem(peers, 16, lanes),
            pltpu.VMEM((table, 32, lanes), bf16),
            pltpu.VMEM((table, lanes, 32), bf16),
            pltpu.VMEM((table, 32, 2 * lanes), bf16),
            pltpu.VMEM((2 * UNROLL, 256, 256), bf16),
            vmem(table, 8, lanes),
            vmem(zrows, lanes),
            vmem(2 * npair, lanes),
            vmem(4, 2 * npair, lanes),
            vmem(cells, lanes),
            vmem(4, cells, lanes),
            vmem(4, cells, lanes),
            pltpu.VMEM((zrows, 2 * npair), bf16),
            vmem(8 * peers, lanes),
            vmem(2, 8, lanes),
            vmem(peers, 8, lanes),
            vmem(2, 16, lanes),
            vmem(peers, 8, lanes),
            vmem(2, 16, lanes),
            vmem(table, lanes),
            vmem(table, lanes),
            vmem(peers, 16, lanes),
            vmem(2, 32, lanes),
            vmem(peers, 16, lanes),
            vmem(2, 32, lanes),
            pltpu.SemaphoreType.DMA((3,)),
            pltpu.SemaphoreType.DMA((5, peers + 2)),
            pltpu.SemaphoreType.DMA((5, peers + 2)),
        ],
        compiler_params=pltpu.CompilerParams(
            collective_id=0, has_side_effects=True, vmem_limit_bytes=40 * 1024 * 1024
        ),
        name="force_step",
    )(ints, vecs, state)
    return density[None, None], rates.reshape(1, 1, cells, 4, lanes)


def solution(mesh):
    return jax.shard_map(
        shards,
        mesh=mesh,
        in_specs=(
            P("slab", "plane", None, None, None),
            P("slab", "plane", None, None, None),
            P("slab", "plane", None, None),
            P("slab", "plane", None, None),
            P("slab", "plane", None),
            P("slab", "plane", None),
            P(),
            P("slab", "plane", None, None),
            P("slab", "plane", None),
            P("slab", "plane", None, None),
            P("slab", "plane"),
        ),
        out_specs=(P("slab", "plane", None, None), P("slab", "plane", None, None, None)),
        check_vma=False,
    )
```

```python
import functools
import jax
import jax.numpy as jnp
from jax import lax
from jax.experimental import pallas as pl
from jax.experimental.pallas import tpu as pltpu
from jax.sharding import PartitionSpec as P

E = 6
LAYERS = 8
UNROLL = 16
SELF_UNROLL = 16
DENS_UNROLL = 32
PREP_UNROLL = 8

press_coef = 0.2
visc_coef = 0.1
tension_coef = 2.0

f32 = jnp.float32
bf16 = jnp.bfloat16
MESH = pl.DeviceIdType.MESH


def dot(a, b):
    return lax.dot_general(a, b, (((1,), (0,)), ((), ())), preferred_element_type=f32)


def split2(x):
    hi = x.astype(bf16)
    return hi, (x - hi.astype(f32)).astype(bf16)


def split3(x):
    a = x.astype(bf16).astype(f32)
    b = (x - a).astype(bf16).astype(f32)
    return a, b, x - a - b


def exact_dot(select, values):
    a, b, c = split3(values)
    parts = jnp.concatenate([a.astype(bf16), b.astype(bf16), c.astype(bf16)], axis=1)
    out = dot(select, parts)
    n = values.shape[1]
    return out[:, 0:n] + out[:, n : 2 * n] + out[:, 2 * n : 3 * n]


def wide(row):
    return jnp.broadcast_to(row, (8, 128))


def step_kernel(
    cells,
    lanes,
    peers,
    slabs,
    npair,
    coords_in,
    speeds_in,
    warmth_in,
    weights_in,
    fill_in,
    tier_in,
    heat_in,
    picks_in,
    lent_in,
    couples_in,
    count_in,
    dens_out,
    rates_out,
    coords,
    speeds,
    warmth,
    weights,
    fill,
    tier,
    heat,
    picks,
    picks_row,
    lent,
    lent_row,
    couples,
    couples_row,
    count,
    gate_ref,
    xo,
    yo,
    xt,
    yt,
    sx,
    sy,
    feat,
    gcol,
    coef,
    wbuf,
    xd,
    acc,
    dpart,
    rpart,
    selfd,
    selfr,
    ownr,
    zmat,
    rd,
    rdr,
    si,
    sir,
    ri,
    rir,
    invt,
    kt,
    sr,
    srr,
    rr,
    rrr,
    load_sem,
    send_sem,
    recv_sem,
):
    slots = 4
    ghosts = peers * slots
    rim0 = cells + ghosts
    me = lax.axis_index("plane")
    slab = lax.axis_index("slab")
    below = lax.rem(slab + slabs - 1, slabs)
    above = lax.rem(slab + 1, slabs)
    has_below = jnp.where(slab > 0, 1.0, 0.0).astype(f32)
    has_above = jnp.where(slab < slabs - 1, 1.0, 0.0).astype(f32)
    row8 = lax.broadcasted_iota(jnp.int32, (8, 128), 0)
    top = row8 < 4

    loads = [
        pltpu.make_async_copy(src, dst, load_sem.at[n])
        for n, (src, dst) in enumerate(
            (
                (coords_in, coords),
                (weights_in, weights),
                (fill_in, fill),
                (picks_in, picks),
                (lent_in, lent),
                (speeds_in, speeds),
                (warmth_in, warmth),
                (tier_in, tier),
                (heat_in, heat),
                (picks_in, picks_row),
                (lent_in, lent_row),
                (couples_in, couples),
                (couples_in, couples_row),
                (count_in, count),
            )
        )
    ]
    for load in loads:
        load.start()

    def turn(d):
        q = me + d
        return jnp.where(q >= peers, q - peers, q)

    barrier = pltpu.get_barrier_semaphore()

    def greet(d, c):
        pl.semaphore_signal(
            barrier, inc=1, device_id=(slab, turn(d)), device_id_type=MESH
        )
        return c

    lax.fori_loop(1, peers, greet, 0, unroll=True)
    pl.semaphore_signal(barrier, inc=1, device_id=(below, me), device_id_type=MESH)
    pl.semaphore_signal(barrier, inc=1, device_id=(above, me), device_id_type=MESH)

    def peer_copy(phase, src, dst, d):
        q = turn(d)
        return pltpu.make_async_remote_copy(
            src_ref=src(q),
            dst_ref=dst(me),
            send_sem=send_sem.at[phase, 0],
            recv_sem=recv_sem.at[phase, 0],
            device_id=(slab, q),
            device_id_type=MESH,
        )

    def rim_copies(phase, to_above, in_below, to_below, in_above):
        return (
            pltpu.make_async_remote_copy(
                src_ref=to_above,
                dst_ref=in_below,
                send_sem=send_sem.at[phase, 1],
                recv_sem=recv_sem.at[phase, 1],
                device_id=(above, me),
                device_id_type=MESH,
            ),
            pltpu.make_async_remote_copy(
                src_ref=to_below,
                dst_ref=in_above,
                send_sem=send_sem.at[phase, 2],
                recv_sem=recv_sem.at[phase, 2],
                device_id=(below, me),
                device_id_type=MESH,
            ),
        )

    def send_all(phase, src, dst, rims):
        def go(d, c):
            peer_copy(phase, src, dst, d).start()
            return c

        lax.fori_loop(1, peers, go, 0, unroll=True)
        for rim in rims:
            rim.start()

    def wait_all(phase, arrivals, rims):
        pltpu.make_async_copy(arrivals, arrivals, recv_sem.at[phase, 0]).wait()
        for rim in rims:
            rim.wait_recv()

    def drain(phase, arrivals, rims):
        pltpu.make_async_copy(arrivals, arrivals, send_sem.at[phase, 0]).wait()
        for rim in rims:
            rim.wait_send()

    def stage_blocks(table, stage, with_mass):
        def go(q, c):
            here = lent[0, q]
            for k in range(slots):
                pick = picks[k, q]
                block = table[pl.ds(pick * 4, 4), :]
                if with_mass:
                    live = jnp.minimum(jnp.maximum(here - k, 0), 1).astype(f32)
                    block = block * jnp.where(row8[0:4] < 3, 1.0, live)
                stage[q, 4 * k : 4 * k + 4, :] = block
            return c

        lax.fori_loop(0, peers, go, 0, unroll=4)

    x_src = lambda q: sx.at[q]
    x_dst = lambda q: xt.at[pl.ds(pl.multiple_of(4 * cells + 16 * q, 8), 16)]
    x_rims = rim_copies(
        0,
        xo.at[pl.ds(4 * (cells - E), 4 * E)],
        xt.at[pl.ds(4 * rim0, 4 * E)],
        xo.at[pl.ds(0, 4 * E)],
        xt.at[pl.ds(4 * rim0 + 4 * E, 4 * E)],
    )
    y_src = lambda q: sy.at[q]
    y_dst = lambda q: yt.at[pl.ds(pl.multiple_of(4 * cells + 16 * q, 8), 16)]
    y_rims = rim_copies(
        1,
        yo.at[pl.ds(4 * (cells - E), 4 * E)],
        yt.at[pl.ds(4 * rim0, 4 * E)],
        yo.at[pl.ds(0, 4 * E)],
        yt.at[pl.ds(4 * rim0 + 4 * E, 4 * E)],
    )

    x_all = xt.at[pl.ds(4 * cells, 16 * (peers - 1))]
    y_all = yt.at[pl.ds(4 * cells, 16 * (peers - 1))]

    def column(row):
        up = lax.broadcasted_iota(jnp.int32, (cells, cells), 0)
        along = lax.broadcasted_iota(jnp.int32, (cells, cells), 1)
        return jnp.sum(jnp.where(up == along, row.astype(f32), 0.0), axis=1, keepdims=True)

    for n in range(5):
        loads[n].wait()
    place = lax.broadcasted_iota(jnp.int32, (cells, lanes), 1).astype(f32)
    gate_ref[...] = jnp.where(place < column(fill[...]), 1.0, 0.0)
    mass = weights[...]
    root = jnp.exp(jnp.log(mass) * (1.0 / 3.0))
    root = root - (root * root * root - mass) / (3.0 * root * root)
    for c in range(3):
        xo[pl.ds(c, cells, stride=4), :] = coords[c] - 0.5
    xo[pl.ds(3, cells, stride=4), :] = root * gate_ref[...]
    stage_blocks(xo, sx, True)
    pl.semaphore_wait(barrier, peers + 1)
    send_all(0, x_src, x_dst, x_rims)
    xt[0 : 4 * cells, :] = xo[...]
    xt[pl.ds(pl.multiple_of(4 * cells + 16 * me, 8), 16), :] = sx[me]
    for n in range(5, 14):
        loads[n].wait()
    for c in range(3):
        yo[pl.ds(c, cells, stride=4), :] = speeds[c]
    yo[pl.ds(3, cells, stride=4), :] = warmth[...]
    stage_blocks(yo, sy, False)
    send_all(1, y_src, y_dst, y_rims)
    yt[0 : 4 * cells, :] = yo[...]
    yt[pl.ds(pl.multiple_of(4 * cells + 16 * me, 8), 16), :] = sy[me]
    layer = column(tier[...])
    conduct = jnp.zeros((cells, lanes), f32)
    for n in range(LAYERS):
        conduct = jnp.where(layer == float(n), heat[0, n], conduct)
    kt[0:cells, :] = conduct

    def features(t, scale):
        base = t * 4
        x0, x1, x2, mu = (wide(xt[pl.ds(base + c, 1), :]) for c in range(4))
        if scale is not None:
            mu = mu * scale
        rm = row8 & 3
        sq = x0 * x0 + x1 * x1 + x2 * x2
        xyz = jnp.where(rm == 0, x0, jnp.where(rm == 1, x1, x2))
        last = rm == 3
        xd[t] = jnp.where(last, 1.0, xyz)
        q1, q2, q3 = split3(jnp.where(last, -sq, xyz))
        ones = jnp.where(row8 < 3, 1.0, 0.0)
        feat[t] = jnp.concatenate(
            [jnp.where(top, q1, q2), jnp.where(top, q3, q1), jnp.where(top, q2, q1), ones], axis=0
        ).astype(bf16)
        p1, p2, p3 = split3(mu * jnp.where(last, 1.0, xyz * 2.0))
        u1, u2, u3 = split3(mu * (1.0 - sq))
        tail = jnp.where(
            row8 == 0, u1, jnp.where(row8 == 1, u2, jnp.where(row8 == 2, u3, 0.0))
        )
        return [p1, jnp.where(top, p1, p2), jnp.where(top, p2, p3), tail]

    def prepare(first, count, scale):
        def go(g, c):
            base = first + g * 4
            tiles = []
            for k in range(4):
                tiles += features(base + k, scale(base + k))
            turned = jnp.concatenate(tiles, axis=0).T
            for k in range(4):
                gcol[base + k] = turned[:, 32 * k : 32 * k + 32].astype(bf16)
            return c

        lax.fori_loop(0, count // 4, go, 0, unroll=PREP_UNROLL if count // 4 % PREP_UNROLL == 0 else 1)

    def rim_scale(t):
        return jnp.where(t < rim0 + E, has_below, has_above)

    def weight(s, t):
        return jnp.maximum(dot(gcol[s], feat[t]), 0.0)

    def density_part(slot, s, t):
        w = weight(s, t)
        wbuf[slot] = w
        return jnp.sum(w * w * w, axis=0, keepdims=True)

    prepare(0, cells, lambda t: None)

    def own_density(t, c):
        selfd[pl.ds(t, 1), :] = density_part(2 * npair + t, t, t)
        return c

    lax.fori_loop(0, cells, own_density, 0, unroll=16)

    zrow = lax.broadcasted_iota(jnp.int32, (cells + 8 * peers + 16, 2 * npair), 0)
    ghost_row = cells + ((zrow - cells) >> 3) * 4 + (zrow & 3)
    rim_row = zrow - (cells + 8 * peers)
    rim_block = jnp.where((rim_row & 7) < E, rim0 + (rim_row >> 3) * E + (rim_row & 7), -2)
    block_of = jnp.where(zrow < cells, zrow, jnp.where(rim_row < 0, ghost_row, rim_block))
    alive = lax.broadcasted_iota(jnp.int32, (1, npair), 1) < count[0, 0]
    ends = jnp.concatenate(
        [jnp.where(alive, couples_row[0:1, :], -1), jnp.where(alive, couples_row[1:2, :], -1)], axis=1
    )
    zmat[...] = jnp.where(ends == block_of, 1.0, 0.0).astype(bf16)

    wait_all(0, x_all, x_rims)
    prepare(cells, ghosts, lambda t: None)
    prepare(rim0, 2 * E, rim_scale)

    def pair_density(g, c):
        for u in range(DENS_UNROLL):
            n = g * DENS_UNROLL + u
            a = couples[0, n]
            b = couples[1, n]
            dpart[pl.ds(n, 1), :] = density_part(n, b, a)
            dpart[pl.ds(npair + n, 1), :] = density_part(npair + n, a, b)
        return c

    lax.fori_loop(0, npair // DENS_UNROLL, pair_density, 0)

    acc[...] = exact_dot(zmat[...], dpart[...])

    d_src = lambda q: acc.at[pl.ds(pl.multiple_of(cells + 8 * q, 8), 8)]
    d_dst = lambda q: rd.at[pl.ds(pl.multiple_of(8 * q, 8), 8)]
    rim_at = cells + 8 * peers
    d_rims = rim_copies(
        2, acc.at[pl.ds(rim_at + 8, 8)], rdr.at[0], acc.at[pl.ds(rim_at, 8)], rdr.at[1]
    )
    send_all(2, d_src, d_dst, d_rims)
    rd[pl.ds(pl.multiple_of(8 * me, 8), 8), :] = acc[pl.ds(pl.multiple_of(cells + 8 * me, 8), 8), :]
    back = jnp.concatenate(
        [jnp.where(lent_row[...] > k, picks_row[k : k + 1, :], -1) for k in range(slots)], axis=1
    )
    own_row = lax.broadcasted_iota(jnp.int32, (cells, ghosts), 0)
    zback = jnp.where(back == own_row, 1.0, 0.0).astype(bf16)
    base = selfd[...] + acc[0:cells, :]
    d_all = rd.at[pl.ds(0, 8 * (peers - 1))]
    wait_all(2, d_all, d_rims)
    got = jnp.concatenate([rd[pl.ds(k, peers, stride=8), :] for k in range(slots)], axis=0)
    selfd[...] = base + exact_dot(zback, got)
    selfd[0:E, :] = selfd[0:E, :] + rdr[0, 0:E, :] * has_below
    selfd[cells - E : cells, :] = selfd[cells - E : cells, :] + rdr[1, 0:E, :] * has_above
    gate = gate_ref[...]
    density = selfd[...]
    dens_out[...] = density * gate
    invt[0:cells, :] = jnp.where(gate > 0.0, 1.0 / jnp.where(gate > 0.0, density, 1.0), 0.0)

    def stage_inverse(q, c):
        for k in range(slots):
            pick = picks[k, q]
            si[q, k : k + 1, :] = invt[pl.ds(pick, 1), :]
            si[q, slots + k : slots + k + 1, :] = kt[pl.ds(pick, 1), :]
        return c

    lax.fori_loop(0, peers, stage_inverse, 0, unroll=4)
    for side, start in ((0, cells - E), (1, 0)):
        sir[side, 0:E, :] = invt[start : start + E, :]
        sir[side, 8 : 8 + E, :] = kt[start : start + E, :]
    i_src = lambda q: si.at[q]
    i_dst = lambda q: ri.at[q]
    i_rims = rim_copies(3, sir.at[0], rir.at[0], sir.at[1], rir.at[1])
    send_all(3, i_src, i_dst, i_rims)
    ri[me] = si[me]

    def coefficients(t, scale):
        base = t * 4
        mu = wide(xt[pl.ds(base + 3, 1), :])
        if scale is not None:
            mu = mu * scale
        inv = wide(invt[pl.ds(t, 1), :])
        y4 = yt[pl.ds(pl.multiple_of(base, 4), 4), :]
        y8 = jnp.concatenate([y4, jnp.ones_like(y4)], axis=0)
        place = mu * xd[t]
        press = jnp.where(top, 1.0, (6.0 * press_coef) * inv + tension_coef) * place
        flow = (mu * inv) * y8
        linear = jnp.where(top, 0.0, (-0.5 * tension_coef) * mu * place)
        square = jnp.concatenate([press, flow], axis=0)
        line = jnp.concatenate([linear, jnp.zeros_like(linear)], axis=0)
        sh, sl = split2(square)
        lh, ll = split2(line)
        coef[t, 0:16, 0:128] = sh
        coef[t, 16:32, 0:128] = sl
        coef[t, 0:16, 128:256] = lh
        coef[t, 16:32, 128:256] = ll

    def force_part(slot, s, t, heat):
        w = wbuf[slot]
        qh, ql = split2(w * w)
        wh, wl = split2(w)
        tile = jnp.concatenate(
            [jnp.concatenate([qh, ql], axis=1), jnp.concatenate([wh, wl], axis=1)], axis=0
        )
        out = dot(coef[s], tile)
        out = out[0:16, 0:128] + out[0:16, 128:256] + out[16:32, 0:128] + out[16:32, 128:256]
        ae = out[0:8]
        flow = out[8:16]
        moved = xd[t] * jnp.where(top, wide(ae[3:4]), wide(ae[7:8])) - ae
        y4 = yt[pl.ds(t * 4, 4), :]
        carried = flow[0:4] - y4 * flow[4:5]
        gain = jnp.where(row8[0:4] == 3, jnp.broadcast_to(heat, (4, 128)), visc_coef)
        inv = invt[pl.ds(t, 1), :]
        return inv * ((6.0 * press_coef) * moved[0:4] + gain * carried) + moved[4:8]

    def own_coef(t, c):
        coefficients(t, None)
        return c

    lax.fori_loop(0, cells, own_coef, 0, unroll=4)

    def own_force(t, c):
        part = force_part(2 * npair + t, t, t, kt[pl.ds(t, 1), :])
        for k in range(4):
            selfr[k, pl.ds(t, 1), :] = part[k : k + 1, :]
        return c

    lax.fori_loop(0, cells, own_force, 0, unroll=SELF_UNROLL)

    wait_all(1, y_all, y_rims)
    wait_all(3, ri.at[pl.ds(0, peers - 1)], i_rims)

    def spread(q, c):
        invt[pl.ds(cells + 4 * q, 4), :] = ri[q, 0:4, :]
        kt[pl.ds(cells + 4 * q, 4), :] = ri[q, 4:8, :]
        return c

    lax.fori_loop(0, peers, spread, 0, unroll=4)
    for side in range(2):
        invt[rim0 + side * E : rim0 + side * E + E, :] = rir[side, 0:E, :]
        kt[rim0 + side * E : rim0 + side * E + E, :] = rir[side, 8 : 8 + E, :]

    def ghost_coef(t, c):
        coefficients(cells + t, None)
        return c

    lax.fori_loop(0, ghosts, ghost_coef, 0, unroll=4)

    def rim_coef(t, c):
        coefficients(rim0 + t, rim_scale(rim0 + t))
        return c

    lax.fori_loop(0, 2 * E, rim_coef, 0, unroll=4)

    def pair_force(g, c):
        for u in range(UNROLL):
            n = g * UNROLL + u
            a = couples[0, n]
            b = couples[1, n]
            ka = kt[pl.ds(a, 1), :]
            kb = kt[pl.ds(b, 1), :]
            heat = 2.0 * ka * kb / (ka + kb)
            first = force_part(n, b, a, heat)
            second = force_part(npair + n, a, b, heat)
            for k in range(4):
                rpart[k, pl.ds(n, 1), :] = first[k : k + 1, :]
                rpart[k, pl.ds(npair + n, 1), :] = second[k : k + 1, :]
        return c

    lax.fori_loop(0, npair // UNROLL, pair_force, 0)

    held = None
    half = (lax.broadcasted_iota(jnp.int32, (8 * peers, 128), 0) & 7) < 4
    for k in range(4):
        sums = exact_dot(zmat[...], rpart[k])
        ownr[k] = sums[0:cells]
        for side in range(2):
            srr[side, 8 * k : 8 * k + 8, :] = sums[rim_at + 8 * side : rim_at + 8 * side + 8]
        lent = sums[cells:rim_at]
        if k % 2 == 0:
            held = lent
        else:
            sr[:, 4 * (k - 1) : 4 * (k - 1) + 8, :] = jnp.where(half, held, lent).reshape(peers, 8, 128)

    r_src = lambda q: sr.at[q]
    r_dst = lambda q: rr.at[pl.ds(pl.multiple_of(16 * q, 8), 16)]
    r_rims = rim_copies(4, srr.at[1], rrr.at[0], srr.at[0], rrr.at[1])
    send_all(4, r_src, r_dst, r_rims)
    rr[pl.ds(pl.multiple_of(16 * me, 8), 16), :] = sr[me]
    drain(0, x_all, x_rims)
    drain(1, y_all, y_rims)
    drain(2, d_all, d_rims)
    drain(3, ri.at[pl.ds(0, peers - 1)], i_rims)
    r_all = rr.at[pl.ds(0, 16 * (peers - 1))]
    wait_all(4, r_all, r_rims)
    for k in range(4):
        got = jnp.concatenate(
            [rr[pl.ds(4 * k + n, peers, stride=16), :] for n in range(slots)], axis=0
        )
        ownr[k] = ownr[k] + selfr[k] + exact_dot(zback, got)
        ownr[k, 0:E, :] = ownr[k, 0:E, :] + rrr[0, 8 * k : 8 * k + E, :] * has_below
        ownr[k, cells - E : cells, :] = (
            ownr[k, cells - E : cells, :] + rrr[1, 8 * k : 8 * k + E, :] * has_above
        )
        rates_out[pl.ds(k, cells, stride=4), :] = ownr[k] * gate
    drain(4, r_all, r_rims)


def shards(
    grain_coordinates,
    grain_motion_speeds,
    grain_warmth,
    grain_weights,
    cell_grain_tally,
    cell_deposit_tier,
    tier_thermal_coefficient,
    loaned_cell_indices,
    loaned_cell_tally,
    cell_couples,
    couple_entry_tally,
):
    coords = grain_coordinates[0, 0].transpose(1, 0, 2)
    speeds = grain_motion_speeds[0, 0].transpose(1, 0, 2)
    _, cells, lanes = coords.shape
    picks = loaned_cell_indices[0, 0].T
    slots, peers = picks.shape
    slabs = lax.axis_size("slab")
    couples = cell_couples[0, 0].T
    npair = couples.shape[1]
    table = cells + slots * peers + 2 * E
    zrows = cells + 8 * peers + 16
    vmem = lambda *shape: pltpu.VMEM(shape, f32)
    density, rates = pl.pallas_call(
        functools.partial(step_kernel, cells, lanes, peers, slabs, npair),
        out_shape=(
            jax.ShapeDtypeStruct((cells, lanes), f32),
            jax.ShapeDtypeStruct((4 * cells, lanes), f32),
        ),
        in_specs=[pl.BlockSpec(memory_space=pl.ANY)] * 11,
        out_specs=(
            pl.BlockSpec(memory_space=pltpu.VMEM),
            pl.BlockSpec(memory_space=pltpu.VMEM),
        ),
        scratch_shapes=[
            vmem(3, cells, lanes),
            vmem(3, cells, lanes),
            vmem(cells, lanes),
            vmem(cells, lanes),
            pltpu.VMEM((1, cells), jnp.int32),
            pltpu.VMEM((1, cells), jnp.int32),
            pltpu.SMEM((1, LAYERS), f32),
            pltpu.SMEM((slots, peers), jnp.int32),
            pltpu.VMEM((slots, peers), jnp.int32),
            pltpu.SMEM((1, peers), jnp.int32),
            pltpu.VMEM((1, peers), jnp.int32),
            pltpu.SMEM((2, npair), jnp.int32),
            pltpu.VMEM((2, npair), jnp.int32),
            pltpu.SMEM((1, 1), jnp.int32),
            vmem(cells, lanes),
            vmem(4 * cells, lanes),
            vmem(4 * cells, lanes),
            vmem(4 * table, lanes),
            vmem(4 * table, lanes),
            vmem(peers, 16, lanes),
            vmem(peers, 16, lanes),
            pltpu.VMEM((table, 32, lanes), bf16),
            pltpu.VMEM((table, lanes, 32), bf16),
            pltpu.VMEM((table, 32, 2 * lanes), bf16),
            vmem(2 * npair + cells, lanes, lanes),
            vmem(table, 8, lanes),
            vmem(zrows, lanes),
            vmem(2 * npair, lanes),
            vmem(4, 2 * npair, lanes),
            vmem(cells, lanes),
            vmem(4, cells, lanes),
            vmem(4, cells, lanes),
            pltpu.VMEM((zrows, 2 * npair), bf16),
            vmem(8 * peers, lanes),
            vmem(2, 8, lanes),
            vmem(peers, 8, lanes),
            vmem(2, 16, lanes),
            vmem(peers, 8, lanes),
            vmem(2, 16, lanes),
            vmem(table, lanes),
            vmem(table, lanes),
            vmem(peers, 16, lanes),
            vmem(2, 32, lanes),
            vmem(16 * peers, lanes),
            vmem(2, 32, lanes),
            pltpu.SemaphoreType.DMA((14,)),
            pltpu.SemaphoreType.DMA((5, 3)),
            pltpu.SemaphoreType.DMA((5, 3)),
        ],
        compiler_params=pltpu.CompilerParams(
            collective_id=0, has_side_effects=True, vmem_limit_bytes=60 * 1024 * 1024
        ),
        name="force_step",
    )(
        coords,
        speeds,
        grain_warmth[0, 0],
        grain_weights[0, 0],
        cell_grain_tally[0],
        cell_deposit_tier[0],
        tier_thermal_coefficient[None],
        picks,
        loaned_cell_tally[0],
        couples,
        couple_entry_tally,
    )
    return density[None, None], rates.reshape(1, 1, cells, 4, lanes)


def solution(mesh):
    return jax.shard_map(
        shards,
        mesh=mesh,
        in_specs=(
            P("slab", "plane", None, None, None),
            P("slab", "plane", None, None, None),
            P("slab", "plane", None, None),
            P("slab", "plane", None, None),
            P("slab", "plane", None),
            P("slab", "plane", None),
            P(),
            P("slab", "plane", None, None),
            P("slab", "plane", None),
            P("slab", "plane", None, None),
            P("slab", "plane"),
        ),
        out_specs=(P("slab", "plane", None, None), P("slab", "plane", None, None, None)),
        check_vma=False,
    )
```

```python
import functools
import jax
import jax.numpy as jnp
from jax import lax
from jax.experimental import pallas as pl
from jax.experimental.pallas import tpu as pltpu
from jax.sharding import PartitionSpec as P

E = 6
LAYERS = 8
UNROLL = 32
SELF_UNROLL = 16
DENS_UNROLL = 32
PREP_UNROLL = 8

press_coef = 0.2
visc_coef = 0.1
tension_coef = 2.0

f32 = jnp.float32
bf16 = jnp.bfloat16
MESH = pl.DeviceIdType.MESH


def dot(a, b):
    return lax.dot_general(a, b, (((1,), (0,)), ((), ())), preferred_element_type=f32)


def split2(x):
    hi = x.astype(bf16)
    return hi, (x - hi.astype(f32)).astype(bf16)


def split3(x):
    a = x.astype(bf16).astype(f32)
    b = (x - a).astype(bf16).astype(f32)
    return a, b, x - a - b


def exact_dot(select, values):
    a, b, c = split3(values)
    parts = jnp.concatenate([a.astype(bf16), b.astype(bf16), c.astype(bf16)], axis=1)
    out = dot(select, parts)
    n = values.shape[1]
    return out[:, 0:n] + out[:, n : 2 * n] + out[:, 2 * n : 3 * n]


def wide(row):
    return jnp.broadcast_to(row, (8, 128))


def step_kernel(
    cells,
    lanes,
    peers,
    slabs,
    npair,
    coords_in,
    speeds_in,
    warmth_in,
    weights_in,
    fill_in,
    tier_in,
    heat_in,
    picks_in,
    lent_in,
    couples_in,
    count_in,
    dens_out,
    rates_out,
    coords,
    speeds,
    warmth,
    weights,
    fill,
    tier,
    heat,
    picks,
    picks_row,
    lent,
    lent_row,
    couples,
    couples_row,
    count,
    gate_ref,
    xo,
    yo,
    xt,
    yt,
    sx,
    sy,
    feat,
    gcol,
    wbuf,
    xd,
    acc,
    dpart,
    rpart,
    selfd,
    selfr,
    ownr,
    zown,
    zlent,
    rd,
    rdr,
    si,
    sir,
    ri,
    rir,
    invt,
    kt,
    sr,
    srr,
    rr,
    rrr,
    load_sem,
    send_sem,
    recv_sem,
):
    slots = 4
    ghosts = peers * slots
    rim0 = cells + ghosts
    me = lax.axis_index("plane")
    slab = lax.axis_index("slab")
    below = lax.rem(slab + slabs - 1, slabs)
    above = lax.rem(slab + 1, slabs)
    has_below = jnp.where(slab > 0, 1.0, 0.0).astype(f32)
    has_above = jnp.where(slab < slabs - 1, 1.0, 0.0).astype(f32)
    row8 = lax.broadcasted_iota(jnp.int32, (8, 128), 0)
    top = row8 < 4

    loads = [
        pltpu.make_async_copy(src, dst, load_sem.at[n])
        for n, (src, dst) in enumerate(
            (
                (coords_in, coords),
                (weights_in, weights),
                (fill_in, fill),
                (picks_in, picks),
                (lent_in, lent),
                (speeds_in, speeds),
                (warmth_in, warmth),
                (tier_in, tier),
                (heat_in, heat),
                (picks_in, picks_row),
                (lent_in, lent_row),
                (couples_in, couples),
                (couples_in, couples_row),
                (count_in, count),
            )
        )
    ]
    for load in loads:
        load.start()

    def turn(d):
        q = me + d
        return jnp.where(q >= peers, q - peers, q)

    barrier = pltpu.get_barrier_semaphore()

    def greet(d, c):
        pl.semaphore_signal(
            barrier, inc=1, device_id=(slab, turn(d)), device_id_type=MESH
        )
        return c

    lax.fori_loop(1, peers, greet, 0, unroll=True)
    pl.semaphore_signal(barrier, inc=1, device_id=(below, me), device_id_type=MESH)
    pl.semaphore_signal(barrier, inc=1, device_id=(above, me), device_id_type=MESH)

    def peer_copy(phase, src, dst, d):
        q = turn(d)
        return pltpu.make_async_remote_copy(
            src_ref=src(q),
            dst_ref=dst(me),
            send_sem=send_sem.at[phase, 0],
            recv_sem=recv_sem.at[phase, 0],
            device_id=(slab, q),
            device_id_type=MESH,
        )

    def rim_copies(phase, to_above, in_below, to_below, in_above):
        return (
            pltpu.make_async_remote_copy(
                src_ref=to_above,
                dst_ref=in_below,
                send_sem=send_sem.at[phase, 1],
                recv_sem=recv_sem.at[phase, 1],
                device_id=(above, me),
                device_id_type=MESH,
            ),
            pltpu.make_async_remote_copy(
                src_ref=to_below,
                dst_ref=in_above,
                send_sem=send_sem.at[phase, 2],
                recv_sem=recv_sem.at[phase, 2],
                device_id=(below, me),
                device_id_type=MESH,
            ),
        )

    def send_all(phase, src, dst, rims):
        def go(d, c):
            peer_copy(phase, src, dst, d).start()
            return c

        lax.fori_loop(1, peers, go, 0, unroll=True)
        for rim in rims:
            rim.start()

    def wait_all(phase, arrivals, rims):
        pltpu.make_async_copy(arrivals, arrivals, recv_sem.at[phase, 0]).wait()
        for rim in rims:
            rim.wait_recv()

    def drain(phase, arrivals, rims):
        pltpu.make_async_copy(arrivals, arrivals, send_sem.at[phase, 0]).wait()
        for rim in rims:
            rim.wait_send()

    def stage_blocks(table, stage, with_mass):
        def go(q, c):
            here = lent[0, q]
            for k in range(slots):
                pick = picks[k, q]
                block = table[pl.ds(pick * 4, 4), :]
                if with_mass:
                    live = jnp.minimum(jnp.maximum(here - k, 0), 1).astype(f32)
                    block = block * jnp.where(row8[0:4] < 3, 1.0, live)
                stage[q, 4 * k : 4 * k + 4, :] = block
            return c

        lax.fori_loop(0, peers, go, 0, unroll=4)

    x_src = lambda q: sx.at[q]
    x_dst = lambda q: xt.at[pl.ds(pl.multiple_of(4 * cells + 16 * q, 8), 16)]
    x_rims = rim_copies(
        0,
        xo.at[pl.ds(4 * (cells - E), 4 * E)],
        xt.at[pl.ds(4 * rim0, 4 * E)],
        xo.at[pl.ds(0, 4 * E)],
        xt.at[pl.ds(4 * rim0 + 4 * E, 4 * E)],
    )
    y_src = lambda q: sy.at[q]
    y_dst = lambda q: yt.at[pl.ds(pl.multiple_of(4 * cells + 16 * q, 8), 16)]
    y_rims = rim_copies(
        1,
        yo.at[pl.ds(4 * (cells - E), 4 * E)],
        yt.at[pl.ds(4 * rim0, 4 * E)],
        yo.at[pl.ds(0, 4 * E)],
        yt.at[pl.ds(4 * rim0 + 4 * E, 4 * E)],
    )

    x_all = xt.at[pl.ds(4 * cells, 16 * (peers - 1))]
    y_all = yt.at[pl.ds(4 * cells, 16 * (peers - 1))]

    def column(row):
        up = lax.broadcasted_iota(jnp.int32, (cells, cells), 0)
        along = lax.broadcasted_iota(jnp.int32, (cells, cells), 1)
        return jnp.sum(jnp.where(up == along, row.astype(f32), 0.0), axis=1, keepdims=True)

    for n in range(5):
        loads[n].wait()
    place = lax.broadcasted_iota(jnp.int32, (cells, lanes), 1).astype(f32)
    gate_ref[...] = jnp.where(place < column(fill[...]), 1.0, 0.0)
    mass = weights[...]
    root = jnp.exp(jnp.log(mass) * (1.0 / 3.0))
    root = root - (root * root * root - mass) / (3.0 * root * root)
    for c in range(3):
        xo[pl.ds(c, cells, stride=4), :] = coords[c] - 0.5
    xo[pl.ds(3, cells, stride=4), :] = root * gate_ref[...]
    stage_blocks(xo, sx, True)
    pl.semaphore_wait(barrier, peers + 1)
    send_all(0, x_src, x_dst, x_rims)
    xt[0 : 4 * cells, :] = xo[...]
    xt[pl.ds(pl.multiple_of(4 * cells + 16 * me, 8), 16), :] = sx[me]
    for n in range(5, 14):
        loads[n].wait()
    for c in range(3):
        yo[pl.ds(c, cells, stride=4), :] = speeds[c]
    yo[pl.ds(3, cells, stride=4), :] = warmth[...]
    stage_blocks(yo, sy, False)
    send_all(1, y_src, y_dst, y_rims)
    yt[0 : 4 * cells, :] = yo[...]
    yt[pl.ds(pl.multiple_of(4 * cells + 16 * me, 8), 16), :] = sy[me]
    layer = column(tier[...])
    conduct = jnp.zeros((cells, lanes), f32)
    for n in range(LAYERS):
        conduct = jnp.where(layer == float(n), heat[0, n], conduct)
    kt[0:cells, :] = conduct

    def features(t, scale):
        base = t * 4
        x0, x1, x2, mu = (wide(xt[pl.ds(base + c, 1), :]) for c in range(4))
        if scale is not None:
            mu = mu * scale
        rm = row8 & 3
        sq = x0 * x0 + x1 * x1 + x2 * x2
        xyz = jnp.where(rm == 0, x0, jnp.where(rm == 1, x1, x2))
        last = rm == 3
        xd[t] = jnp.where(last, 1.0, xyz)
        q1, q2, q3 = split3(jnp.where(last, -sq, xyz))
        ones = jnp.where(row8 < 3, 1.0, 0.0)
        feat[t] = jnp.concatenate(
            [jnp.where(top, q1, q2), jnp.where(top, q3, q1), jnp.where(top, q2, q1), ones], axis=0
        ).astype(bf16)
        p1, p2, p3 = split3(mu * jnp.where(last, 1.0, xyz * 2.0))
        u1, u2, u3 = split3(mu * (1.0 - sq))
        tail = jnp.where(
            row8 == 0, u1, jnp.where(row8 == 1, u2, jnp.where(row8 == 2, u3, 0.0))
        )
        return [p1, jnp.where(top, p1, p2), jnp.where(top, p2, p3), tail]

    def prepare(first, count, scale):
        def go(g, c):
            base = first + g * 4
            tiles = []
            for k in range(4):
                tiles += features(base + k, scale(base + k))
            turned = jnp.concatenate(tiles, axis=0).T
            for k in range(4):
                gcol[base + k, :, 0:32] = turned[:, 32 * k : 32 * k + 32].astype(bf16)
            return c

        lax.fori_loop(0, count // 4, go, 0, unroll=PREP_UNROLL if count // 4 % PREP_UNROLL == 0 else 1)

    def rim_scale(t):
        return jnp.where(t < rim0 + E, has_below, has_above)

    def weight(s, t):
        return jnp.maximum(dot(gcol[s, :, 0:32], feat[t]), 0.0)

    def density_part(slot, s, t):
        w = weight(s, t)
        wbuf[slot] = w
        return jnp.sum(w * w * w, axis=0, keepdims=True)

    prepare(0, cells, lambda t: None)

    def own_density(t, c):
        selfd[pl.ds(t, 1), :] = density_part(2 * npair + t, t, t)
        return c

    lax.fori_loop(0, cells, own_density, 0, unroll=16)

    alive = lax.broadcasted_iota(jnp.int32, (1, npair), 1) < count[0, 0]
    first = jnp.where(alive, couples_row[0:1, :], -1)
    second = jnp.where(alive, couples_row[1:2, :], -1)
    own_block = lax.broadcasted_iota(jnp.int32, (cells, npair), 0)
    zown[:, 0:npair] = jnp.where(first == own_block, 1.0, 0.0).astype(bf16)
    zown[:, npair : 2 * npair] = jnp.where(second == own_block, 1.0, 0.0).astype(bf16)
    rim_at = 8 * peers
    zrow = lax.broadcasted_iota(jnp.int32, (rim_at + 16, npair), 0)
    ghost_row = cells + (zrow >> 3) * 4 + (zrow & 3)
    rim_row = zrow - rim_at
    rim_block = jnp.where((rim_row & 7) < E, rim0 + (rim_row >> 3) * E + (rim_row & 7), -2)
    zlent[...] = jnp.where(second == jnp.where(rim_row < 0, ghost_row, rim_block), 1.0, 0.0).astype(bf16)

    wait_all(0, x_all, x_rims)
    prepare(cells, ghosts, lambda t: None)
    prepare(rim0, 2 * E, rim_scale)

    def second_density(g, c):
        for u in range(DENS_UNROLL):
            n = g * DENS_UNROLL + u
            dpart[pl.ds(npair + n, 1), :] = density_part(npair + n, couples[0, n], couples[1, n])
        return c

    lax.fori_loop(0, npair // DENS_UNROLL, second_density, 0)
    acc[...] = exact_dot(zlent[...], dpart[npair : 2 * npair, :])

    d_src = lambda q: acc.at[pl.ds(pl.multiple_of(8 * q, 8), 8)]
    d_dst = lambda q: rd.at[pl.ds(pl.multiple_of(8 * q, 8), 8)]
    d_rims = rim_copies(
        2, acc.at[pl.ds(rim_at + 8, 8)], rdr.at[0], acc.at[pl.ds(rim_at, 8)], rdr.at[1]
    )
    send_all(2, d_src, d_dst, d_rims)
    rd[pl.ds(pl.multiple_of(8 * me, 8), 8), :] = acc[pl.ds(pl.multiple_of(8 * me, 8), 8), :]

    def first_density(g, c):
        for u in range(DENS_UNROLL):
            n = g * DENS_UNROLL + u
            dpart[pl.ds(n, 1), :] = density_part(n, couples[1, n], couples[0, n])
        return c

    lax.fori_loop(0, npair // DENS_UNROLL, first_density, 0)

    back = jnp.concatenate(
        [jnp.where(lent_row[...] > k, picks_row[k : k + 1, :], -1) for k in range(slots)], axis=1
    )
    own_row = lax.broadcasted_iota(jnp.int32, (cells, ghosts), 0)
    zback = jnp.where(back == own_row, 1.0, 0.0).astype(bf16)
    base = selfd[...] + exact_dot(zown[...], dpart[...])
    d_all = rd.at[pl.ds(0, 8 * (peers - 1))]
    wait_all(2, d_all, d_rims)
    got = jnp.concatenate([rd[pl.ds(k, peers, stride=8), :] for k in range(slots)], axis=0)
    selfd[...] = base + exact_dot(zback, got)
    selfd[0:E, :] = selfd[0:E, :] + rdr[0, 0:E, :] * has_below
    selfd[cells - E : cells, :] = selfd[cells - E : cells, :] + rdr[1, 0:E, :] * has_above
    gate = gate_ref[...]
    density = selfd[...]
    dens_out[...] = density * gate
    invt[0:cells, :] = jnp.where(gate > 0.0, 1.0 / jnp.where(gate > 0.0, density, 1.0), 0.0)

    def stage_inverse(q, c):
        for k in range(slots):
            pick = picks[k, q]
            si[q, k : k + 1, :] = invt[pl.ds(pick, 1), :]
            si[q, slots + k : slots + k + 1, :] = kt[pl.ds(pick, 1), :]
        return c

    lax.fori_loop(0, peers, stage_inverse, 0, unroll=4)
    for side, start in ((0, cells - E), (1, 0)):
        sir[side, 0:E, :] = invt[start : start + E, :]
        sir[side, 8 : 8 + E, :] = kt[start : start + E, :]
    i_src = lambda q: si.at[q]
    i_dst = lambda q: ri.at[q]
    i_rims = rim_copies(3, sir.at[0], rir.at[0], sir.at[1], rir.at[1])
    send_all(3, i_src, i_dst, i_rims)
    ri[me] = si[me]

    def coefficients(t, scale):
        base = t * 4
        mu = wide(xt[pl.ds(base + 3, 1), :])
        if scale is not None:
            mu = mu * scale
        inv = wide(invt[pl.ds(t, 1), :])
        y4 = yt[pl.ds(pl.multiple_of(base, 4), 4), :]
        y8 = jnp.concatenate([y4, jnp.ones_like(y4)], axis=0)
        place = mu * xd[t]
        press = jnp.where(top, 1.0, (6.0 * press_coef) * inv + tension_coef) * place
        flow = (mu * inv) * y8
        linear = jnp.where(top, 0.0, (-0.5 * tension_coef) * mu * place)
        square = jnp.concatenate([press, flow], axis=0)
        line = jnp.concatenate([linear, jnp.zeros_like(linear)], axis=0)
        sh, sl = split2(square)
        lh, ll = split2(line)
        gcol[t, 0:16, :] = sh
        gcol[t, 16:32, :] = sl
        gcol[t, 32:48, :] = lh
        gcol[t, 48:64, :] = ll

    def force_part(slot, s, t, heat):
        w = wbuf[slot]
        qh, ql = split2(w * w)
        wh, wl = split2(w)
        tile = jnp.concatenate(
            [jnp.concatenate([qh, ql], axis=1), jnp.concatenate([wh, wl], axis=1)], axis=0
        )
        out = dot(jnp.concatenate([gcol[s, 0:32, :], gcol[s, 32:64, :]], axis=1), tile)
        out = out[0:16, 0:128] + out[0:16, 128:256] + out[16:32, 0:128] + out[16:32, 128:256]
        ae = out[0:8]
        flow = out[8:16]
        moved = xd[t] * jnp.where(top, wide(ae[3:4]), wide(ae[7:8])) - ae
        y4 = yt[pl.ds(t * 4, 4), :]
        carried = flow[0:4] - y4 * flow[4:5]
        gain = jnp.where(row8[0:4] == 3, jnp.broadcast_to(heat, (4, 128)), visc_coef)
        inv = invt[pl.ds(t, 1), :]
        return inv * ((6.0 * press_coef) * moved[0:4] + gain * carried) + moved[4:8]

    def own_coef(t, c):
        coefficients(t, None)
        return c

    lax.fori_loop(0, cells, own_coef, 0, unroll=4)

    def own_force(t, c):
        part = force_part(2 * npair + t, t, t, kt[pl.ds(t, 1), :])
        for k in range(4):
            selfr[k, pl.ds(t, 1), :] = part[k : k + 1, :]
        return c

    lax.fori_loop(0, cells, own_force, 0, unroll=SELF_UNROLL)

    wait_all(1, y_all, y_rims)
    wait_all(3, ri.at[pl.ds(0, peers - 1)], i_rims)

    def spread(q, c):
        invt[pl.ds(cells + 4 * q, 4), :] = ri[q, 0:4, :]
        kt[pl.ds(cells + 4 * q, 4), :] = ri[q, 4:8, :]
        return c

    lax.fori_loop(0, peers, spread, 0, unroll=4)
    for side in range(2):
        invt[rim0 + side * E : rim0 + side * E + E, :] = rir[side, 0:E, :]
        kt[rim0 + side * E : rim0 + side * E + E, :] = rir[side, 8 : 8 + E, :]

    def ghost_coef(t, c):
        coefficients(cells + t, None)
        return c

    lax.fori_loop(0, ghosts, ghost_coef, 0, unroll=4)

    def rim_coef(t, c):
        coefficients(rim0 + t, rim_scale(rim0 + t))
        return c

    lax.fori_loop(0, 2 * E, rim_coef, 0, unroll=4)

    def pair_force(slot, s, t):
        ks = kt[pl.ds(s, 1), :]
        kd = kt[pl.ds(t, 1), :]
        part = force_part(slot, s, t, 2.0 * ks * kd / (ks + kd))
        for k in range(4):
            rpart[k, pl.ds(slot, 1), :] = part[k : k + 1, :]

    def second_force(g, c):
        for u in range(UNROLL):
            n = g * UNROLL + u
            pair_force(npair + n, couples[0, n], couples[1, n])
        return c

    lax.fori_loop(0, npair // UNROLL, second_force, 0)

    held = None
    half = (lax.broadcasted_iota(jnp.int32, (8 * peers, 128), 0) & 7) < 4
    for k in range(4):
        sums = exact_dot(zlent[...], rpart[k, npair : 2 * npair, :])
        for side in range(2):
            srr[side, 8 * k : 8 * k + 8, :] = sums[rim_at + 8 * side : rim_at + 8 * side + 8]
        lent_sums = sums[0:rim_at]
        if k % 2 == 0:
            held = lent_sums
        else:
            sr[:, 4 * (k - 1) : 4 * (k - 1) + 8, :] = jnp.where(half, held, lent_sums).reshape(
                peers, 8, 128
            )

    r_src = lambda q: sr.at[q]
    r_dst = lambda q: rr.at[pl.ds(pl.multiple_of(16 * q, 8), 16)]
    r_rims = rim_copies(4, srr.at[1], rrr.at[0], srr.at[0], rrr.at[1])
    send_all(4, r_src, r_dst, r_rims)
    rr[pl.ds(pl.multiple_of(16 * me, 8), 16), :] = sr[me]

    def first_force(g, c):
        for u in range(UNROLL):
            n = g * UNROLL + u
            pair_force(n, couples[1, n], couples[0, n])
        return c

    lax.fori_loop(0, npair // UNROLL, first_force, 0)
    for k in range(4):
        ownr[k] = selfr[k] + exact_dot(zown[...], rpart[k])
    drain(0, x_all, x_rims)
    drain(1, y_all, y_rims)
    drain(2, d_all, d_rims)
    drain(3, ri.at[pl.ds(0, peers - 1)], i_rims)
    r_all = rr.at[pl.ds(0, 16 * (peers - 1))]
    wait_all(4, r_all, r_rims)
    for k in range(4):
        got = jnp.concatenate(
            [rr[pl.ds(4 * k + n, peers, stride=16), :] for n in range(slots)], axis=0
        )
        ownr[k] = ownr[k] + exact_dot(zback, got)
        ownr[k, 0:E, :] = ownr[k, 0:E, :] + rrr[0, 8 * k : 8 * k + E, :] * has_below
        ownr[k, cells - E : cells, :] = (
            ownr[k, cells - E : cells, :] + rrr[1, 8 * k : 8 * k + E, :] * has_above
        )
        rates_out[pl.ds(k, cells, stride=4), :] = ownr[k] * gate
    drain(4, r_all, r_rims)


def shards(
    grain_coordinates,
    grain_motion_speeds,
    grain_warmth,
    grain_weights,
    cell_grain_tally,
    cell_deposit_tier,
    tier_thermal_coefficient,
    loaned_cell_indices,
    loaned_cell_tally,
    cell_couples,
    couple_entry_tally,
):
    coords = grain_coordinates[0, 0].transpose(1, 0, 2)
    speeds = grain_motion_speeds[0, 0].transpose(1, 0, 2)
    _, cells, lanes = coords.shape
    picks = loaned_cell_indices[0, 0].T
    slots, peers = picks.shape
    slabs = lax.axis_size("slab")
    couples = cell_couples[0, 0].T
    npair = couples.shape[1]
    table = cells + slots * peers + 2 * E
    vmem = lambda *shape: pltpu.VMEM(shape, f32)
    density, rates = pl.pallas_call(
        functools.partial(step_kernel, cells, lanes, peers, slabs, npair),
        out_shape=(
            jax.ShapeDtypeStruct((cells, lanes), f32),
            jax.ShapeDtypeStruct((4 * cells, lanes), f32),
        ),
        in_specs=[pl.BlockSpec(memory_space=pl.ANY)] * 11,
        out_specs=(
            pl.BlockSpec(memory_space=pltpu.VMEM),
            pl.BlockSpec(memory_space=pltpu.VMEM),
        ),
        scratch_shapes=[
            vmem(3, cells, lanes),
            vmem(3, cells, lanes),
            vmem(cells, lanes),
            vmem(cells, lanes),
            pltpu.VMEM((1, cells), jnp.int32),
            pltpu.VMEM((1, cells), jnp.int32),
            pltpu.SMEM((1, LAYERS), f32),
            pltpu.SMEM((slots, peers), jnp.int32),
            pltpu.VMEM((slots, peers), jnp.int32),
            pltpu.SMEM((1, peers), jnp.int32),
            pltpu.VMEM((1, peers), jnp.int32),
            pltpu.SMEM((2, npair), jnp.int32),
            pltpu.VMEM((2, npair), jnp.int32),
            pltpu.SMEM((1, 1), jnp.int32),
            vmem(cells, lanes),
            vmem(4 * cells, lanes),
            vmem(4 * cells, lanes),
            vmem(4 * table, lanes),
            vmem(4 * table, lanes),
            vmem(peers, 16, lanes),
            vmem(peers, 16, lanes),
            pltpu.VMEM((table, 32, lanes), bf16),
            pltpu.VMEM((table, lanes, lanes), bf16),
            vmem(2 * npair + cells, lanes, lanes),
            vmem(table, 8, lanes),
            vmem(8 * peers + 16, lanes),
            vmem(2 * npair, lanes),
            vmem(4, 2 * npair, lanes),
            vmem(cells, lanes),
            vmem(4, cells, lanes),
            vmem(4, cells, lanes),
            pltpu.VMEM((cells, 2 * npair), bf16),
            pltpu.VMEM((8 * peers + 16, npair), bf16),
            vmem(8 * peers, lanes),
            vmem(2, 8, lanes),
            vmem(peers, 8, lanes),
            vmem(2, 16, lanes),
            vmem(peers, 8, lanes),
            vmem(2, 16, lanes),
            vmem(table, lanes),
            vmem(table, lanes),
            vmem(peers, 16, lanes),
            vmem(2, 32, lanes),
            vmem(16 * peers, lanes),
            vmem(2, 32, lanes),
            pltpu.SemaphoreType.DMA((14,)),
            pltpu.SemaphoreType.DMA((5, 3)),
            pltpu.SemaphoreType.DMA((5, 3)),
        ],
        compiler_params=pltpu.CompilerParams(
            collective_id=0, has_side_effects=True, vmem_limit_bytes=60 * 1024 * 1024
        ),
        name="force_step",
    )(
        coords,
        speeds,
        grain_warmth[0, 0],
        grain_weights[0, 0],
        cell_grain_tally[0],
        cell_deposit_tier[0],
        tier_thermal_coefficient[None],
        picks,
        loaned_cell_tally[0],
        couples,
        couple_entry_tally,
    )
    return density[None, None], rates.reshape(1, 1, cells, 4, lanes)


def solution(mesh):
    return jax.shard_map(
        shards,
        mesh=mesh,
        in_specs=(
            P("slab", "plane", None, None, None),
            P("slab", "plane", None, None, None),
            P("slab", "plane", None, None),
            P("slab", "plane", None, None),
            P("slab", "plane", None),
            P("slab", "plane", None),
            P(),
            P("slab", "plane", None, None),
            P("slab", "plane", None),
            P("slab", "plane", None, None),
            P("slab", "plane"),
        ),
        out_specs=(P("slab", "plane", None, None), P("slab", "plane", None, None, None)),
        check_vma=False,
    )
```

```python
import functools
import jax
import jax.numpy as jnp
from jax import lax
from jax.experimental import pallas as pl
from jax.experimental.pallas import tpu as pltpu
from jax.sharding import PartitionSpec as P

E = 6
LAYERS = 8
UNROLL = 32
SELF_UNROLL = 16
DENS_UNROLL = 32
PREP_UNROLL = 8
PEER_UNROLL = 6

press_coef = 0.2
visc_coef = 0.1
tension_coef = 2.0

f32 = jnp.float32
bf16 = jnp.bfloat16
MESH = pl.DeviceIdType.MESH


def dot(a, b):
    return lax.dot_general(a, b, (((1,), (0,)), ((), ())), preferred_element_type=f32)


def split2(x):
    hi = x.astype(bf16)
    return hi, (x - hi.astype(f32)).astype(bf16)


def split3(x):
    a = x.astype(bf16).astype(f32)
    b = (x - a).astype(bf16).astype(f32)
    return a, b, x - a - b


def exact_dot(select, values):
    a, b, c = split3(values)
    parts = jnp.concatenate([a.astype(bf16), b.astype(bf16), c.astype(bf16)], axis=1)
    out = dot(select, parts)
    n = values.shape[1]
    return out[:, 0:n] + out[:, n : 2 * n] + out[:, 2 * n : 3 * n]


def wide(row):
    return jnp.broadcast_to(row, (8, 128))


def step_kernel(
    cells,
    lanes,
    peers,
    slabs,
    npair,
    coords_in,
    speeds_in,
    warmth_in,
    weights_in,
    fill_in,
    tier_in,
    heat_in,
    picks_in,
    lent_in,
    couples_in,
    count_in,
    dens_out,
    rates_out,
    coords,
    speeds,
    warmth,
    weights,
    fill,
    tier,
    heat,
    picks,
    picks_row,
    lent,
    lent_row,
    couples,
    couples_row,
    count,
    gate_ref,
    xo,
    yo,
    xt,
    yt,
    sx,
    sy,
    syr,
    ry,
    ryr,
    feat,
    gcol,
    wbuf,
    xd,
    acc,
    dpart,
    rpart,
    raw,
    selfd,
    selfr,
    ownr,
    zown,
    zlent,
    rd,
    rdr,
    si,
    sir,
    ri,
    rir,
    invt,
    kt,
    sr,
    srr,
    rr,
    rrr,
    load_sem,
    send_sem,
    recv_sem,
    state_sem,
):
    slots = 4
    ghosts = peers * slots
    rim0 = cells + ghosts
    me = lax.axis_index("plane")
    slab = lax.axis_index("slab")
    below = lax.rem(slab + slabs - 1, slabs)
    above = lax.rem(slab + 1, slabs)
    has_below = jnp.where(slab > 0, 1.0, 0.0).astype(f32)
    has_above = jnp.where(slab < slabs - 1, 1.0, 0.0).astype(f32)
    row8 = lax.broadcasted_iota(jnp.int32, (8, 128), 0)
    top = row8 < 4

    loads = [
        pltpu.make_async_copy(src, dst, load_sem.at[n])
        for n, (src, dst) in enumerate(
            (
                (coords_in, coords),
                (weights_in, weights),
                (fill_in, fill),
                (picks_in, picks),
                (lent_in, lent),
                (speeds_in, speeds),
                (warmth_in, warmth),
                (tier_in, tier),
                (heat_in, heat),
                (picks_in, picks_row),
                (lent_in, lent_row),
                (couples_in, couples),
                (couples_in, couples_row),
                (count_in, count),
            )
        )
    ]
    for load in loads:
        load.start()

    def turn(d):
        q = me + d
        return jnp.where(q >= peers, q - peers, q)

    barrier = pltpu.get_barrier_semaphore()

    def greet(d, c):
        pl.semaphore_signal(
            barrier, inc=1, device_id=(slab, turn(d)), device_id_type=MESH
        )
        return c

    lax.fori_loop(1, peers, greet, 0, unroll=True)
    pl.semaphore_signal(barrier, inc=1, device_id=(below, me), device_id_type=MESH)
    pl.semaphore_signal(barrier, inc=1, device_id=(above, me), device_id_type=MESH)

    def peer_copy(phase, src, dst, d):
        q = turn(d)
        return pltpu.make_async_remote_copy(
            src_ref=src(q),
            dst_ref=dst(me),
            send_sem=send_sem.at[phase, 0],
            recv_sem=state_sem.at[me] if phase == 0 else recv_sem.at[phase, 0],
            device_id=(slab, q),
            device_id_type=MESH,
        )

    def rim_copies(phase, to_above, in_below, to_below, in_above):
        return (
            pltpu.make_async_remote_copy(
                src_ref=to_above,
                dst_ref=in_below,
                send_sem=send_sem.at[phase, 1],
                recv_sem=recv_sem.at[phase, 1],
                device_id=(above, me),
                device_id_type=MESH,
            ),
            pltpu.make_async_remote_copy(
                src_ref=to_below,
                dst_ref=in_above,
                send_sem=send_sem.at[phase, 2],
                recv_sem=recv_sem.at[phase, 2],
                device_id=(below, me),
                device_id_type=MESH,
            ),
        )

    def send_all(phase, src, dst, rims):
        def go(d, c):
            peer_copy(phase, src, dst, d).start()
            return c

        lax.fori_loop(1, peers, go, 0, unroll=True)
        for rim in rims:
            rim.start()

    def wait_all(phase, arrivals, rims):
        pltpu.make_async_copy(arrivals, arrivals, recv_sem.at[phase, 0]).wait()
        for rim in rims:
            rim.wait_recv()

    def drain(phase, arrivals, rims):
        pltpu.make_async_copy(arrivals, arrivals, send_sem.at[phase, 0]).wait()
        for rim in rims:
            rim.wait_send()

    def stage_state(q, c):
        here = lent[0, q]
        for k in range(slots):
            block = xo[pl.ds(picks[k, q] * 4, 4), :]
            live = jnp.minimum(jnp.maximum(here - k, 0), 1).astype(f32)
            sx[q, 4 * k : 4 * k + 4, :] = block * jnp.where(row8[0:4] < 3, 1.0, live)
        return c

    def stage_flow(q, c):
        for k in range(slots):
            sy[q, 4 * k : 4 * k + 4, :] = yo[pl.ds(picks[k, q] * 4, 4), :]
            heats = kt[pl.ds(picks[k, q], 1), :]
            sy[q, 16 + k : 17 + k, :] = heats
            sy[q, 20 + k : 21 + k, :] = heats
        return c

    x_src = lambda q: sx.at[q]
    x_dst = lambda q: xt.at[pl.ds(pl.multiple_of(4 * cells + 16 * q, 8), 16)]
    x_rims = rim_copies(
        0,
        xo.at[pl.ds(4 * (cells - E), 4 * E)],
        xt.at[pl.ds(4 * rim0, 4 * E)],
        xo.at[pl.ds(0, 4 * E)],
        xt.at[pl.ds(4 * rim0 + 4 * E, 4 * E)],
    )
    y_src = lambda q: sy.at[q]
    y_dst = lambda q: ry.at[q]
    y_rims = rim_copies(1, syr.at[0], ryr.at[0], syr.at[1], ryr.at[1])
    x_all = xt.at[pl.ds(4 * cells, 16 * (peers - 1))]
    y_all = ry.at[pl.ds(0, peers - 1)]

    def column(row):
        up = lax.broadcasted_iota(jnp.int32, (cells, cells), 0)
        along = lax.broadcasted_iota(jnp.int32, (cells, cells), 1)
        return jnp.sum(jnp.where(up == along, row.astype(f32), 0.0), axis=1, keepdims=True)

    for n in range(5):
        loads[n].wait()
    place = lax.broadcasted_iota(jnp.int32, (cells, lanes), 1).astype(f32)
    gate_ref[...] = jnp.where(place < column(fill[...]), 1.0, 0.0)
    mass = weights[...]
    root = jnp.exp(jnp.log(mass) * (1.0 / 3.0))
    root = root - (root * root * root - mass) / (3.0 * root * root)
    for c in range(3):
        xo[pl.ds(c, cells, stride=4), :] = coords[c] - 0.5
    xo[pl.ds(3, cells, stride=4), :] = root * gate_ref[...]
    lax.fori_loop(0, peers, stage_state, 0, unroll=4)
    pl.semaphore_wait(barrier, peers + 1)
    send_all(0, x_src, x_dst, x_rims)
    xt[0 : 4 * cells, :] = xo[...]
    xt[pl.ds(pl.multiple_of(4 * cells + 16 * me, 8), 16), :] = sx[me]
    for n in range(5, 14):
        loads[n].wait()
    for c in range(3):
        yo[pl.ds(c, cells, stride=4), :] = speeds[c]
    yo[pl.ds(3, cells, stride=4), :] = warmth[...]
    layer = column(tier[...])
    conduct = jnp.zeros((cells, lanes), f32)
    for n in range(LAYERS):
        conduct = jnp.where(layer == float(n), heat[0, n], conduct)
    kt[0:cells, :] = conduct
    lax.fori_loop(0, peers, stage_flow, 0, unroll=4)
    for side, start in ((0, cells - E), (1, 0)):
        syr[side, 0 : 4 * E, :] = yo[4 * start : 4 * (start + E), :]
        syr[side, 24 : 24 + E, :] = conduct[start : start + E, :]
        syr[side, 24 + E : 32, :] = conduct[0 : 8 - E, :]
    send_all(1, y_src, y_dst, y_rims)
    yt[0 : 4 * cells, :] = yo[...]
    ry[me] = sy[me]

    def features(t, scale):
        base = t * 4
        x0, x1, x2, mu = (wide(xt[pl.ds(base + c, 1), :]) for c in range(4))
        if scale is not None:
            mu = mu * scale
        rm = row8 & 3
        sq = x0 * x0 + x1 * x1 + x2 * x2
        xyz = jnp.where(rm == 0, x0, jnp.where(rm == 1, x1, x2))
        last = rm == 3
        xd[t] = jnp.where(last, 1.0, xyz)
        q1, q2, q3 = split3(jnp.where(last, -sq, xyz))
        ones = jnp.where(row8 < 3, 1.0, 0.0)
        feat[t] = jnp.concatenate(
            [jnp.where(top, q1, q2), jnp.where(top, q3, q1), jnp.where(top, q2, q1), ones], axis=0
        ).astype(bf16)
        p1, p2, p3 = split3(mu * jnp.where(last, 1.0, xyz * 2.0))
        u1, u2, u3 = split3(mu * (1.0 - sq))
        tail = jnp.where(
            row8 == 0, u1, jnp.where(row8 == 1, u2, jnp.where(row8 == 2, u3, 0.0))
        )
        return [p1, jnp.where(top, p1, p2), jnp.where(top, p2, p3), tail]

    def prepare(base, scale):
        tiles = []
        for k in range(4):
            tiles += features(base + k, scale(base + k))
        turned = jnp.concatenate(tiles, axis=0).T
        for k in range(4):
            gcol[base + k, :, 0:32] = turned[:, 32 * k : 32 * k + 32].astype(bf16)

    def unscaled(t):
        return None

    def own_prepare(g, c):
        prepare(4 * g, unscaled)
        return c

    def rim_scale(t):
        return jnp.where(t < rim0 + E, has_below, has_above)

    def weight(s, t):
        return jnp.maximum(dot(gcol[s, :, 0:32], feat[t]), 0.0)

    def density_part(slot, s, t):
        w = weight(s, t)
        wbuf[slot] = w
        return jnp.sum(w * w * w, axis=0, keepdims=True)

    lax.fori_loop(0, cells // 4, own_prepare, 0, unroll=PREP_UNROLL)

    def own_density(t, c):
        selfd[pl.ds(t, 1), :] = density_part(2 * npair + t, t, t)
        return c

    lax.fori_loop(0, cells, own_density, 0, unroll=16)

    alive = lax.broadcasted_iota(jnp.int32, (1, npair), 1) < count[0, 0]
    first = jnp.where(alive, couples_row[0:1, :], -1)
    second = jnp.where(alive, couples_row[1:2, :], -1)
    own_block = lax.broadcasted_iota(jnp.int32, (cells, npair), 0)
    zown[:, 0:npair] = jnp.where(first == own_block, 1.0, 0.0).astype(bf16)
    zown[:, npair : 2 * npair] = jnp.where(second == own_block, 1.0, 0.0).astype(bf16)
    rim_at = 8 * peers
    zrow = lax.broadcasted_iota(jnp.int32, (rim_at + 16, npair), 0)
    ghost_row = cells + (zrow >> 3) * 4 + (zrow & 3)
    rim_row = zrow - rim_at
    rim_block = jnp.where((rim_row & 7) < E, rim0 + (rim_row >> 3) * E + (rim_row & 7), -2)
    zlent[...] = jnp.where(second == jnp.where(rim_row < 0, ghost_row, rim_block), 1.0, 0.0).astype(bf16)

    def arrived(d):
        q = jnp.where(me >= d, me - d, me - d + peers)
        block = xt.at[pl.ds(pl.multiple_of(4 * cells + 16 * q, 8), 16)]
        pltpu.make_async_copy(block, block, state_sem.at[q]).wait()
        return q

    def lent_prepare(g, c):
        came = [arrived(1 + g * PEER_UNROLL + u) for u in range(PEER_UNROLL)]
        for q in came:
            prepare(cells + slots * q, unscaled)
        return c

    rounds = (peers - 1) // PEER_UNROLL
    lax.fori_loop(0, rounds, lent_prepare, 0)
    came = [me] + [arrived(d) for d in range(1 + rounds * PEER_UNROLL, peers)]
    for rim in x_rims:
        rim.wait_recv()
    for q in came:
        prepare(cells + slots * q, unscaled)
    for g in range(2 * E // 4):
        prepare(rim0 + 4 * g, rim_scale)

    def second_density(g, c):
        for u in range(DENS_UNROLL):
            n = g * DENS_UNROLL + u
            dpart[pl.ds(npair + n, 1), :] = density_part(npair + n, couples[0, n], couples[1, n])
        return c

    lax.fori_loop(0, npair // DENS_UNROLL, second_density, 0)
    acc[...] = exact_dot(zlent[...], dpart[npair : 2 * npair, :])

    d_src = lambda q: acc.at[pl.ds(pl.multiple_of(8 * q, 8), 8)]
    d_dst = lambda q: rd.at[pl.ds(pl.multiple_of(8 * q, 8), 8)]
    d_rims = rim_copies(
        2, acc.at[pl.ds(rim_at + 8, 8)], rdr.at[0], acc.at[pl.ds(rim_at, 8)], rdr.at[1]
    )
    send_all(2, d_src, d_dst, d_rims)
    rd[pl.ds(pl.multiple_of(8 * me, 8), 8), :] = acc[pl.ds(pl.multiple_of(8 * me, 8), 8), :]

    def first_density(g, c):
        for u in range(DENS_UNROLL):
            n = g * DENS_UNROLL + u
            dpart[pl.ds(n, 1), :] = density_part(n, couples[1, n], couples[0, n])
        return c

    lax.fori_loop(0, npair // DENS_UNROLL, first_density, 0)

    back = jnp.concatenate(
        [jnp.where(lent_row[...] > k, picks_row[k : k + 1, :], -1) for k in range(slots)], axis=1
    )
    own_row = lax.broadcasted_iota(jnp.int32, (cells, ghosts), 0)
    zback = jnp.where(back == own_row, 1.0, 0.0).astype(bf16)
    base = selfd[...] + exact_dot(zown[...], dpart[...])
    d_all = rd.at[pl.ds(0, 8 * (peers - 1))]
    wait_all(2, d_all, d_rims)
    got = jnp.concatenate([rd[pl.ds(k, peers, stride=8), :] for k in range(slots)], axis=0)
    selfd[...] = base + exact_dot(zback, got)
    selfd[0:E, :] = selfd[0:E, :] + rdr[0, 0:E, :] * has_below
    selfd[cells - E : cells, :] = selfd[cells - E : cells, :] + rdr[1, 0:E, :] * has_above
    gate = gate_ref[...]
    density = selfd[...]
    dens_out[...] = density * gate
    invt[0:cells, :] = jnp.where(gate > 0.0, 1.0 / jnp.where(gate > 0.0, density, 1.0), 0.0)

    def stage_inverse(q, c):
        for k in range(slots):
            si[q, k : k + 1, :] = invt[pl.ds(picks[k, q], 1), :]
        return c

    lax.fori_loop(0, peers, stage_inverse, 0, unroll=4)
    for side, start in ((0, cells - E), (1, 0)):
        sir[side, 0:E, :] = invt[start : start + E, :]
        sir[side, E:8, :] = invt[0 : 8 - E, :]
    i_src = lambda q: si.at[q]
    i_dst = lambda q: ri.at[q]
    i_rims = rim_copies(3, sir.at[0], rir.at[0], sir.at[1], rir.at[1])
    send_all(3, i_src, i_dst, i_rims)
    ri[me] = si[me]

    def coefficients(t, scale):
        base = t * 4
        mu = wide(xt[pl.ds(base + 3, 1), :])
        if scale is not None:
            mu = mu * scale
        inv = wide(invt[pl.ds(t, 1), :])
        y4 = yt[pl.ds(pl.multiple_of(base, 4), 4), :]
        y8 = jnp.concatenate([y4, jnp.ones_like(y4)], axis=0)
        place = mu * xd[t]
        press = jnp.where(top, 1.0, (6.0 * press_coef) * inv + tension_coef) * place
        flow = (mu * inv) * y8
        linear = jnp.where(top, 0.0, (-0.5 * tension_coef) * mu * place)
        square = jnp.concatenate([press, flow], axis=0)
        line = jnp.concatenate([linear, jnp.zeros_like(linear)], axis=0)
        sh, sl = split2(square)
        lh, ll = split2(line)
        gcol[t, 0:16, :] = sh
        gcol[t, 16:32, :] = sl
        gcol[t, 32:48, :] = lh
        gcol[t, 48:64, :] = ll

    def force_sums(slot, s):
        w = wbuf[slot]
        qh, ql = split2(w * w)
        wh, wl = split2(w)
        tile = jnp.concatenate(
            [jnp.concatenate([qh, ql], axis=1), jnp.concatenate([wh, wl], axis=1)], axis=0
        )
        out = dot(jnp.concatenate([gcol[s, 0:32, :], gcol[s, 32:64, :]], axis=1), tile)
        return out[0:16, 0:128] + out[0:16, 128:256] + out[16:32, 0:128] + out[16:32, 128:256]

    def force_at(out, t, heat):
        ae = out[0:8]
        flow = out[8:16]
        moved = xd[t] * jnp.where(top, wide(ae[3:4]), wide(ae[7:8])) - ae
        y4 = yt[pl.ds(t * 4, 4), :]
        carried = flow[0:4] - y4 * flow[4:5]
        gain = jnp.where(row8[0:4] == 3, jnp.broadcast_to(heat, (4, 128)), visc_coef)
        inv = invt[pl.ds(t, 1), :]
        return inv * ((6.0 * press_coef) * moved[0:4] + gain * carried) + moved[4:8]

    def own_coef(t, c):
        coefficients(t, None)
        return c

    lax.fori_loop(0, cells, own_coef, 0, unroll=4)

    def second_sums(g, c):
        for u in range(UNROLL):
            n = g * UNROLL + u
            raw[n] = force_sums(npair + n, couples[0, n])
        return c

    lax.fori_loop(0, npair // UNROLL, second_sums, 0)

    wait_all(1, y_all, y_rims)
    wait_all(3, ri.at[pl.ds(0, peers - 1)], i_rims)

    def spread(q, c):
        invt[pl.ds(cells + 4 * q, 4), :] = ri[q]
        yt[pl.ds(pl.multiple_of(4 * cells + 16 * q, 8), 16), :] = ry[q, 0:16, :]
        kt[pl.ds(cells + 4 * q, 4), :] = ry[q, 16:20, :]
        return c

    lax.fori_loop(0, peers, spread, 0, unroll=4)
    for side in range(2):
        at = rim0 + side * E
        invt[at : at + E, :] = rir[side, 0:E, :]
        yt[4 * at : 4 * (at + E), :] = ryr[side, 0 : 4 * E, :]
        kt[at : at + E, :] = ryr[side, 24 : 24 + E, :]

    def pair_force(slot, sums, s, t):
        ks = kt[pl.ds(s, 1), :]
        kd = kt[pl.ds(t, 1), :]
        part = force_at(sums, t, 2.0 * ks * kd / (ks + kd))
        for k in range(4):
            rpart[k, pl.ds(slot, 1), :] = part[k : k + 1, :]

    def second_force(g, c):
        for u in range(UNROLL):
            n = g * UNROLL + u
            pair_force(npair + n, raw[n], couples[0, n], couples[1, n])
        return c

    lax.fori_loop(0, npair // UNROLL, second_force, 0)

    held = None
    half = (lax.broadcasted_iota(jnp.int32, (8 * peers, 128), 0) & 7) < 4
    for k in range(4):
        sums = exact_dot(zlent[...], rpart[k, npair : 2 * npair, :])
        for side in range(2):
            srr[side, 8 * k : 8 * k + 8, :] = sums[rim_at + 8 * side : rim_at + 8 * side + 8]
        lent_sums = sums[0:rim_at]
        if k % 2 == 0:
            held = lent_sums
        else:
            sr[:, 4 * (k - 1) : 4 * (k - 1) + 8, :] = jnp.where(half, held, lent_sums).reshape(
                peers, 8, 128
            )

    r_src = lambda q: sr.at[q]
    r_dst = lambda q: rr.at[pl.ds(pl.multiple_of(16 * q, 8), 16)]
    r_rims = rim_copies(4, srr.at[1], rrr.at[0], srr.at[0], rrr.at[1])
    send_all(4, r_src, r_dst, r_rims)
    rr[pl.ds(pl.multiple_of(16 * me, 8), 16), :] = sr[me]

    def ghost_coef(t, c):
        coefficients(cells + t, None)
        return c

    lax.fori_loop(0, ghosts, ghost_coef, 0, unroll=4)

    def rim_coef(t, c):
        coefficients(rim0 + t, rim_scale(rim0 + t))
        return c

    lax.fori_loop(0, 2 * E, rim_coef, 0, unroll=4)

    def own_force(t, c):
        part = force_at(force_sums(2 * npair + t, t), t, kt[pl.ds(t, 1), :])
        for k in range(4):
            selfr[k, pl.ds(t, 1), :] = part[k : k + 1, :]
        return c

    lax.fori_loop(0, cells, own_force, 0, unroll=SELF_UNROLL)

    def first_force(g, c):
        for u in range(UNROLL):
            n = g * UNROLL + u
            pair_force(n, force_sums(n, couples[1, n]), couples[1, n], couples[0, n])
        return c

    lax.fori_loop(0, npair // UNROLL, first_force, 0)
    for k in range(4):
        ownr[k] = selfr[k] + exact_dot(zown[...], rpart[k])
    drain(0, x_all, x_rims)
    drain(1, y_all, y_rims)
    drain(2, d_all, d_rims)
    drain(3, ri.at[pl.ds(0, peers - 1)], i_rims)
    r_all = rr.at[pl.ds(0, 16 * (peers - 1))]
    wait_all(4, r_all, r_rims)
    for k in range(4):
        got = jnp.concatenate(
            [rr[pl.ds(4 * k + n, peers, stride=16), :] for n in range(slots)], axis=0
        )
        ownr[k] = ownr[k] + exact_dot(zback, got)
        ownr[k, 0:E, :] = ownr[k, 0:E, :] + rrr[0, 8 * k : 8 * k + E, :] * has_below
        ownr[k, cells - E : cells, :] = (
            ownr[k, cells - E : cells, :] + rrr[1, 8 * k : 8 * k + E, :] * has_above
        )
        rates_out[pl.ds(k, cells, stride=4), :] = ownr[k] * gate
    drain(4, r_all, r_rims)


def shards(
    grain_coordinates,
    grain_motion_speeds,
    grain_warmth,
    grain_weights,
    cell_grain_tally,
    cell_deposit_tier,
    tier_thermal_coefficient,
    loaned_cell_indices,
    loaned_cell_tally,
    cell_couples,
    couple_entry_tally,
):
    coords = grain_coordinates[0, 0].transpose(1, 0, 2)
    speeds = grain_motion_speeds[0, 0].transpose(1, 0, 2)
    _, cells, lanes = coords.shape
    picks = loaned_cell_indices[0, 0].T
    slots, peers = picks.shape
    slabs = lax.axis_size("slab")
    couples = cell_couples[0, 0].T
    npair = couples.shape[1]
    table = cells + slots * peers + 2 * E
    vmem = lambda *shape: pltpu.VMEM(shape, f32)
    density, rates = pl.pallas_call(
        functools.partial(step_kernel, cells, lanes, peers, slabs, npair),
        out_shape=(
            jax.ShapeDtypeStruct((cells, lanes), f32),
            jax.ShapeDtypeStruct((4 * cells, lanes), f32),
        ),
        in_specs=[pl.BlockSpec(memory_space=pl.ANY)] * 11,
        out_specs=(
            pl.BlockSpec(memory_space=pltpu.VMEM),
            pl.BlockSpec(memory_space=pltpu.VMEM),
        ),
        scratch_shapes=[
            vmem(3, cells, lanes),
            vmem(3, cells, lanes),
            vmem(cells, lanes),
            vmem(cells, lanes),
            pltpu.VMEM((1, cells), jnp.int32),
            pltpu.VMEM((1, cells), jnp.int32),
            pltpu.SMEM((1, LAYERS), f32),
            pltpu.SMEM((slots, peers), jnp.int32),
            pltpu.VMEM((slots, peers), jnp.int32),
            pltpu.SMEM((1, peers), jnp.int32),
            pltpu.VMEM((1, peers), jnp.int32),
            pltpu.SMEM((2, npair), jnp.int32),
            pltpu.VMEM((2, npair), jnp.int32),
            pltpu.SMEM((1, 1), jnp.int32),
            vmem(cells, lanes),
            vmem(4 * cells, lanes),
            vmem(4 * cells, lanes),
            vmem(4 * table, lanes),
            vmem(4 * table, lanes),
            vmem(peers, 16, lanes),
            vmem(peers, 24, lanes),
            vmem(2, 32, lanes),
            vmem(peers, 24, lanes),
            vmem(2, 32, lanes),
            pltpu.VMEM((table, 32, lanes), bf16),
            pltpu.VMEM((table, lanes, lanes), bf16),
            vmem(2 * npair + cells, lanes, lanes),
            vmem(table, 8, lanes),
            vmem(8 * peers + 16, lanes),
            vmem(2 * npair, lanes),
            vmem(4, 2 * npair, lanes),
            vmem(npair, 16, lanes),
            vmem(cells, lanes),
            vmem(4, cells, lanes),
            vmem(4, cells, lanes),
            pltpu.VMEM((cells, 2 * npair), bf16),
            pltpu.VMEM((8 * peers + 16, npair), bf16),
            vmem(8 * peers, lanes),
            vmem(2, 8, lanes),
            vmem(peers, 4, lanes),
            vmem(2, 8, lanes),
            vmem(peers, 4, lanes),
            vmem(2, 8, lanes),
            vmem(table, lanes),
            vmem(table, lanes),
            vmem(peers, 16, lanes),
            vmem(2, 32, lanes),
            vmem(16 * peers, lanes),
            vmem(2, 32, lanes),
            pltpu.SemaphoreType.DMA((14,)),
            pltpu.SemaphoreType.DMA((5, 3)),
            pltpu.SemaphoreType.DMA((5, 3)),
            pltpu.SemaphoreType.DMA((peers,)),
        ],
        compiler_params=pltpu.CompilerParams(
            collective_id=0, has_side_effects=True, vmem_limit_bytes=60 * 1024 * 1024
        ),
        name="force_step",
    )(
        coords,
        speeds,
        grain_warmth[0, 0],
        grain_weights[0, 0],
        cell_grain_tally[0],
        cell_deposit_tier[0],
        tier_thermal_coefficient[None],
        picks,
        loaned_cell_tally[0],
        couples,
        couple_entry_tally,
    )
    return density[None, None], rates.reshape(1, 1, cells, 4, lanes)


def solution(mesh):
    return jax.shard_map(
        shards,
        mesh=mesh,
        in_specs=(
            P("slab", "plane", None, None, None),
            P("slab", "plane", None, None, None),
            P("slab", "plane", None, None),
            P("slab", "plane", None, None),
            P("slab", "plane", None),
            P("slab", "plane", None),
            P(),
            P("slab", "plane", None, None),
            P("slab", "plane", None),
            P("slab", "plane", None, None),
            P("slab", "plane"),
        ),
        out_specs=(P("slab", "plane", None, None), P("slab", "plane", None, None, None)),
        check_vma=False,
    )
```

```python
import functools
import jax
import jax.numpy as jnp
from jax import lax
from jax.experimental import pallas as pl
from jax.experimental.pallas import tpu as pltpu
from jax.sharding import PartitionSpec as P

E = 6
LAYERS = 8
UNROLL = 64
SELF_UNROLL = 32
DENS_UNROLL = 64
PREP_UNROLL = 8
PEER_UNROLL = 10

press_coef = 0.2
visc_coef = 0.1
tension_coef = 2.0

f32 = jnp.float32
bf16 = jnp.bfloat16
MESH = pl.DeviceIdType.MESH


def dot(a, b):
    return lax.dot_general(a, b, (((1,), (0,)), ((), ())), preferred_element_type=f32)


def split2(x):
    hi = x.astype(bf16)
    return hi, (x - hi.astype(f32)).astype(bf16)


def split3(x):
    a = x.astype(bf16).astype(f32)
    b = (x - a).astype(bf16).astype(f32)
    return a, b, x - a - b


def exact_dot(select, values):
    a, b, c = split3(values)
    parts = jnp.concatenate([a.astype(bf16), b.astype(bf16), c.astype(bf16)], axis=1)
    out = dot(select, parts)
    n = values.shape[1]
    return out[:, 0:n] + out[:, n : 2 * n] + out[:, 2 * n : 3 * n]


def wide(row):
    return jnp.broadcast_to(row, (8, 128))


def step_kernel(
    cells,
    lanes,
    peers,
    slabs,
    npair,
    coords_in,
    speeds_in,
    warmth_in,
    weights_in,
    fill_in,
    tier_in,
    heat_in,
    picks_in,
    lent_in,
    couples_in,
    count_in,
    dens_out,
    rates_out,
    coords,
    speeds,
    warmth,
    weights,
    fill,
    tier,
    heat,
    picks,
    picks_row,
    lent,
    lent_row,
    couples,
    couples_row,
    count,
    gate_ref,
    xo,
    yo,
    xt,
    yt,
    sx,
    sy,
    syr,
    ry,
    ryr,
    feat,
    gcol,
    wbuf,
    xd,
    acc,
    dpart,
    rpart,
    raw,
    selfd,
    selfr,
    ownr,
    zown,
    zlent,
    rd,
    rdr,
    si,
    sir,
    ri,
    rir,
    invt,
    kt,
    sr,
    srr,
    rr,
    rrr,
    load_sem,
    send_sem,
    recv_sem,
    state_sem,
):
    slots = 4
    ghosts = peers * slots
    rim0 = cells + ghosts
    me = lax.axis_index("plane")
    slab = lax.axis_index("slab")
    below = lax.rem(slab + slabs - 1, slabs)
    above = lax.rem(slab + 1, slabs)
    has_below = jnp.where(slab > 0, 1.0, 0.0).astype(f32)
    has_above = jnp.where(slab < slabs - 1, 1.0, 0.0).astype(f32)
    row8 = lax.broadcasted_iota(jnp.int32, (8, 128), 0)
    top = row8 < 4

    loads = [
        pltpu.make_async_copy(src, dst, load_sem.at[n])
        for n, (src, dst) in enumerate(
            (
                (coords_in, coords),
                (weights_in, weights),
                (fill_in, fill),
                (picks_in, picks),
                (lent_in, lent),
                (speeds_in, speeds),
                (warmth_in, warmth),
                (tier_in, tier),
                (heat_in, heat),
                (picks_in, picks_row),
                (lent_in, lent_row),
                (couples_in, couples),
                (couples_in, couples_row),
                (count_in, count),
            )
        )
    ]
    for load in loads:
        load.start()

    def turn(d):
        q = me + d
        return jnp.where(q >= peers, q - peers, q)

    barrier = pltpu.get_barrier_semaphore()

    def greet(d, c):
        pl.semaphore_signal(
            barrier, inc=1, device_id=(slab, turn(d)), device_id_type=MESH
        )
        return c

    lax.fori_loop(1, peers, greet, 0, unroll=True)
    pl.semaphore_signal(barrier, inc=1, device_id=(below, me), device_id_type=MESH)
    pl.semaphore_signal(barrier, inc=1, device_id=(above, me), device_id_type=MESH)

    def peer_copy(phase, src, dst, d):
        q = turn(d)
        return pltpu.make_async_remote_copy(
            src_ref=src(q),
            dst_ref=dst(me),
            send_sem=send_sem.at[phase, 0],
            recv_sem=state_sem.at[me] if phase == 0 else recv_sem.at[phase, 0],
            device_id=(slab, q),
            device_id_type=MESH,
        )

    def rim_copies(phase, to_above, in_below, to_below, in_above):
        return (
            pltpu.make_async_remote_copy(
                src_ref=to_above,
                dst_ref=in_below,
                send_sem=send_sem.at[phase, 1],
                recv_sem=recv_sem.at[phase, 1],
                device_id=(above, me),
                device_id_type=MESH,
            ),
            pltpu.make_async_remote_copy(
                src_ref=to_below,
                dst_ref=in_above,
                send_sem=send_sem.at[phase, 2],
                recv_sem=recv_sem.at[phase, 2],
                device_id=(below, me),
                device_id_type=MESH,
            ),
        )

    def send_all(phase, src, dst, rims):
        def go(d, c):
            peer_copy(phase, src, dst, d).start()
            return c

        lax.fori_loop(1, peers, go, 0, unroll=True)
        for rim in rims:
            rim.start()

    def wait_all(phase, arrivals, rims):
        pltpu.make_async_copy(arrivals, arrivals, recv_sem.at[phase, 0]).wait()
        for rim in rims:
            rim.wait_recv()

    def drain(phase, arrivals, rims):
        pltpu.make_async_copy(arrivals, arrivals, send_sem.at[phase, 0]).wait()
        for rim in rims:
            rim.wait_send()

    def stage_state(q, c):
        here = lent[0, q]
        for k in range(slots):
            block = xo[pl.ds(picks[k, q] * 4, 4), :]
            live = jnp.minimum(jnp.maximum(here - k, 0), 1).astype(f32)
            sx[q, 4 * k : 4 * k + 4, :] = block * jnp.where(row8[0:4] < 3, 1.0, live)
        return c

    def stage_flow(q, c):
        for k in range(slots):
            sy[q, 4 * k : 4 * k + 4, :] = yo[pl.ds(picks[k, q] * 4, 4), :]
            heats = kt[pl.ds(picks[k, q], 1), :]
            sy[q, 16 + k : 17 + k, :] = heats
            sy[q, 20 + k : 21 + k, :] = heats
        return c

    x_src = lambda q: sx.at[q]
    x_dst = lambda q: xt.at[pl.ds(pl.multiple_of(4 * cells + 16 * q, 8), 16)]
    x_rims = rim_copies(
        0,
        xo.at[pl.ds(4 * (cells - E), 4 * E)],
        xt.at[pl.ds(4 * rim0, 4 * E)],
        xo.at[pl.ds(0, 4 * E)],
        xt.at[pl.ds(4 * rim0 + 4 * E, 4 * E)],
    )
    y_src = lambda q: sy.at[q]
    y_dst = lambda q: ry.at[q]
    y_rims = rim_copies(1, syr.at[0], ryr.at[0], syr.at[1], ryr.at[1])
    x_all = xt.at[pl.ds(4 * cells, 16 * (peers - 1))]
    y_all = ry.at[pl.ds(0, peers - 1)]

    def column(row):
        up = lax.broadcasted_iota(jnp.int32, (cells, cells), 0)
        along = lax.broadcasted_iota(jnp.int32, (cells, cells), 1)
        return jnp.sum(jnp.where(up == along, row.astype(f32), 0.0), axis=1, keepdims=True)

    for n in range(5):
        loads[n].wait()
    place = lax.broadcasted_iota(jnp.int32, (cells, lanes), 1).astype(f32)
    gate_ref[...] = jnp.where(place < column(fill[...]), 1.0, 0.0)
    mass = weights[...]
    root = jnp.exp(jnp.log(mass) * (1.0 / 3.0))
    root = root - (root * root * root - mass) / (3.0 * root * root)
    for c in range(3):
        xo[pl.ds(c, cells, stride=4), :] = coords[c] - 0.5
    xo[pl.ds(3, cells, stride=4), :] = root * gate_ref[...]
    lax.fori_loop(0, peers, stage_state, 0, unroll=4)
    pl.semaphore_wait(barrier, peers + 1)
    send_all(0, x_src, x_dst, x_rims)
    xt[0 : 4 * cells, :] = xo[...]
    xt[pl.ds(pl.multiple_of(4 * cells + 16 * me, 8), 16), :] = sx[me]
    for n in range(5, 14):
        loads[n].wait()
    for c in range(3):
        yo[pl.ds(c, cells, stride=4), :] = speeds[c]
    yo[pl.ds(3, cells, stride=4), :] = warmth[...]
    layer = column(tier[...])
    conduct = jnp.zeros((cells, lanes), f32)
    for n in range(LAYERS):
        conduct = jnp.where(layer == float(n), heat[0, n], conduct)
    kt[0:cells, :] = conduct
    lax.fori_loop(0, peers, stage_flow, 0, unroll=4)
    for side, start in ((0, cells - E), (1, 0)):
        syr[side, 0 : 4 * E, :] = yo[4 * start : 4 * (start + E), :]
        syr[side, 24 : 24 + E, :] = conduct[start : start + E, :]
        syr[side, 24 + E : 32, :] = conduct[0 : 8 - E, :]
    send_all(1, y_src, y_dst, y_rims)
    yt[0 : 4 * cells, :] = yo[...]
    ry[me] = sy[me]

    def features(t, scale):
        base = t * 4
        x0, x1, x2, mu = (wide(xt[pl.ds(base + c, 1), :]) for c in range(4))
        if scale is not None:
            mu = mu * scale
        rm = row8 & 3
        sq = x0 * x0 + x1 * x1 + x2 * x2
        xyz = jnp.where(rm == 0, x0, jnp.where(rm == 1, x1, x2))
        last = rm == 3
        xd[t] = jnp.where(last, 1.0, xyz)
        q1, q2, q3 = split3(jnp.where(last, -sq, xyz))
        ones = jnp.where(row8 < 3, 1.0, 0.0)
        feat[t] = jnp.concatenate(
            [jnp.where(top, q1, q2), jnp.where(top, q3, q1), jnp.where(top, q2, q1), ones], axis=0
        ).astype(bf16)
        p1, p2, p3 = split3(mu * jnp.where(last, 1.0, xyz * 2.0))
        u1, u2, u3 = split3(mu * (1.0 - sq))
        tail = jnp.where(
            row8 == 0, u1, jnp.where(row8 == 1, u2, jnp.where(row8 == 2, u3, 0.0))
        )
        return [p1, jnp.where(top, p1, p2), jnp.where(top, p2, p3), tail]

    def prepare(base, scale):
        tiles = []
        for k in range(4):
            tiles += features(base + k, scale(base + k))
        turned = jnp.concatenate(tiles, axis=0).T
        for k in range(4):
            gcol[base + k, :, 0:32] = turned[:, 32 * k : 32 * k + 32].astype(bf16)

    def unscaled(t):
        return None

    def own_prepare(g, c):
        prepare(4 * g, unscaled)
        return c

    def rim_scale(t):
        return jnp.where(t < rim0 + E, has_below, has_above)

    def weight(s, t):
        return jnp.maximum(dot(gcol[s, :, 0:32], feat[t]), 0.0)

    def density_part(slot, s, t):
        w = weight(s, t)
        wbuf[slot] = w
        return jnp.sum(w * w * w, axis=0, keepdims=True)

    lax.fori_loop(0, cells // 4, own_prepare, 0, unroll=PREP_UNROLL)

    def own_density(t, c):
        selfd[pl.ds(t, 1), :] = density_part(2 * npair + t, t, t)
        return c

    lax.fori_loop(0, cells, own_density, 0, unroll=32)

    alive = lax.broadcasted_iota(jnp.int32, (1, npair), 1) < count[0, 0]
    first = jnp.where(alive, couples_row[0:1, :], -1)
    second = jnp.where(alive, couples_row[1:2, :], -1)
    own_block = lax.broadcasted_iota(jnp.int32, (cells, npair), 0)
    zown[:, 0:npair] = jnp.where(first == own_block, 1.0, 0.0).astype(bf16)
    zown[:, npair : 2 * npair] = jnp.where(second == own_block, 1.0, 0.0).astype(bf16)
    rim_at = 8 * peers
    zrow = lax.broadcasted_iota(jnp.int32, (rim_at + 16, npair), 0)
    ghost_row = cells + (zrow >> 3) * 4 + (zrow & 3)
    rim_row = zrow - rim_at
    rim_block = jnp.where((rim_row & 7) < E, rim0 + (rim_row >> 3) * E + (rim_row & 7), -2)
    zlent[...] = jnp.where(second == jnp.where(rim_row < 0, ghost_row, rim_block), 1.0, 0.0).astype(bf16)

    def arrived(d):
        q = jnp.where(me >= d, me - d, me - d + peers)
        block = xt.at[pl.ds(pl.multiple_of(4 * cells + 16 * q, 8), 16)]
        pltpu.make_async_copy(block, block, state_sem.at[q]).wait()
        return q

    def lent_prepare(g, c):
        came = [arrived(1 + g * PEER_UNROLL + u) for u in range(PEER_UNROLL)]
        for q in came:
            prepare(cells + slots * q, unscaled)
        return c

    rounds = (peers - 1) // PEER_UNROLL
    lax.fori_loop(0, rounds, lent_prepare, 0)
    came = [me] + [arrived(d) for d in range(1 + rounds * PEER_UNROLL, peers)]
    for rim in x_rims:
        rim.wait_recv()
    for q in came:
        prepare(cells + slots * q, unscaled)
    for g in range(2 * E // 4):
        prepare(rim0 + 4 * g, rim_scale)

    def second_density(g, c):
        for u in range(DENS_UNROLL):
            n = g * DENS_UNROLL + u
            dpart[pl.ds(npair + n, 1), :] = density_part(npair + n, couples[0, n], couples[1, n])
        return c

    lax.fori_loop(0, npair // DENS_UNROLL, second_density, 0)
    acc[...] = exact_dot(zlent[...], dpart[npair : 2 * npair, :])

    d_src = lambda q: acc.at[pl.ds(pl.multiple_of(8 * q, 8), 8)]
    d_dst = lambda q: rd.at[pl.ds(pl.multiple_of(8 * q, 8), 8)]
    d_rims = rim_copies(
        2, acc.at[pl.ds(rim_at + 8, 8)], rdr.at[0], acc.at[pl.ds(rim_at, 8)], rdr.at[1]
    )
    send_all(2, d_src, d_dst, d_rims)
    rd[pl.ds(pl.multiple_of(8 * me, 8), 8), :] = acc[pl.ds(pl.multiple_of(8 * me, 8), 8), :]

    def first_density(g, c):
        for u in range(DENS_UNROLL):
            n = g * DENS_UNROLL + u
            dpart[pl.ds(n, 1), :] = density_part(n, couples[1, n], couples[0, n])
        return c

    lax.fori_loop(0, npair // DENS_UNROLL, first_density, 0)

    back = jnp.concatenate(
        [jnp.where(lent_row[...] > k, picks_row[k : k + 1, :], -1) for k in range(slots)], axis=1
    )
    own_row = lax.broadcasted_iota(jnp.int32, (cells, ghosts), 0)
    zback = jnp.where(back == own_row, 1.0, 0.0).astype(bf16)
    base = selfd[...] + exact_dot(zown[...], dpart[...])
    d_all = rd.at[pl.ds(0, 8 * (peers - 1))]
    wait_all(2, d_all, d_rims)
    got = jnp.concatenate([rd[pl.ds(k, peers, stride=8), :] for k in range(slots)], axis=0)
    selfd[...] = base + exact_dot(zback, got)
    selfd[0:E, :] = selfd[0:E, :] + rdr[0, 0:E, :] * has_below
    selfd[cells - E : cells, :] = selfd[cells - E : cells, :] + rdr[1, 0:E, :] * has_above
    gate = gate_ref[...]
    density = selfd[...]
    dens_out[...] = density * gate
    invt[0:cells, :] = jnp.where(gate > 0.0, 1.0 / jnp.where(gate > 0.0, density, 1.0), 0.0)

    def stage_inverse(q, c):
        for k in range(slots):
            si[q, k : k + 1, :] = invt[pl.ds(picks[k, q], 1), :]
        return c

    lax.fori_loop(0, peers, stage_inverse, 0, unroll=4)
    for side, start in ((0, cells - E), (1, 0)):
        sir[side, 0:E, :] = invt[start : start + E, :]
        sir[side, E:8, :] = invt[0 : 8 - E, :]
    i_src = lambda q: si.at[q]
    i_dst = lambda q: ri.at[q]
    i_rims = rim_copies(3, sir.at[0], rir.at[0], sir.at[1], rir.at[1])
    send_all(3, i_src, i_dst, i_rims)
    ri[me] = si[me]

    def coefficients(t, scale):
        base = t * 4
        mu = wide(xt[pl.ds(base + 3, 1), :])
        if scale is not None:
            mu = mu * scale
        inv = wide(invt[pl.ds(t, 1), :])
        y4 = yt[pl.ds(pl.multiple_of(base, 4), 4), :]
        y8 = jnp.concatenate([y4, jnp.ones_like(y4)], axis=0)
        place = mu * xd[t]
        press = jnp.where(top, 1.0, (6.0 * press_coef) * inv + tension_coef) * place
        flow = (mu * inv) * y8
        linear = jnp.where(top, 0.0, (-0.5 * tension_coef) * mu * place)
        square = jnp.concatenate([press, flow], axis=0)
        line = jnp.concatenate([linear, jnp.zeros_like(linear)], axis=0)
        sh, sl = split2(square)
        lh, ll = split2(line)
        gcol[t, 0:16, :] = sh
        gcol[t, 16:32, :] = sl
        gcol[t, 32:48, :] = lh
        gcol[t, 48:64, :] = ll

    def force_sums(slot, s):
        w = wbuf[slot]
        qh, ql = split2(w * w)
        wh, wl = split2(w)
        tile = jnp.concatenate(
            [jnp.concatenate([qh, ql], axis=1), jnp.concatenate([wh, wl], axis=1)], axis=0
        )
        out = dot(jnp.concatenate([gcol[s, 0:32, :], gcol[s, 32:64, :]], axis=1), tile)
        return out[0:16, 0:128] + out[0:16, 128:256] + out[16:32, 0:128] + out[16:32, 128:256]

    def force_at(out, t, heat):
        ae = out[0:8]
        flow = out[8:16]
        moved = xd[t] * jnp.where(top, wide(ae[3:4]), wide(ae[7:8])) - ae
        y4 = yt[pl.ds(t * 4, 4), :]
        carried = flow[0:4] - y4 * flow[4:5]
        gain = jnp.where(row8[0:4] == 3, jnp.broadcast_to(heat, (4, 128)), visc_coef)
        inv = invt[pl.ds(t, 1), :]
        return inv * ((6.0 * press_coef) * moved[0:4] + gain * carried) + moved[4:8]

    def own_coef(t, c):
        coefficients(t, None)
        return c

    lax.fori_loop(0, cells, own_coef, 0, unroll=4)

    def second_sums(g, c):
        for u in range(UNROLL):
            n = g * UNROLL + u
            raw[n] = force_sums(npair + n, couples[0, n])
        return c

    lax.fori_loop(0, npair // UNROLL, second_sums, 0)

    wait_all(1, y_all, y_rims)
    wait_all(3, ri.at[pl.ds(0, peers - 1)], i_rims)

    def spread(q, c):
        invt[pl.ds(cells + 4 * q, 4), :] = ri[q]
        yt[pl.ds(pl.multiple_of(4 * cells + 16 * q, 8), 16), :] = ry[q, 0:16, :]
        kt[pl.ds(cells + 4 * q, 4), :] = ry[q, 16:20, :]
        return c

    lax.fori_loop(0, peers, spread, 0, unroll=4)
    for side in range(2):
        at = rim0 + side * E
        invt[at : at + E, :] = rir[side, 0:E, :]
        yt[4 * at : 4 * (at + E), :] = ryr[side, 0 : 4 * E, :]
        kt[at : at + E, :] = ryr[side, 24 : 24 + E, :]

    def pair_force(slot, sums, s, t):
        ks = kt[pl.ds(s, 1), :]
        kd = kt[pl.ds(t, 1), :]
        part = force_at(sums, t, 2.0 * ks * kd / (ks + kd))
        for k in range(4):
            rpart[k, pl.ds(slot, 1), :] = part[k : k + 1, :]

    def second_force(g, c):
        for u in range(UNROLL):
            n = g * UNROLL + u
            pair_force(npair + n, raw[n], couples[0, n], couples[1, n])
        return c

    lax.fori_loop(0, npair // UNROLL, second_force, 0)

    held = None
    half = (lax.broadcasted_iota(jnp.int32, (8 * peers, 128), 0) & 7) < 4
    for k in range(4):
        sums = exact_dot(zlent[...], rpart[k, npair : 2 * npair, :])
        for side in range(2):
            srr[side, 8 * k : 8 * k + 8, :] = sums[rim_at + 8 * side : rim_at + 8 * side + 8]
        lent_sums = sums[0:rim_at]
        if k % 2 == 0:
            held = lent_sums
        else:
            sr[:, 4 * (k - 1) : 4 * (k - 1) + 8, :] = jnp.where(half, held, lent_sums).reshape(
                peers, 8, 128
            )

    r_src = lambda q: sr.at[q]
    r_dst = lambda q: rr.at[pl.ds(pl.multiple_of(16 * q, 8), 16)]
    r_rims = rim_copies(4, srr.at[1], rrr.at[0], srr.at[0], rrr.at[1])
    send_all(4, r_src, r_dst, r_rims)
    rr[pl.ds(pl.multiple_of(16 * me, 8), 16), :] = sr[me]

    def ghost_coef(t, c):
        coefficients(cells + t, None)
        return c

    lax.fori_loop(0, ghosts, ghost_coef, 0, unroll=4)

    def rim_coef(t, c):
        coefficients(rim0 + t, rim_scale(rim0 + t))
        return c

    lax.fori_loop(0, 2 * E, rim_coef, 0, unroll=4)

    def own_force(t, c):
        part = force_at(force_sums(2 * npair + t, t), t, kt[pl.ds(t, 1), :])
        for k in range(4):
            selfr[k, pl.ds(t, 1), :] = part[k : k + 1, :]
        return c

    lax.fori_loop(0, cells, own_force, 0, unroll=SELF_UNROLL)

    def first_force(g, c):
        for u in range(UNROLL):
            n = g * UNROLL + u
            pair_force(n, force_sums(n, couples[1, n]), couples[1, n], couples[0, n])
        return c

    lax.fori_loop(0, npair // UNROLL, first_force, 0)
    for k in range(4):
        ownr[k] = selfr[k] + exact_dot(zown[...], rpart[k])
    drain(0, x_all, x_rims)
    drain(1, y_all, y_rims)
    drain(2, d_all, d_rims)
    drain(3, ri.at[pl.ds(0, peers - 1)], i_rims)
    r_all = rr.at[pl.ds(0, 16 * (peers - 1))]
    wait_all(4, r_all, r_rims)
    for k in range(4):
        got = jnp.concatenate(
            [rr[pl.ds(4 * k + n, peers, stride=16), :] for n in range(slots)], axis=0
        )
        ownr[k] = ownr[k] + exact_dot(zback, got)
        ownr[k, 0:E, :] = ownr[k, 0:E, :] + rrr[0, 8 * k : 8 * k + E, :] * has_below
        ownr[k, cells - E : cells, :] = (
            ownr[k, cells - E : cells, :] + rrr[1, 8 * k : 8 * k + E, :] * has_above
        )
        rates_out[pl.ds(k, cells, stride=4), :] = ownr[k] * gate
    drain(4, r_all, r_rims)


def shards(
    grain_coordinates,
    grain_motion_speeds,
    grain_warmth,
    grain_weights,
    cell_grain_tally,
    cell_deposit_tier,
    tier_thermal_coefficient,
    loaned_cell_indices,
    loaned_cell_tally,
    cell_couples,
    couple_entry_tally,
):
    coords = grain_coordinates[0, 0].transpose(1, 0, 2)
    speeds = grain_motion_speeds[0, 0].transpose(1, 0, 2)
    _, cells, lanes = coords.shape
    picks = loaned_cell_indices[0, 0].T
    slots, peers = picks.shape
    slabs = lax.axis_size("slab")
    couples = cell_couples[0, 0].T
    npair = couples.shape[1]
    table = cells + slots * peers + 2 * E
    vmem = lambda *shape: pltpu.VMEM(shape, f32)
    density, rates = pl.pallas_call(
        functools.partial(step_kernel, cells, lanes, peers, slabs, npair),
        out_shape=(
            jax.ShapeDtypeStruct((cells, lanes), f32),
            jax.ShapeDtypeStruct((4 * cells, lanes), f32),
        ),
        in_specs=[pl.BlockSpec(memory_space=pl.ANY)] * 11,
        out_specs=(
            pl.BlockSpec(memory_space=pltpu.VMEM),
            pl.BlockSpec(memory_space=pltpu.VMEM),
        ),
        scratch_shapes=[
            vmem(3, cells, lanes),
            vmem(3, cells, lanes),
            vmem(cells, lanes),
            vmem(cells, lanes),
            pltpu.VMEM((1, cells), jnp.int32),
            pltpu.VMEM((1, cells), jnp.int32),
            pltpu.SMEM((1, LAYERS), f32),
            pltpu.SMEM((slots, peers), jnp.int32),
            pltpu.VMEM((slots, peers), jnp.int32),
            pltpu.SMEM((1, peers), jnp.int32),
            pltpu.VMEM((1, peers), jnp.int32),
            pltpu.SMEM((2, npair), jnp.int32),
            pltpu.VMEM((2, npair), jnp.int32),
            pltpu.SMEM((1, 1), jnp.int32),
            vmem(cells, lanes),
            vmem(4 * cells, lanes),
            vmem(4 * cells, lanes),
            vmem(4 * table, lanes),
            vmem(4 * table, lanes),
            vmem(peers, 16, lanes),
            vmem(peers, 24, lanes),
            vmem(2, 32, lanes),
            vmem(peers, 24, lanes),
            vmem(2, 32, lanes),
            pltpu.VMEM((table, 32, lanes), bf16),
            pltpu.VMEM((table, lanes, lanes), bf16),
            vmem(2 * npair + cells, lanes, lanes),
            vmem(table, 8, lanes),
            vmem(8 * peers + 16, lanes),
            vmem(2 * npair, lanes),
            vmem(4, 2 * npair, lanes),
            vmem(npair, 16, lanes),
            vmem(cells, lanes),
            vmem(4, cells, lanes),
            vmem(4, cells, lanes),
            pltpu.VMEM((cells, 2 * npair), bf16),
            pltpu.VMEM((8 * peers + 16, npair), bf16),
            vmem(8 * peers, lanes),
            vmem(2, 8, lanes),
            vmem(peers, 4, lanes),
            vmem(2, 8, lanes),
            vmem(peers, 4, lanes),
            vmem(2, 8, lanes),
            vmem(table, lanes),
            vmem(table, lanes),
            vmem(peers, 16, lanes),
            vmem(2, 32, lanes),
            vmem(16 * peers, lanes),
            vmem(2, 32, lanes),
            pltpu.SemaphoreType.DMA((14,)),
            pltpu.SemaphoreType.DMA((5, 3)),
            pltpu.SemaphoreType.DMA((5, 3)),
            pltpu.SemaphoreType.DMA((peers,)),
        ],
        compiler_params=pltpu.CompilerParams(
            collective_id=0, has_side_effects=True, vmem_limit_bytes=60 * 1024 * 1024
        ),
        name="force_step",
    )(
        coords,
        speeds,
        grain_warmth[0, 0],
        grain_weights[0, 0],
        cell_grain_tally[0],
        cell_deposit_tier[0],
        tier_thermal_coefficient[None],
        picks,
        loaned_cell_tally[0],
        couples,
        couple_entry_tally,
    )
    return density[None, None], rates.reshape(1, 1, cells, 4, lanes)


def solution(mesh):
    return jax.shard_map(
        shards,
        mesh=mesh,
        in_specs=(
            P("slab", "plane", None, None, None),
            P("slab", "plane", None, None, None),
            P("slab", "plane", None, None),
            P("slab", "plane", None, None),
            P("slab", "plane", None),
            P("slab", "plane", None),
            P(),
            P("slab", "plane", None, None),
            P("slab", "plane", None),
            P("slab", "plane", None, None),
            P("slab", "plane"),
        ),
        out_specs=(P("slab", "plane", None, None), P("slab", "plane", None, None, None)),
        check_vma=False,
    )
```

```python
import functools
import jax
import jax.numpy as jnp
from jax import lax
from jax.experimental import pallas as pl
from jax.experimental.pallas import tpu as pltpu
from jax.sharding import PartitionSpec as P

E = 6
LAYERS = 8
UNROLL = 64
SELF_UNROLL = 32
DENS_UNROLL = 64
PREP_UNROLL = 8
PEER_UNROLL = 10

press_coef = 0.2
visc_coef = 0.1
tension_coef = 2.0

f32 = jnp.float32
bf16 = jnp.bfloat16
MESH = pl.DeviceIdType.MESH


def dot(a, b):
    return lax.dot_general(a, b, (((1,), (0,)), ((), ())), preferred_element_type=f32)


def split2(x):
    hi = x.astype(bf16)
    return hi, (x - hi.astype(f32)).astype(bf16)


def split3(x):
    a = x.astype(bf16).astype(f32)
    b = (x - a).astype(bf16).astype(f32)
    return a, b, x - a - b


def exact_dot(select, values):
    a, b, c = split3(values)
    parts = jnp.concatenate([a.astype(bf16), b.astype(bf16), c.astype(bf16)], axis=1)
    out = dot(select, parts)
    n = values.shape[1]
    return out[:, 0:n] + out[:, n : 2 * n] + out[:, 2 * n : 3 * n]


def wide(row):
    return jnp.broadcast_to(row, (8, 128))


def step_kernel(
    cells,
    lanes,
    peers,
    slabs,
    npair,
    coords_in,
    speeds_in,
    warmth_in,
    weights_in,
    fill_in,
    tier_in,
    heat_in,
    picks_in,
    lent_in,
    couples_in,
    count_in,
    dens_out,
    rates_out,
    coords,
    speeds,
    warmth,
    weights,
    fill,
    tier,
    heat,
    picks,
    picks_row,
    lent,
    lent_row,
    couples,
    couples_row,
    count,
    gate_ref,
    xo,
    yo,
    xt,
    yt,
    sx,
    sy,
    syr,
    ry,
    ryr,
    feat,
    gcol,
    wbuf,
    xd,
    acc,
    dpart,
    rpart,
    raw,
    selfd,
    selfr,
    ownr,
    zown,
    zlent,
    rd,
    rdr,
    si,
    sir,
    ri,
    rir,
    invt,
    kt,
    sr,
    srr,
    rr,
    rrr,
    load_sem,
    send_sem,
    recv_sem,
    state_sem,
):
    slots = 4
    ghosts = peers * slots
    rim0 = cells + ghosts
    me = lax.axis_index("plane")
    slab = lax.axis_index("slab")
    below = lax.rem(slab + slabs - 1, slabs)
    above = lax.rem(slab + 1, slabs)
    has_below = jnp.where(slab > 0, 1.0, 0.0).astype(f32)
    has_above = jnp.where(slab < slabs - 1, 1.0, 0.0).astype(f32)
    row8 = lax.broadcasted_iota(jnp.int32, (8, 128), 0)
    top = row8 < 4

    loads = [
        pltpu.make_async_copy(src, dst, load_sem.at[n])
        for n, (src, dst) in enumerate(
            (
                (coords_in, coords),
                (weights_in, weights),
                (fill_in, fill),
                (picks_in, picks),
                (lent_in, lent),
                (speeds_in, speeds),
                (warmth_in, warmth),
                (tier_in, tier),
                (heat_in, heat),
                (picks_in, picks_row),
                (lent_in, lent_row),
                (couples_in, couples),
                (couples_in, couples_row),
                (count_in, count),
            )
        )
    ]
    for load in loads:
        load.start()

    def turn(d):
        q = me + d
        return jnp.where(q >= peers, q - peers, q)

    barrier = pltpu.get_barrier_semaphore()

    def greet(d, c):
        pl.semaphore_signal(
            barrier, inc=1, device_id=(slab, turn(d)), device_id_type=MESH
        )
        return c

    lax.fori_loop(1, peers, greet, 0, unroll=True)
    pl.semaphore_signal(barrier, inc=1, device_id=(below, me), device_id_type=MESH)
    pl.semaphore_signal(barrier, inc=1, device_id=(above, me), device_id_type=MESH)

    def peer_copy(phase, src, dst, d):
        q = turn(d)
        return pltpu.make_async_remote_copy(
            src_ref=src(q),
            dst_ref=dst(me),
            send_sem=send_sem.at[phase, 0],
            recv_sem=state_sem.at[me] if phase == 0 else recv_sem.at[phase, 0],
            device_id=(slab, q),
            device_id_type=MESH,
        )

    def rim_copies(phase, to_above, in_below, to_below, in_above):
        return (
            pltpu.make_async_remote_copy(
                src_ref=to_above,
                dst_ref=in_below,
                send_sem=send_sem.at[phase, 1],
                recv_sem=recv_sem.at[phase, 1],
                device_id=(above, me),
                device_id_type=MESH,
            ),
            pltpu.make_async_remote_copy(
                src_ref=to_below,
                dst_ref=in_above,
                send_sem=send_sem.at[phase, 2],
                recv_sem=recv_sem.at[phase, 2],
                device_id=(below, me),
                device_id_type=MESH,
            ),
        )

    def send_all(phase, src, dst, rims):
        def go(d, c):
            peer_copy(phase, src, dst, d).start()
            return c

        lax.fori_loop(1, peers, go, 0, unroll=True)
        for rim in rims:
            rim.start()

    def wait_all(phase, arrivals, rims):
        pltpu.make_async_copy(arrivals, arrivals, recv_sem.at[phase, 0]).wait()
        for rim in rims:
            rim.wait_recv()

    def drain(phase, arrivals, rims):
        pltpu.make_async_copy(arrivals, arrivals, send_sem.at[phase, 0]).wait()
        for rim in rims:
            rim.wait_send()

    def stage_state(q, c):
        here = lent[0, q]
        for k in range(slots):
            block = xo[pl.ds(picks[k, q] * 4, 4), :]
            live = jnp.minimum(jnp.maximum(here - k, 0), 1).astype(f32)
            sx[q, 4 * k : 4 * k + 4, :] = block * jnp.where(row8[0:4] < 3, 1.0, live)
        return c

    def stage_flow(q, c):
        for k in range(slots):
            sy[q, 4 * k : 4 * k + 4, :] = yo[pl.ds(picks[k, q] * 4, 4), :]
            heats = kt[pl.ds(picks[k, q], 1), :]
            sy[q, 16 + k : 17 + k, :] = heats
            sy[q, 20 + k : 21 + k, :] = heats
        return c

    x_src = lambda q: sx.at[q]
    x_dst = lambda q: xt.at[pl.ds(pl.multiple_of(4 * cells + 16 * q, 8), 16)]
    x_rims = rim_copies(
        0,
        xo.at[pl.ds(4 * (cells - E), 4 * E)],
        xt.at[pl.ds(4 * rim0, 4 * E)],
        xo.at[pl.ds(0, 4 * E)],
        xt.at[pl.ds(4 * rim0 + 4 * E, 4 * E)],
    )
    y_src = lambda q: sy.at[q]
    y_dst = lambda q: ry.at[q]
    y_rims = rim_copies(1, syr.at[0], ryr.at[0], syr.at[1], ryr.at[1])
    x_all = xt.at[pl.ds(4 * cells, 16 * (peers - 1))]
    y_all = ry.at[pl.ds(0, peers - 1)]

    def column(row):
        up = lax.broadcasted_iota(jnp.int32, (cells, cells), 0)
        along = lax.broadcasted_iota(jnp.int32, (cells, cells), 1)
        return jnp.sum(jnp.where(up == along, row.astype(f32), 0.0), axis=1, keepdims=True)

    for n in range(5):
        loads[n].wait()
    place = lax.broadcasted_iota(jnp.int32, (cells, lanes), 1).astype(f32)
    gate_ref[...] = jnp.where(place < column(fill[...]), 1.0, 0.0)
    mass = weights[...]
    root = jnp.exp(jnp.log(mass) * (1.0 / 3.0))
    root = root - (root * root * root - mass) / (3.0 * root * root)
    for c in range(3):
        xo[pl.ds(c, cells, stride=4), :] = coords[c] - 0.5
    xo[pl.ds(3, cells, stride=4), :] = root * gate_ref[...]
    lax.fori_loop(0, peers, stage_state, 0, unroll=4)
    pl.semaphore_wait(barrier, peers + 1)
    send_all(0, x_src, x_dst, x_rims)
    xt[0 : 4 * cells, :] = xo[...]
    xt[pl.ds(pl.multiple_of(4 * cells + 16 * me, 8), 16), :] = sx[me]
    def features(t, scale):
        base = t * 4
        x0, x1, x2, mu = (wide(xt[pl.ds(base + c, 1), :]) for c in range(4))
        if scale is not None:
            mu = mu * scale
        rm = row8 & 3
        sq = x0 * x0 + x1 * x1 + x2 * x2
        xyz = jnp.where(rm == 0, x0, jnp.where(rm == 1, x1, x2))
        last = rm == 3
        xd[t] = jnp.where(last, 1.0, xyz)
        q1, q2, q3 = split3(jnp.where(last, -sq, xyz))
        ones = jnp.where(row8 < 3, 1.0, 0.0)
        feat[t] = jnp.concatenate(
            [jnp.where(top, q1, q2), jnp.where(top, q3, q1), jnp.where(top, q2, q1), ones], axis=0
        ).astype(bf16)
        p1, p2, p3 = split3(mu * jnp.where(last, 1.0, xyz * 2.0))
        u1, u2, u3 = split3(mu * (1.0 - sq))
        tail = jnp.where(
            row8 == 0, u1, jnp.where(row8 == 1, u2, jnp.where(row8 == 2, u3, 0.0))
        )
        return [p1, jnp.where(top, p1, p2), jnp.where(top, p2, p3), tail]

    def prepare(base, scale):
        tiles = []
        for k in range(4):
            tiles += features(base + k, scale(base + k))
        turned = jnp.concatenate(tiles, axis=0).T
        for k in range(4):
            gcol[base + k, :, 0:32] = turned[:, 32 * k : 32 * k + 32].astype(bf16)

    def unscaled(t):
        return None

    def own_prepare(g, c):
        prepare(4 * g, unscaled)
        return c

    def rim_scale(t):
        return jnp.where(t < rim0 + E, has_below, has_above)

    def weight(s, t):
        return jnp.maximum(dot(gcol[s, :, 0:32], feat[t]), 0.0)

    def density_part(slot, s, t):
        w = weight(s, t)
        wbuf[slot] = w
        return jnp.sum(w * w * w, axis=0, keepdims=True)

    lax.fori_loop(0, cells // 4, own_prepare, 0, unroll=PREP_UNROLL)

    def own_density(t, c):
        selfd[pl.ds(t, 1), :] = density_part(2 * npair + t, t, t)
        return c

    lax.fori_loop(0, cells, own_density, 0, unroll=32)

    for n in range(5, 14):
        loads[n].wait()
    for c in range(3):
        yo[pl.ds(c, cells, stride=4), :] = speeds[c]
    yo[pl.ds(3, cells, stride=4), :] = warmth[...]
    layer = column(tier[...])
    conduct = jnp.zeros((cells, lanes), f32)
    for n in range(LAYERS):
        conduct = jnp.where(layer == float(n), heat[0, n], conduct)
    kt[0:cells, :] = conduct
    lax.fori_loop(0, peers, stage_flow, 0, unroll=4)
    for side, start in ((0, cells - E), (1, 0)):
        syr[side, 0 : 4 * E, :] = yo[4 * start : 4 * (start + E), :]
        syr[side, 24 : 24 + E, :] = conduct[start : start + E, :]
        syr[side, 24 + E : 32, :] = conduct[0 : 8 - E, :]
    send_all(1, y_src, y_dst, y_rims)
    yt[0 : 4 * cells, :] = yo[...]
    ry[me] = sy[me]

    alive = lax.broadcasted_iota(jnp.int32, (1, npair), 1) < count[0, 0]
    first = jnp.where(alive, couples_row[0:1, :], -1)
    second = jnp.where(alive, couples_row[1:2, :], -1)
    own_block = lax.broadcasted_iota(jnp.int32, (cells, npair), 0)
    zown[:, 0:npair] = jnp.where(first == own_block, 1.0, 0.0).astype(bf16)
    zown[:, npair : 2 * npair] = jnp.where(second == own_block, 1.0, 0.0).astype(bf16)
    rim_at = 8 * peers
    zrow = lax.broadcasted_iota(jnp.int32, (rim_at + 16, npair), 0)
    ghost_row = cells + (zrow >> 3) * 4 + (zrow & 3)
    rim_row = zrow - rim_at
    rim_block = jnp.where((rim_row & 7) < E, rim0 + (rim_row >> 3) * E + (rim_row & 7), -2)
    zlent[...] = jnp.where(second == jnp.where(rim_row < 0, ghost_row, rim_block), 1.0, 0.0).astype(bf16)

    def arrived(d):
        q = jnp.where(me >= d, me - d, me - d + peers)
        block = xt.at[pl.ds(pl.multiple_of(4 * cells + 16 * q, 8), 16)]
        pltpu.make_async_copy(block, block, state_sem.at[q]).wait()
        return q

    def lent_prepare(g, c):
        came = [arrived(1 + g * PEER_UNROLL + u) for u in range(PEER_UNROLL)]
        for q in came:
            prepare(cells + slots * q, unscaled)
        return c

    rounds = (peers - 1) // PEER_UNROLL
    lax.fori_loop(0, rounds, lent_prepare, 0)
    came = [me] + [arrived(d) for d in range(1 + rounds * PEER_UNROLL, peers)]
    for rim in x_rims:
        rim.wait_recv()
    for q in came:
        prepare(cells + slots * q, unscaled)
    for g in range(2 * E // 4):
        prepare(rim0 + 4 * g, rim_scale)

    def second_density(g, c):
        for u in range(DENS_UNROLL):
            n = g * DENS_UNROLL + u
            dpart[pl.ds(npair + n, 1), :] = density_part(npair + n, couples[0, n], couples[1, n])
        return c

    lax.fori_loop(0, npair // DENS_UNROLL, second_density, 0)
    acc[...] = exact_dot(zlent[...], dpart[npair : 2 * npair, :])

    d_src = lambda q: acc.at[pl.ds(pl.multiple_of(8 * q, 8), 8)]
    d_dst = lambda q: rd.at[pl.ds(pl.multiple_of(8 * q, 8), 8)]
    d_rims = rim_copies(
        2, acc.at[pl.ds(rim_at + 8, 8)], rdr.at[0], acc.at[pl.ds(rim_at, 8)], rdr.at[1]
    )
    send_all(2, d_src, d_dst, d_rims)
    rd[pl.ds(pl.multiple_of(8 * me, 8), 8), :] = acc[pl.ds(pl.multiple_of(8 * me, 8), 8), :]

    def first_density(g, c):
        for u in range(DENS_UNROLL):
            n = g * DENS_UNROLL + u
            dpart[pl.ds(n, 1), :] = density_part(n, couples[1, n], couples[0, n])
        return c

    lax.fori_loop(0, npair // DENS_UNROLL, first_density, 0)

    back = jnp.concatenate(
        [jnp.where(lent_row[...] > k, picks_row[k : k + 1, :], -1) for k in range(slots)], axis=1
    )
    own_row = lax.broadcasted_iota(jnp.int32, (cells, ghosts), 0)
    zback = jnp.where(back == own_row, 1.0, 0.0).astype(bf16)
    base = selfd[...] + exact_dot(zown[...], dpart[...])
    d_all = rd.at[pl.ds(0, 8 * (peers - 1))]
    wait_all(2, d_all, d_rims)
    got = jnp.concatenate([rd[pl.ds(k, peers, stride=8), :] for k in range(slots)], axis=0)
    selfd[...] = base + exact_dot(zback, got)
    selfd[0:E, :] = selfd[0:E, :] + rdr[0, 0:E, :] * has_below
    selfd[cells - E : cells, :] = selfd[cells - E : cells, :] + rdr[1, 0:E, :] * has_above
    gate = gate_ref[...]
    density = selfd[...]
    dens_out[...] = density * gate
    invt[0:cells, :] = jnp.where(gate > 0.0, 1.0 / jnp.where(gate > 0.0, density, 1.0), 0.0)

    def stage_inverse(q, c):
        for k in range(slots):
            si[q, k : k + 1, :] = invt[pl.ds(picks[k, q], 1), :]
        return c

    lax.fori_loop(0, peers, stage_inverse, 0, unroll=4)
    for side, start in ((0, cells - E), (1, 0)):
        sir[side, 0:E, :] = invt[start : start + E, :]
        sir[side, E:8, :] = invt[0 : 8 - E, :]
    i_src = lambda q: si.at[q]
    i_dst = lambda q: ri.at[q]
    i_rims = rim_copies(3, sir.at[0], rir.at[0], sir.at[1], rir.at[1])
    send_all(3, i_src, i_dst, i_rims)
    ri[me] = si[me]

    def coefficients(t, scale):
        base = t * 4
        mu = wide(xt[pl.ds(base + 3, 1), :])
        if scale is not None:
            mu = mu * scale
        inv = wide(invt[pl.ds(t, 1), :])
        y4 = yt[pl.ds(pl.multiple_of(base, 4), 4), :]
        y8 = jnp.concatenate([y4, jnp.ones_like(y4)], axis=0)
        place = mu * xd[t]
        press = jnp.where(top, 1.0, (6.0 * press_coef) * inv + tension_coef) * place
        flow = (mu * inv) * y8
        linear = jnp.where(top, 0.0, (-0.5 * tension_coef) * mu * place)
        square = jnp.concatenate([press, flow], axis=0)
        line = jnp.concatenate([linear, jnp.zeros_like(linear)], axis=0)
        sh, sl = split2(square)
        lh, ll = split2(line)
        gcol[t, 0:16, :] = sh
        gcol[t, 16:32, :] = sl
        gcol[t, 32:48, :] = lh
        gcol[t, 48:64, :] = ll

    def force_sums(slot, s):
        w = wbuf[slot]
        qh, ql = split2(w * w)
        wh, wl = split2(w)
        tile = jnp.concatenate(
            [jnp.concatenate([qh, ql], axis=1), jnp.concatenate([wh, wl], axis=1)], axis=0
        )
        out = dot(jnp.concatenate([gcol[s, 0:32, :], gcol[s, 32:64, :]], axis=1), tile)
        return out[0:16, 0:128] + out[0:16, 128:256] + out[16:32, 0:128] + out[16:32, 128:256]

    def force_at(out, t, heat):
        ae = out[0:8]
        flow = out[8:16]
        moved = xd[t] * jnp.where(top, wide(ae[3:4]), wide(ae[7:8])) - ae
        y4 = yt[pl.ds(t * 4, 4), :]
        carried = flow[0:4] - y4 * flow[4:5]
        gain = jnp.where(row8[0:4] == 3, jnp.broadcast_to(heat, (4, 128)), visc_coef)
        inv = invt[pl.ds(t, 1), :]
        return inv * ((6.0 * press_coef) * moved[0:4] + gain * carried) + moved[4:8]

    def own_coef(t, c):
        coefficients(t, None)
        return c

    lax.fori_loop(0, cells, own_coef, 0, unroll=4)

    def second_sums(g, c):
        for u in range(UNROLL):
            n = g * UNROLL + u
            raw[n] = force_sums(npair + n, couples[0, n])
        return c

    lax.fori_loop(0, npair // UNROLL, second_sums, 0)

    wait_all(1, y_all, y_rims)
    wait_all(3, ri.at[pl.ds(0, peers - 1)], i_rims)

    def spread(q, c):
        invt[pl.ds(cells + 4 * q, 4), :] = ri[q]
        yt[pl.ds(pl.multiple_of(4 * cells + 16 * q, 8), 16), :] = ry[q, 0:16, :]
        kt[pl.ds(cells + 4 * q, 4), :] = ry[q, 16:20, :]
        return c

    lax.fori_loop(0, peers, spread, 0, unroll=4)
    for side in range(2):
        at = rim0 + side * E
        invt[at : at + E, :] = rir[side, 0:E, :]
        yt[4 * at : 4 * (at + E), :] = ryr[side, 0 : 4 * E, :]
        kt[at : at + E, :] = ryr[side, 24 : 24 + E, :]

    def pair_force(slot, sums, s, t):
        ks = kt[pl.ds(s, 1), :]
        kd = kt[pl.ds(t, 1), :]
        part = force_at(sums, t, 2.0 * ks * kd / (ks + kd))
        for k in range(4):
            rpart[k, pl.ds(slot, 1), :] = part[k : k + 1, :]

    def second_force(g, c):
        for u in range(UNROLL):
            n = g * UNROLL + u
            pair_force(npair + n, raw[n], couples[0, n], couples[1, n])
        return c

    lax.fori_loop(0, npair // UNROLL, second_force, 0)

    held = None
    half = (lax.broadcasted_iota(jnp.int32, (8 * peers, 128), 0) & 7) < 4
    for k in range(4):
        sums = exact_dot(zlent[...], rpart[k, npair : 2 * npair, :])
        for side in range(2):
            srr[side, 8 * k : 8 * k + 8, :] = sums[rim_at + 8 * side : rim_at + 8 * side + 8]
        lent_sums = sums[0:rim_at]
        if k % 2 == 0:
            held = lent_sums
        else:
            sr[:, 4 * (k - 1) : 4 * (k - 1) + 8, :] = jnp.where(half, held, lent_sums).reshape(
                peers, 8, 128
            )

    r_src = lambda q: sr.at[q]
    r_dst = lambda q: rr.at[pl.ds(pl.multiple_of(16 * q, 8), 16)]
    r_rims = rim_copies(4, srr.at[1], rrr.at[0], srr.at[0], rrr.at[1])
    send_all(4, r_src, r_dst, r_rims)
    rr[pl.ds(pl.multiple_of(16 * me, 8), 16), :] = sr[me]

    def ghost_coef(t, c):
        coefficients(cells + t, None)
        return c

    lax.fori_loop(0, ghosts, ghost_coef, 0, unroll=4)

    def rim_coef(t, c):
        coefficients(rim0 + t, rim_scale(rim0 + t))
        return c

    lax.fori_loop(0, 2 * E, rim_coef, 0, unroll=4)

    def own_force(t, c):
        part = force_at(force_sums(2 * npair + t, t), t, kt[pl.ds(t, 1), :])
        for k in range(4):
            selfr[k, pl.ds(t, 1), :] = part[k : k + 1, :]
        return c

    lax.fori_loop(0, cells, own_force, 0, unroll=SELF_UNROLL)

    def first_force(g, c):
        for u in range(UNROLL):
            n = g * UNROLL + u
            pair_force(n, force_sums(n, couples[1, n]), couples[1, n], couples[0, n])
        return c

    lax.fori_loop(0, npair // UNROLL, first_force, 0)
    for k in range(4):
        ownr[k] = selfr[k] + exact_dot(zown[...], rpart[k])
    drain(0, x_all, x_rims)
    drain(1, y_all, y_rims)
    drain(2, d_all, d_rims)
    drain(3, ri.at[pl.ds(0, peers - 1)], i_rims)
    r_all = rr.at[pl.ds(0, 16 * (peers - 1))]
    wait_all(4, r_all, r_rims)
    for k in range(4):
        got = jnp.concatenate(
            [rr[pl.ds(4 * k + n, peers, stride=16), :] for n in range(slots)], axis=0
        )
        ownr[k] = ownr[k] + exact_dot(zback, got)
        ownr[k, 0:E, :] = ownr[k, 0:E, :] + rrr[0, 8 * k : 8 * k + E, :] * has_below
        ownr[k, cells - E : cells, :] = (
            ownr[k, cells - E : cells, :] + rrr[1, 8 * k : 8 * k + E, :] * has_above
        )
        rates_out[pl.ds(k, cells, stride=4), :] = ownr[k] * gate
    drain(4, r_all, r_rims)


def shards(
    grain_coordinates,
    grain_motion_speeds,
    grain_warmth,
    grain_weights,
    cell_grain_tally,
    cell_deposit_tier,
    tier_thermal_coefficient,
    loaned_cell_indices,
    loaned_cell_tally,
    cell_couples,
    couple_entry_tally,
):
    coords = grain_coordinates[0, 0].transpose(1, 0, 2)
    speeds = grain_motion_speeds[0, 0].transpose(1, 0, 2)
    _, cells, lanes = coords.shape
    picks = loaned_cell_indices[0, 0].T
    slots, peers = picks.shape
    slabs = lax.axis_size("slab")
    couples = cell_couples[0, 0].T
    npair = couples.shape[1]
    table = cells + slots * peers + 2 * E
    vmem = lambda *shape: pltpu.VMEM(shape, f32)
    density, rates = pl.pallas_call(
        functools.partial(step_kernel, cells, lanes, peers, slabs, npair),
        out_shape=(
            jax.ShapeDtypeStruct((cells, lanes), f32),
            jax.ShapeDtypeStruct((4 * cells, lanes), f32),
        ),
        in_specs=[pl.BlockSpec(memory_space=pl.ANY)] * 11,
        out_specs=(
            pl.BlockSpec(memory_space=pltpu.VMEM),
            pl.BlockSpec(memory_space=pltpu.VMEM),
        ),
        scratch_shapes=[
            vmem(3, cells, lanes),
            vmem(3, cells, lanes),
            vmem(cells, lanes),
            vmem(cells, lanes),
            pltpu.VMEM((1, cells), jnp.int32),
            pltpu.VMEM((1, cells), jnp.int32),
            pltpu.SMEM((1, LAYERS), f32),
            pltpu.SMEM((slots, peers), jnp.int32),
            pltpu.VMEM((slots, peers), jnp.int32),
            pltpu.SMEM((1, peers), jnp.int32),
            pltpu.VMEM((1, peers), jnp.int32),
            pltpu.SMEM((2, npair), jnp.int32),
            pltpu.VMEM((2, npair), jnp.int32),
            pltpu.SMEM((1, 1), jnp.int32),
            vmem(cells, lanes),
            vmem(4 * cells, lanes),
            vmem(4 * cells, lanes),
            vmem(4 * table, lanes),
            vmem(4 * table, lanes),
            vmem(peers, 16, lanes),
            vmem(peers, 24, lanes),
            vmem(2, 32, lanes),
            vmem(peers, 24, lanes),
            vmem(2, 32, lanes),
            pltpu.VMEM((table, 32, lanes), bf16),
            pltpu.VMEM((table, lanes, lanes), bf16),
            vmem(2 * npair + cells, lanes, lanes),
            vmem(table, 8, lanes),
            vmem(8 * peers + 16, lanes),
            vmem(2 * npair, lanes),
            vmem(4, 2 * npair, lanes),
            vmem(npair, 16, lanes),
            vmem(cells, lanes),
            vmem(4, cells, lanes),
            vmem(4, cells, lanes),
            pltpu.VMEM((cells, 2 * npair), bf16),
            pltpu.VMEM((8 * peers + 16, npair), bf16),
            vmem(8 * peers, lanes),
            vmem(2, 8, lanes),
            vmem(peers, 4, lanes),
            vmem(2, 8, lanes),
            vmem(peers, 4, lanes),
            vmem(2, 8, lanes),
            vmem(table, lanes),
            vmem(table, lanes),
            vmem(peers, 16, lanes),
            vmem(2, 32, lanes),
            vmem(16 * peers, lanes),
            vmem(2, 32, lanes),
            pltpu.SemaphoreType.DMA((14,)),
            pltpu.SemaphoreType.DMA((5, 3)),
            pltpu.SemaphoreType.DMA((5, 3)),
            pltpu.SemaphoreType.DMA((peers,)),
        ],
        compiler_params=pltpu.CompilerParams(
            collective_id=0, has_side_effects=True, vmem_limit_bytes=60 * 1024 * 1024
        ),
        name="force_step",
    )(
        coords,
        speeds,
        grain_warmth[0, 0],
        grain_weights[0, 0],
        cell_grain_tally[0],
        cell_deposit_tier[0],
        tier_thermal_coefficient[None],
        picks,
        loaned_cell_tally[0],
        couples,
        couple_entry_tally,
    )
    return density[None, None], rates.reshape(1, 1, cells, 4, lanes)


def solution(mesh):
    return jax.shard_map(
        shards,
        mesh=mesh,
        in_specs=(
            P("slab", "plane", None, None, None),
            P("slab", "plane", None, None, None),
            P("slab", "plane", None, None),
            P("slab", "plane", None, None),
            P("slab", "plane", None),
            P("slab", "plane", None),
            P(),
            P("slab", "plane", None, None),
            P("slab", "plane", None),
            P("slab", "plane", None, None),
            P("slab", "plane"),
        ),
        out_specs=(P("slab", "plane", None, None), P("slab", "plane", None, None, None)),
        check_vma=False,
    )
```

```python
import functools
import jax
import jax.numpy as jnp
from jax import lax
from jax.experimental import pallas as pl
from jax.experimental.pallas import tpu as pltpu
from jax.sharding import PartitionSpec as P

E = 6
LAYERS = 8
UNROLL = 64
SELF_UNROLL = 32
DENS_UNROLL = 64
PREP_UNROLL = 8
PEER_UNROLL = 10

press_coef = 0.2
visc_coef = 0.1
tension_coef = 2.0

f32 = jnp.float32
bf16 = jnp.bfloat16
MESH = pl.DeviceIdType.MESH


def dot(a, b):
    return lax.dot_general(a, b, (((1,), (0,)), ((), ())), preferred_element_type=f32)


def split2(x):
    hi = x.astype(bf16)
    return hi, (x - hi.astype(f32)).astype(bf16)


def split3(x):
    a = x.astype(bf16).astype(f32)
    b = (x - a).astype(bf16).astype(f32)
    return a, b, x - a - b


def exact_dot(select, values):
    a, b, c = split3(values)
    parts = jnp.concatenate([a.astype(bf16), b.astype(bf16), c.astype(bf16)], axis=1)
    out = dot(select, parts)
    n = values.shape[1]
    return out[:, 0:n] + out[:, n : 2 * n] + out[:, 2 * n : 3 * n]


def sum_dot(select, values):
    out = dot(select, jnp.concatenate(split2(values), axis=1))
    n = values.shape[1]
    return out[:, 0:n] + out[:, n : 2 * n]


def wide(row):
    return jnp.broadcast_to(row, (8, 128))


def step_kernel(
    cells,
    lanes,
    peers,
    slabs,
    npair,
    coords_in,
    speeds_in,
    warmth_in,
    weights_in,
    fill_in,
    tier_in,
    heat_in,
    picks_in,
    lent_in,
    couples_in,
    count_in,
    dens_out,
    rates_out,
    coords,
    speeds,
    warmth,
    weights,
    fill,
    tier,
    heat,
    picks,
    picks_row,
    lent,
    lent_row,
    couples,
    couples_row,
    count,
    gate_ref,
    xo,
    yo,
    xt,
    yt,
    sx,
    sy,
    syr,
    ry,
    ryr,
    feat,
    gcol,
    wbuf,
    xd,
    acc,
    dpart,
    rpart,
    raw,
    selfd,
    selfr,
    ownr,
    zown,
    zlent,
    rd,
    rdr,
    si,
    sir,
    ri,
    rir,
    invt,
    kt,
    sr,
    srr,
    rr,
    rrr,
    load_sem,
    send_sem,
    recv_sem,
    state_sem,
):
    slots = 4
    ghosts = peers * slots
    rim0 = cells + ghosts
    me = lax.axis_index("plane")
    slab = lax.axis_index("slab")
    below = lax.rem(slab + slabs - 1, slabs)
    above = lax.rem(slab + 1, slabs)
    has_below = jnp.where(slab > 0, 1.0, 0.0).astype(f32)
    has_above = jnp.where(slab < slabs - 1, 1.0, 0.0).astype(f32)
    row8 = lax.broadcasted_iota(jnp.int32, (8, 128), 0)
    top = row8 < 4

    loads = [
        pltpu.make_async_copy(src, dst, load_sem.at[n])
        for n, (src, dst) in enumerate(
            (
                (coords_in, coords),
                (weights_in, weights),
                (fill_in, fill),
                (picks_in, picks),
                (lent_in, lent),
                (speeds_in, speeds),
                (warmth_in, warmth),
                (tier_in, tier),
                (heat_in, heat),
                (picks_in, picks_row),
                (lent_in, lent_row),
                (couples_in, couples),
                (couples_in, couples_row),
                (count_in, count),
            )
        )
    ]
    for load in loads:
        load.start()

    def turn(d):
        q = me + d
        return jnp.where(q >= peers, q - peers, q)

    barrier = pltpu.get_barrier_semaphore()

    def greet(d, c):
        pl.semaphore_signal(
            barrier, inc=1, device_id=(slab, turn(d)), device_id_type=MESH
        )
        return c

    lax.fori_loop(1, peers, greet, 0, unroll=True)
    pl.semaphore_signal(barrier, inc=1, device_id=(below, me), device_id_type=MESH)
    pl.semaphore_signal(barrier, inc=1, device_id=(above, me), device_id_type=MESH)

    def peer_copy(phase, src, dst, d):
        q = turn(d)
        return pltpu.make_async_remote_copy(
            src_ref=src(q),
            dst_ref=dst(me),
            send_sem=send_sem.at[phase, 0],
            recv_sem=state_sem.at[me] if phase == 0 else recv_sem.at[phase, 0],
            device_id=(slab, q),
            device_id_type=MESH,
        )

    def rim_copies(phase, to_above, in_below, to_below, in_above):
        return (
            pltpu.make_async_remote_copy(
                src_ref=to_above,
                dst_ref=in_below,
                send_sem=send_sem.at[phase, 1],
                recv_sem=recv_sem.at[phase, 1],
                device_id=(above, me),
                device_id_type=MESH,
            ),
            pltpu.make_async_remote_copy(
                src_ref=to_below,
                dst_ref=in_above,
                send_sem=send_sem.at[phase, 2],
                recv_sem=recv_sem.at[phase, 2],
                device_id=(below, me),
                device_id_type=MESH,
            ),
        )

    def send_all(phase, src, dst, rims):
        def go(d, c):
            peer_copy(phase, src, dst, d).start()
            return c

        lax.fori_loop(1, peers, go, 0, unroll=True)
        for rim in rims:
            rim.start()

    def wait_all(phase, arrivals, rims):
        pltpu.make_async_copy(arrivals, arrivals, recv_sem.at[phase, 0]).wait()
        for rim in rims:
            rim.wait_recv()

    def drain(phase, arrivals, rims):
        pltpu.make_async_copy(arrivals, arrivals, send_sem.at[phase, 0]).wait()
        for rim in rims:
            rim.wait_send()

    def stage_state(q, c):
        here = lent[0, q]
        for k in range(slots):
            block = xo[pl.ds(picks[k, q] * 4, 4), :]
            live = jnp.minimum(jnp.maximum(here - k, 0), 1).astype(f32)
            sx[q, 4 * k : 4 * k + 4, :] = block * jnp.where(row8[0:4] < 3, 1.0, live)
        return c

    def stage_flow(q, c):
        for k in range(slots):
            sy[q, 4 * k : 4 * k + 4, :] = yo[pl.ds(picks[k, q] * 4, 4), :]
            heats = kt[pl.ds(picks[k, q], 1), :]
            sy[q, 16 + k : 17 + k, :] = heats
            sy[q, 20 + k : 21 + k, :] = heats
        return c

    x_src = lambda q: sx.at[q]
    x_dst = lambda q: xt.at[pl.ds(pl.multiple_of(4 * cells + 16 * q, 8), 16)]
    x_rims = rim_copies(
        0,
        xo.at[pl.ds(4 * (cells - E), 4 * E)],
        xt.at[pl.ds(4 * rim0, 4 * E)],
        xo.at[pl.ds(0, 4 * E)],
        xt.at[pl.ds(4 * rim0 + 4 * E, 4 * E)],
    )
    y_src = lambda q: sy.at[q]
    y_dst = lambda q: ry.at[q]
    y_rims = rim_copies(1, syr.at[0], ryr.at[0], syr.at[1], ryr.at[1])
    x_all = xt.at[pl.ds(4 * cells, 16 * (peers - 1))]
    y_all = ry.at[pl.ds(0, peers - 1)]

    def column(row):
        up = lax.broadcasted_iota(jnp.int32, (cells, cells), 0)
        along = lax.broadcasted_iota(jnp.int32, (cells, cells), 1)
        return jnp.sum(jnp.where(up == along, row.astype(f32), 0.0), axis=1, keepdims=True)

    for n in range(5):
        loads[n].wait()
    place = lax.broadcasted_iota(jnp.int32, (cells, lanes), 1).astype(f32)
    gate_ref[...] = jnp.where(place < column(fill[...]), 1.0, 0.0)
    mass = weights[...]
    root = jnp.exp(jnp.log(mass) * (1.0 / 3.0))
    root = root - (root * root * root - mass) / (3.0 * root * root)
    for c in range(3):
        xo[pl.ds(c, cells, stride=4), :] = coords[c] - 0.5
    xo[pl.ds(3, cells, stride=4), :] = root * gate_ref[...]
    lax.fori_loop(0, peers, stage_state, 0, unroll=4)
    pl.semaphore_wait(barrier, peers + 1)
    send_all(0, x_src, x_dst, x_rims)
    xt[0 : 4 * cells, :] = xo[...]
    xt[pl.ds(pl.multiple_of(4 * cells + 16 * me, 8), 16), :] = sx[me]
    def features(t, scale):
        base = t * 4
        x0, x1, x2, mu = (wide(xt[pl.ds(base + c, 1), :]) for c in range(4))
        if scale is not None:
            mu = mu * scale
        rm = row8 & 3
        sq = x0 * x0 + x1 * x1 + x2 * x2
        xyz = jnp.where(rm == 0, x0, jnp.where(rm == 1, x1, x2))
        last = rm == 3
        xd[t] = jnp.where(last, 1.0, xyz)
        q1, q2, q3 = split3(jnp.where(last, -sq, xyz))
        ones = jnp.where(row8 < 3, 1.0, 0.0)
        feat[t] = jnp.concatenate(
            [jnp.where(top, q1, q2), jnp.where(top, q3, q1), jnp.where(top, q2, q1), ones], axis=0
        ).astype(bf16)
        p1, p2, p3 = split3(mu * jnp.where(last, 1.0, xyz * 2.0))
        u1, u2, u3 = split3(mu * (1.0 - sq))
        tail = jnp.where(
            row8 == 0, u1, jnp.where(row8 == 1, u2, jnp.where(row8 == 2, u3, 0.0))
        )
        return [p1, jnp.where(top, p1, p2), jnp.where(top, p2, p3), tail]

    def prepare(base, scale):
        tiles = []
        for k in range(4):
            tiles += features(base + k, scale(base + k))
        turned = jnp.concatenate(tiles, axis=0).T
        for k in range(4):
            gcol[base + k, :, 0:32] = turned[:, 32 * k : 32 * k + 32].astype(bf16)

    def unscaled(t):
        return None

    def own_prepare(g, c):
        prepare(4 * g, unscaled)
        return c

    def rim_scale(t):
        return jnp.where(t < rim0 + E, has_below, has_above)

    def weight(s, t):
        return jnp.maximum(dot(gcol[s, :, 0:32], feat[t]), 0.0)

    def density_part(slot, s, t):
        w = weight(s, t)
        wbuf[slot] = w
        return jnp.sum(w * w * w, axis=0, keepdims=True)

    lax.fori_loop(0, cells // 4, own_prepare, 0, unroll=PREP_UNROLL)

    def own_density(t, c):
        selfd[pl.ds(t, 1), :] = density_part(2 * npair + t, t, t)
        return c

    lax.fori_loop(0, cells, own_density, 0, unroll=32)

    for n in range(5, 14):
        loads[n].wait()
    for c in range(3):
        yo[pl.ds(c, cells, stride=4), :] = speeds[c]
    yo[pl.ds(3, cells, stride=4), :] = warmth[...]
    layer = column(tier[...])
    conduct = jnp.zeros((cells, lanes), f32)
    for n in range(LAYERS):
        conduct = jnp.where(layer == float(n), heat[0, n], conduct)
    kt[0:cells, :] = conduct
    lax.fori_loop(0, peers, stage_flow, 0, unroll=4)
    for side, start in ((0, cells - E), (1, 0)):
        syr[side, 0 : 4 * E, :] = yo[4 * start : 4 * (start + E), :]
        syr[side, 24 : 24 + E, :] = conduct[start : start + E, :]
        syr[side, 24 + E : 32, :] = conduct[0 : 8 - E, :]
    send_all(1, y_src, y_dst, y_rims)
    yt[0 : 4 * cells, :] = yo[...]
    ry[me] = sy[me]

    alive = lax.broadcasted_iota(jnp.int32, (1, npair), 1) < count[0, 0]
    first = jnp.where(alive, couples_row[0:1, :], -1)
    second = jnp.where(alive, couples_row[1:2, :], -1)
    own_block = lax.broadcasted_iota(jnp.int32, (cells, npair), 0)
    zown[:, 0:npair] = jnp.where(first == own_block, 1.0, 0.0).astype(bf16)
    zown[:, npair : 2 * npair] = jnp.where(second == own_block, 1.0, 0.0).astype(bf16)
    rim_at = 8 * peers
    zrow = lax.broadcasted_iota(jnp.int32, (rim_at + 16, npair), 0)
    ghost_row = cells + (zrow >> 3) * 4 + (zrow & 3)
    rim_row = zrow - rim_at
    rim_block = jnp.where((rim_row & 7) < E, rim0 + (rim_row >> 3) * E + (rim_row & 7), -2)
    zlent[...] = jnp.where(second == jnp.where(rim_row < 0, ghost_row, rim_block), 1.0, 0.0).astype(bf16)

    def arrived(d):
        q = jnp.where(me >= d, me - d, me - d + peers)
        block = xt.at[pl.ds(pl.multiple_of(4 * cells + 16 * q, 8), 16)]
        pltpu.make_async_copy(block, block, state_sem.at[q]).wait()
        return q

    def lent_prepare(g, c):
        came = [arrived(1 + g * PEER_UNROLL + u) for u in range(PEER_UNROLL)]
        for q in came:
            prepare(cells + slots * q, unscaled)
        return c

    rounds = (peers - 1) // PEER_UNROLL
    lax.fori_loop(0, rounds, lent_prepare, 0)
    came = [me] + [arrived(d) for d in range(1 + rounds * PEER_UNROLL, peers)]
    for rim in x_rims:
        rim.wait_recv()
    for q in came:
        prepare(cells + slots * q, unscaled)
    for g in range(2 * E // 4):
        prepare(rim0 + 4 * g, rim_scale)

    def second_density(g, c):
        for u in range(DENS_UNROLL):
            n = g * DENS_UNROLL + u
            dpart[pl.ds(npair + n, 1), :] = density_part(npair + n, couples[0, n], couples[1, n])
        return c

    lax.fori_loop(0, npair // DENS_UNROLL, second_density, 0)
    acc[...] = exact_dot(zlent[...], dpart[npair : 2 * npair, :])

    d_src = lambda q: acc.at[pl.ds(pl.multiple_of(8 * q, 8), 8)]
    d_dst = lambda q: rd.at[pl.ds(pl.multiple_of(8 * q, 8), 8)]
    d_rims = rim_copies(
        2, acc.at[pl.ds(rim_at + 8, 8)], rdr.at[0], acc.at[pl.ds(rim_at, 8)], rdr.at[1]
    )
    send_all(2, d_src, d_dst, d_rims)
    rd[pl.ds(pl.multiple_of(8 * me, 8), 8), :] = acc[pl.ds(pl.multiple_of(8 * me, 8), 8), :]

    def first_density(g, c):
        for u in range(DENS_UNROLL):
            n = g * DENS_UNROLL + u
            dpart[pl.ds(n, 1), :] = density_part(n, couples[1, n], couples[0, n])
        return c

    lax.fori_loop(0, npair // DENS_UNROLL, first_density, 0)

    back = jnp.concatenate(
        [jnp.where(lent_row[...] > k, picks_row[k : k + 1, :], -1) for k in range(slots)], axis=1
    )
    own_row = lax.broadcasted_iota(jnp.int32, (cells, ghosts), 0)
    zback = jnp.where(back == own_row, 1.0, 0.0).astype(bf16)
    base = selfd[...] + exact_dot(zown[...], dpart[...])
    d_all = rd.at[pl.ds(0, 8 * (peers - 1))]
    wait_all(2, d_all, d_rims)
    got = jnp.concatenate([rd[pl.ds(k, peers, stride=8), :] for k in range(slots)], axis=0)
    selfd[...] = base + exact_dot(zback, got)
    selfd[0:E, :] = selfd[0:E, :] + rdr[0, 0:E, :] * has_below
    selfd[cells - E : cells, :] = selfd[cells - E : cells, :] + rdr[1, 0:E, :] * has_above
    gate = gate_ref[...]
    density = selfd[...]
    dens_out[...] = density * gate
    invt[0:cells, :] = jnp.where(gate > 0.0, 1.0 / jnp.where(gate > 0.0, density, 1.0), 0.0)

    def stage_inverse(q, c):
        for k in range(slots):
            si[q, k : k + 1, :] = invt[pl.ds(picks[k, q], 1), :]
        return c

    lax.fori_loop(0, peers, stage_inverse, 0, unroll=4)
    for side, start in ((0, cells - E), (1, 0)):
        sir[side, 0:E, :] = invt[start : start + E, :]
        sir[side, E:8, :] = invt[0 : 8 - E, :]
    i_src = lambda q: si.at[q]
    i_dst = lambda q: ri.at[q]
    i_rims = rim_copies(3, sir.at[0], rir.at[0], sir.at[1], rir.at[1])
    send_all(3, i_src, i_dst, i_rims)
    ri[me] = si[me]

    def coefficients(t, scale):
        base = t * 4
        mu = wide(xt[pl.ds(base + 3, 1), :])
        if scale is not None:
            mu = mu * scale
        inv = wide(invt[pl.ds(t, 1), :])
        y4 = yt[pl.ds(pl.multiple_of(base, 4), 4), :]
        y8 = jnp.concatenate([y4, jnp.ones_like(y4)], axis=0)
        place = mu * xd[t]
        press = jnp.where(top, 1.0, (6.0 * press_coef) * inv + tension_coef) * place
        flow = (mu * inv) * y8
        linear = jnp.where(top, 0.0, (-0.5 * tension_coef) * mu * place)
        square = jnp.concatenate([press, flow], axis=0)
        line = jnp.concatenate([linear, jnp.zeros_like(linear)], axis=0)
        sh, sl = split2(square)
        lh, ll = split2(line)
        gcol[t, 0:16, :] = sh
        gcol[t, 16:32, :] = sl
        gcol[t, 32:48, :] = lh
        gcol[t, 48:64, :] = ll

    def force_sums(slot, s):
        w = wbuf[slot]
        qh, ql = split2(w * w)
        wh, wl = split2(w)
        tile = jnp.concatenate(
            [jnp.concatenate([qh, ql], axis=1), jnp.concatenate([wh, wl], axis=1)], axis=0
        )
        out = dot(jnp.concatenate([gcol[s, 0:32, :], gcol[s, 32:64, :]], axis=1), tile)
        return out[0:16, 0:128] + out[0:16, 128:256] + out[16:32, 0:128] + out[16:32, 128:256]

    def force_at(out, t, heat):
        ae = out[0:8]
        flow = out[8:16]
        moved = xd[t] * jnp.where(top, wide(ae[3:4]), wide(ae[7:8])) - ae
        y4 = yt[pl.ds(t * 4, 4), :]
        carried = flow[0:4] - y4 * flow[4:5]
        gain = jnp.where(row8[0:4] == 3, jnp.broadcast_to(heat, (4, 128)), visc_coef)
        inv = invt[pl.ds(t, 1), :]
        return inv * ((6.0 * press_coef) * moved[0:4] + gain * carried) + moved[4:8]

    def own_coef(t, c):
        coefficients(t, None)
        return c

    lax.fori_loop(0, cells, own_coef, 0, unroll=4)

    def second_sums(g, c):
        for u in range(UNROLL):
            n = g * UNROLL + u
            raw[n] = force_sums(npair + n, couples[0, n])
        return c

    lax.fori_loop(0, npair // UNROLL, second_sums, 0)

    wait_all(1, y_all, y_rims)
    wait_all(3, ri.at[pl.ds(0, peers - 1)], i_rims)

    def spread(q, c):
        invt[pl.ds(cells + 4 * q, 4), :] = ri[q]
        yt[pl.ds(pl.multiple_of(4 * cells + 16 * q, 8), 16), :] = ry[q, 0:16, :]
        kt[pl.ds(cells + 4 * q, 4), :] = ry[q, 16:20, :]
        return c

    lax.fori_loop(0, peers, spread, 0, unroll=4)
    for side in range(2):
        at = rim0 + side * E
        invt[at : at + E, :] = rir[side, 0:E, :]
        yt[4 * at : 4 * (at + E), :] = ryr[side, 0 : 4 * E, :]
        kt[at : at + E, :] = ryr[side, 24 : 24 + E, :]

    def pair_force(slot, sums, s, t):
        ks = kt[pl.ds(s, 1), :]
        kd = kt[pl.ds(t, 1), :]
        part = force_at(sums, t, 2.0 * ks * kd / (ks + kd))
        for k in range(4):
            rpart[k, pl.ds(slot, 1), :] = part[k : k + 1, :]

    def second_force(g, c):
        for u in range(UNROLL):
            n = g * UNROLL + u
            pair_force(npair + n, raw[n], couples[0, n], couples[1, n])
        return c

    lax.fori_loop(0, npair // UNROLL, second_force, 0)

    held = None
    half = (lax.broadcasted_iota(jnp.int32, (8 * peers, 128), 0) & 7) < 4
    for k in range(4):
        sums = sum_dot(zlent[...], rpart[k, npair : 2 * npair, :])
        for side in range(2):
            srr[side, 8 * k : 8 * k + 8, :] = sums[rim_at + 8 * side : rim_at + 8 * side + 8]
        lent_sums = sums[0:rim_at]
        if k % 2 == 0:
            held = lent_sums
        else:
            sr[:, 4 * (k - 1) : 4 * (k - 1) + 8, :] = jnp.where(half, held, lent_sums).reshape(
                peers, 8, 128
            )

    r_src = lambda q: sr.at[q]
    r_dst = lambda q: rr.at[pl.ds(pl.multiple_of(16 * q, 8), 16)]
    r_rims = rim_copies(4, srr.at[1], rrr.at[0], srr.at[0], rrr.at[1])
    send_all(4, r_src, r_dst, r_rims)
    rr[pl.ds(pl.multiple_of(16 * me, 8), 16), :] = sr[me]

    def ghost_coef(t, c):
        coefficients(cells + t, None)
        return c

    lax.fori_loop(0, ghosts, ghost_coef, 0, unroll=4)

    def rim_coef(t, c):
        coefficients(rim0 + t, rim_scale(rim0 + t))
        return c

    lax.fori_loop(0, 2 * E, rim_coef, 0, unroll=4)

    def own_force(t, c):
        part = force_at(force_sums(2 * npair + t, t), t, kt[pl.ds(t, 1), :])
        for k in range(4):
            selfr[k, pl.ds(t, 1), :] = part[k : k + 1, :]
        return c

    lax.fori_loop(0, cells, own_force, 0, unroll=SELF_UNROLL)

    def first_force(g, c):
        for u in range(UNROLL):
            n = g * UNROLL + u
            pair_force(n, force_sums(n, couples[1, n]), couples[1, n], couples[0, n])
        return c

    lax.fori_loop(0, npair // UNROLL, first_force, 0)
    for k in range(4):
        ownr[k] = selfr[k] + sum_dot(zown[...], rpart[k])
    drain(0, x_all, x_rims)
    drain(1, y_all, y_rims)
    drain(2, d_all, d_rims)
    drain(3, ri.at[pl.ds(0, peers - 1)], i_rims)
    r_all = rr.at[pl.ds(0, 16 * (peers - 1))]
    wait_all(4, r_all, r_rims)
    for k in range(4):
        got = jnp.concatenate(
            [rr[pl.ds(4 * k + n, peers, stride=16), :] for n in range(slots)], axis=0
        )
        ownr[k] = ownr[k] + sum_dot(zback, got)
        ownr[k, 0:E, :] = ownr[k, 0:E, :] + rrr[0, 8 * k : 8 * k + E, :] * has_below
        ownr[k, cells - E : cells, :] = (
            ownr[k, cells - E : cells, :] + rrr[1, 8 * k : 8 * k + E, :] * has_above
        )
        rates_out[pl.ds(k, cells, stride=4), :] = ownr[k] * gate
    drain(4, r_all, r_rims)


def shards(
    grain_coordinates,
    grain_motion_speeds,
    grain_warmth,
    grain_weights,
    cell_grain_tally,
    cell_deposit_tier,
    tier_thermal_coefficient,
    loaned_cell_indices,
    loaned_cell_tally,
    cell_couples,
    couple_entry_tally,
):
    coords = grain_coordinates[0, 0].transpose(1, 0, 2)
    speeds = grain_motion_speeds[0, 0].transpose(1, 0, 2)
    _, cells, lanes = coords.shape
    picks = loaned_cell_indices[0, 0].T
    slots, peers = picks.shape
    slabs = lax.axis_size("slab")
    couples = cell_couples[0, 0].T
    npair = couples.shape[1]
    table = cells + slots * peers + 2 * E
    vmem = lambda *shape: pltpu.VMEM(shape, f32)
    density, rates = pl.pallas_call(
        functools.partial(step_kernel, cells, lanes, peers, slabs, npair),
        out_shape=(
            jax.ShapeDtypeStruct((cells, lanes), f32),
            jax.ShapeDtypeStruct((4 * cells, lanes), f32),
        ),
        in_specs=[pl.BlockSpec(memory_space=pl.ANY)] * 11,
        out_specs=(
            pl.BlockSpec(memory_space=pltpu.VMEM),
            pl.BlockSpec(memory_space=pltpu.VMEM),
        ),
        scratch_shapes=[
            vmem(3, cells, lanes),
            vmem(3, cells, lanes),
            vmem(cells, lanes),
            vmem(cells, lanes),
            pltpu.VMEM((1, cells), jnp.int32),
            pltpu.VMEM((1, cells), jnp.int32),
            pltpu.SMEM((1, LAYERS), f32),
            pltpu.SMEM((slots, peers), jnp.int32),
            pltpu.VMEM((slots, peers), jnp.int32),
            pltpu.SMEM((1, peers), jnp.int32),
            pltpu.VMEM((1, peers), jnp.int32),
            pltpu.SMEM((2, npair), jnp.int32),
            pltpu.VMEM((2, npair), jnp.int32),
            pltpu.SMEM((1, 1), jnp.int32),
            vmem(cells, lanes),
            vmem(4 * cells, lanes),
            vmem(4 * cells, lanes),
            vmem(4 * table, lanes),
            vmem(4 * table, lanes),
            vmem(peers, 16, lanes),
            vmem(peers, 24, lanes),
            vmem(2, 32, lanes),
            vmem(peers, 24, lanes),
            vmem(2, 32, lanes),
            pltpu.VMEM((table, 32, lanes), bf16),
            pltpu.VMEM((table, lanes, lanes), bf16),
            vmem(2 * npair + cells, lanes, lanes),
            vmem(table, 8, lanes),
            vmem(8 * peers + 16, lanes),
            vmem(2 * npair, lanes),
            vmem(4, 2 * npair, lanes),
            vmem(npair, 16, lanes),
            vmem(cells, lanes),
            vmem(4, cells, lanes),
            vmem(4, cells, lanes),
            pltpu.VMEM((cells, 2 * npair), bf16),
            pltpu.VMEM((8 * peers + 16, npair), bf16),
            vmem(8 * peers, lanes),
            vmem(2, 8, lanes),
            vmem(peers, 4, lanes),
            vmem(2, 8, lanes),
            vmem(peers, 4, lanes),
            vmem(2, 8, lanes),
            vmem(table, lanes),
            vmem(table, lanes),
            vmem(peers, 16, lanes),
            vmem(2, 32, lanes),
            vmem(16 * peers, lanes),
            vmem(2, 32, lanes),
            pltpu.SemaphoreType.DMA((14,)),
            pltpu.SemaphoreType.DMA((5, 3)),
            pltpu.SemaphoreType.DMA((5, 3)),
            pltpu.SemaphoreType.DMA((peers,)),
        ],
        compiler_params=pltpu.CompilerParams(
            collective_id=0, has_side_effects=True, vmem_limit_bytes=60 * 1024 * 1024
        ),
        name="force_step",
    )(
        coords,
        speeds,
        grain_warmth[0, 0],
        grain_weights[0, 0],
        cell_grain_tally[0],
        cell_deposit_tier[0],
        tier_thermal_coefficient[None],
        picks,
        loaned_cell_tally[0],
        couples,
        couple_entry_tally,
    )
    return density[None, None], rates.reshape(1, 1, cells, 4, lanes)


def solution(mesh):
    return jax.shard_map(
        shards,
        mesh=mesh,
        in_specs=(
            P("slab", "plane", None, None, None),
            P("slab", "plane", None, None, None),
            P("slab", "plane", None, None),
            P("slab", "plane", None, None),
            P("slab", "plane", None),
            P("slab", "plane", None),
            P(),
            P("slab", "plane", None, None),
            P("slab", "plane", None),
            P("slab", "plane", None, None),
            P("slab", "plane"),
        ),
        out_specs=(P("slab", "plane", None, None), P("slab", "plane", None, None, None)),
        check_vma=False,
    )
```
